128 devices in a mesh: seq: 16 (over y, z_hi, core), batch: 8 (over z_lo, x).
Axes of the slice: x: 4, y: 4, z: 4 (z_hi: 2, z_lo: 2; z = z_hi * 2 + z_lo), core: 2. Of those that a mesh axis runs over, the one named last changes fastest.
Arguments:
- base_codes: int32 [8, 2048], P('batch', 'seq'), may hold values from 0 to 3
- stem_weight: bfloat16 [15, 4, 768], replicated, may hold values from -1.5 to 1.5
- conv_weight: bfloat16 [3, 768, 768], replicated, may hold values from -0.125 to 0.125
- down_weight: bfloat16 [768, 1536], replicated, may hold values from -0.21875 to 0.21875
- norm_gain: float32 [1536], replicated, may hold values from 0.1 to 1.9
- query_weight: bfloat16 [1536, 1024], P(None, 'batch'), may hold values from -0.15625 to 0.15625
- key_weight: bfloat16 [1536, 1024], P(None, 'batch'), may hold values from -0.15625 to 0.15625
- value_weight: bfloat16 [1536, 1536], P(None, 'batch'), may hold values from -0.15625 to 0.15625
- output_weight: bfloat16 [1536, 1536], P('batch'), may hold values from -0.15625 to 0.15625
- up_weight: bfloat16 [1536, 768], replicated, may hold values from -0.15625 to 0.15625
- cotangent: bfloat16 [8, 2048, 768], P('batch', 'seq'), may hold values from -6 to 6
Outputs:
- features: bfloat16 [8, 2048, 768], P('batch', 'seq')
- grad_stem: float32 [15, 4, 768], P(None, None, ('seq', 'batch'))
- grad_conv: float32 [3, 768, 768], P(None, None, ('seq', 'batch'))
- grad_down: float32 [768, 1536], P(None, ('seq', 'batch'))
- grad_gain: float32 [1536], P(('seq', 'batch'))
- grad_up: float32 [1536, 768], P(None, ('seq', 'batch'))
- grad_query: float32 [1536, 1024], P('seq', 'batch')
- grad_key: float32 [1536, 1024], P('seq', 'batch')
- grad_value: float32 [1536, 1536], P('seq', 'batch')
- grad_out: float32 [1536, 1536], P('seq', 'batch')
The draws below stay inside these ranges and needn't reach their ends.
All inputs are finite; a program needn't handle non-finite values.
Results may differ from the reference program's by a relative error of at most 0.035.
Values may be sent and summed in bfloat16 or wider, within the bound.
A program may use at most 128 MiB of HBM per device.

```python
import math
import jax
import jax.numpy as jnp
from jax import lax

BASE_WIDTH = 768
WIDTH = 1536
HEADS = 8
KEY_SIZE = 128
STEM = 15
DILATION = 8
WINDOWS = 8
LENGTH = 2048


def touch_ends(result, rng, least, high):
    shape = result.shape
    spot = [jax.random.randint(jax.random.fold_in(rng, axis), (), 0, shape[axis]) for axis in range(len(shape))]
    result = result.at[tuple(spot)].set(least)
    longest = shape.index(max(shape))
    spot[longest] = (spot[longest] + 1) % shape[longest]
    return result.at[tuple(spot)].set(high)


def block_scale(own_key, extent, shards, smallest, top_value):
    loudness = 1.0
    for position, parts in shards:
        steps = jax.random.uniform(jax.random.fold_in(jax.random.fold_in(own_key, 6), position), (parts,), jnp.float32, smallest / len(shards), top_value / len(shards))
        loudness = loudness * jnp.repeat(jnp.exp(steps), extent[position] // parts).reshape((-1,) + (1,) * (len(extent) - 1 - position))
    return loudness


def noise(own_key, shape, scale, bound, cuts=(), held_as=jnp.bfloat16):
    drawn = scale * jax.random.normal(own_key, shape, jnp.float32)
    if cuts:
        drawn = drawn * block_scale(own_key, shape, cuts, -0.22, 0.18)
    return jnp.clip(drawn, -bound, bound).astype(held_as)


def setup_inputs(seed: int = 0) -> dict:
    arg_keys = jax.random.split(jax.random.key(seed), 12)
    return {
        "base_codes": touch_ends(jax.random.randint(arg_keys[0], (WINDOWS, LENGTH), 0, 4), jax.random.fold_in(arg_keys[0], 1), 0, 3).astype(jnp.int32),
        "stem_weight": noise(arg_keys[1], (STEM, 4, BASE_WIDTH), STEM ** -0.5, 1.5),
        "conv_weight": noise(arg_keys[2], (3, BASE_WIDTH, BASE_WIDTH), (3 * BASE_WIDTH) ** -0.5, 0.125),
        "down_weight": noise(arg_keys[3], (BASE_WIDTH, WIDTH), BASE_WIDTH ** -0.5, 0.21875),
        "norm_gain": jnp.clip(1.0 + 0.18 * jax.random.normal(arg_keys[4], (WIDTH,), jnp.float32), 0.1, 1.9),
        "query_weight": noise(arg_keys[5], (WIDTH, HEADS * KEY_SIZE), WIDTH ** -0.5, 0.15625, ((1, 8),)),
        "key_weight": noise(arg_keys[6], (WIDTH, HEADS * KEY_SIZE), WIDTH ** -0.5, 0.15625, ((1, 8),)),
        "value_weight": noise(arg_keys[7], (WIDTH, WIDTH), WIDTH ** -0.5, 0.15625, ((1, 8),)),
        "output_weight": noise(arg_keys[8], (WIDTH, WIDTH), WIDTH ** -0.5, 0.15625, ((0, 8),)),
        "up_weight": noise(arg_keys[9], (WIDTH, BASE_WIDTH), WIDTH ** -0.5, 0.15625),
        "cotangent": noise(arg_keys[10], (WINDOWS, LENGTH, BASE_WIDTH), 1.0, 6.0, ((0, 8), (1, 16))),
    }


EPSILON = 1e-06

def stem_embed(weights, padded_bases):
    tap_count = weights.shape[0]
    row_count = padded_bases.shape[1] - tap_count + 1
    codes = jnp.arange(1, 5, dtype=jnp.int32)
    windows = jnp.stack([padded_bases[:, offset:offset + row_count] for offset in range(tap_count)], axis=2)
    one_hot = (windows[..., None] == codes).astype(jnp.bfloat16).reshape(-1, tap_count * 4)
    summed = jnp.dot(one_hot, weights.reshape(tap_count * 4, -1), preferred_element_type=jnp.float32)
    return summed.reshape(padded_bases.shape[0], row_count, -1).astype(jnp.bfloat16)

def conv_block(weights, padded):
    number, total, channel_count = padded.shape
    row_count = total - 2 * DILATION
    summed = jnp.zeros((number * row_count, channel_count), jnp.float32)
    for tap_index in range(3):
        shifted = padded[:, tap_index * DILATION:tap_index * DILATION + row_count].reshape(-1, channel_count)
        summed = summed + jnp.dot(shifted, weights[tap_index], preferred_element_type=jnp.float32)
    center = padded[:, DILATION:DILATION + row_count].reshape(-1, channel_count).astype(jnp.float32)
    return (center + jax.nn.gelu(summed)).astype(jnp.bfloat16).reshape(number, row_count, channel_count)

def down_block(weights, gain_vector, towered):
    number, row_count, channel_count = towered.shape
    pairs = towered.reshape(number, row_count // 2, 2, channel_count).astype(jnp.float32)
    pooled = (0.5 * (pairs[:, :, 0] + pairs[:, :, 1])).astype(jnp.bfloat16).reshape(-1, channel_count)
    lifted = jnp.dot(pooled, weights, preferred_element_type=jnp.float32).astype(jnp.bfloat16)
    values_f = lifted.astype(jnp.float32)
    factor = lax.rsqrt(lax.optimization_barrier(jnp.mean(values_f * values_f, axis=-1, keepdims=True)) + EPSILON)
    normed = (values_f * factor * gain_vector).astype(jnp.bfloat16)
    return (lifted, normed)

def tail_block(weights, lifted, mixed, towered):
    number, row_count, channel_count = towered.shape
    updated = (lifted.astype(jnp.float32) + mixed).astype(jnp.bfloat16)
    lowered = jnp.dot(updated, weights, preferred_element_type=jnp.float32).reshape(number, row_count // 2, 1, channel_count)
    skipped = towered.reshape(number, row_count // 2, 2, channel_count).astype(jnp.float32)
    return (skipped + lowered).astype(jnp.bfloat16).reshape(number, row_count, channel_count)

def split_heads(array, heads):
    return array.reshape(array.shape[0], array.shape[1], heads, -1).astype(jnp.float32)

def head_scores(queries, keys, heads):
    query_heads = split_heads(queries, heads)
    key_heads = split_heads(keys, heads)
    factor = 1.0 / math.sqrt(query_heads.shape[-1])
    return jnp.einsum('nqhd,nkhd->nhqk', query_heads, key_heads) * factor

def attend_rows(queries, keys, values, heads):
    scores = head_scores(queries, keys, heads)
    log_total = jnp.log(lax.optimization_barrier(jnp.sum(jnp.exp(scores), axis=-1, keepdims=True)))
    weights_b = jnp.exp(scores - log_total).astype(jnp.bfloat16)
    output = jnp.einsum('nhqk,nkhd->nqhd', weights_b.astype(jnp.float32), split_heads(values, heads))
    output = output.astype(jnp.bfloat16).reshape(queries.shape[0], queries.shape[1], -1)
    return (output, jnp.transpose(log_total[..., 0], (0, 2, 1)))

def query_grads(queries, keys, values, log_total, d_attended, heads):
    scores = head_scores(queries, keys, heads)
    softmax_weights = jnp.exp(scores - jnp.transpose(log_total, (0, 2, 1))[..., None])
    d_weights = jnp.einsum('nqhd,nkhd->nhqk', split_heads(d_attended, heads), split_heads(values, heads))
    inner_term = lax.optimization_barrier(jnp.sum(softmax_weights * d_weights, axis=-1))
    d_scores = (softmax_weights * (d_weights - inner_term[..., None])).astype(jnp.bfloat16)
    key_heads = split_heads(keys, heads)
    factor = 1.0 / math.sqrt(key_heads.shape[-1])
    d_queries = jnp.einsum('nhqk,nkhd->nqhd', d_scores.astype(jnp.float32), key_heads) * factor
    return (d_queries.reshape(queries.shape[0], queries.shape[1], -1), jnp.transpose(inner_term, (0, 2, 1)))

def key_grads(queries, d_attended, log_total, inner_term, keys, values, heads):
    scores = head_scores(queries, keys, heads)
    softmax_weights = jnp.exp(scores - jnp.transpose(log_total, (0, 2, 1))[..., None])
    d_heads = split_heads(d_attended, heads)
    d_weights = jnp.einsum('nqhd,nkhd->nhqk', d_heads, split_heads(values, heads))
    d_scores = (softmax_weights * (d_weights - jnp.transpose(inner_term, (0, 2, 1))[..., None])).astype(jnp.bfloat16)
    query_heads = split_heads(queries, heads)
    factor = 1.0 / math.sqrt(query_heads.shape[-1])
    d_keys = jnp.einsum('nhqk,nqhd->nkhd', d_scores.astype(jnp.float32), query_heads) * factor
    weights_b = softmax_weights.astype(jnp.bfloat16).astype(jnp.float32)
    d_values = jnp.einsum('nhqk,nqhd->nkhd', weights_b, d_heads)
    return (d_keys.reshape(keys.shape[0], keys.shape[1], -1), d_values.reshape(values.shape[0], values.shape[1], -1))

def window_grads(group):
    queries, keys, values, log_total, d_attended = [item[None] for item in group]
    d_queries, inner_term = query_grads(queries, keys, values, log_total, d_attended, HEADS)
    d_keys, d_values = key_grads(queries, d_attended, log_total, inner_term, keys, values, HEADS)
    return (d_queries[0], d_keys[0], d_values[0])

def window_attend(group):
    output, log_total = attend_rows(group[0][None], group[1][None], group[2][None], HEADS)
    return (output[0], log_total[0])

def contract_rows(left, right):
    return lax.dot_general(left, right, (((0,), (0,)), ((), ())), preferred_element_type=jnp.float32)

def contract_cols(left, right):
    return lax.dot_general(left, right, (((1,), (1,)), ((), ())), preferred_element_type=jnp.float32)

def reference(base_codes, stem_weight, conv_weight, down_weight, norm_gain, query_weight, key_weight, value_weight, output_weight, up_weight, cotangent):
    reach = (STEM - 1) // 2
    padded_bases = jnp.pad(base_codes + 1, ((0, 0), (reach, reach)))
    embedded, stem_back = jax.vjp(lambda weights: stem_embed(weights, padded_bases), stem_weight)
    padded = jnp.pad(embedded, ((0, 0), (DILATION, DILATION), (0, 0)))
    towered, conv_back = jax.vjp(conv_block, conv_weight, padded)
    (lifted, normed), down_back = jax.vjp(down_block, down_weight, norm_gain, towered)
    coarse = LENGTH // 2
    queries = jnp.dot(normed, query_weight, preferred_element_type=jnp.float32).astype(jnp.bfloat16).reshape(WINDOWS, coarse, -1)
    keys = jnp.dot(normed, key_weight, preferred_element_type=jnp.float32).astype(jnp.bfloat16).reshape(WINDOWS, coarse, -1)
    values = jnp.dot(normed, value_weight, preferred_element_type=jnp.float32).astype(jnp.bfloat16).reshape(WINDOWS, coarse, -1)
    attended, log_total = lax.map(window_attend, (queries, keys, values))
    flat_attended = attended.reshape(-1, WIDTH)
    mixed = jnp.dot(flat_attended, output_weight, preferred_element_type=jnp.float32)
    features, tail_back = jax.vjp(tail_block, up_weight, lifted, mixed, towered)
    d_up, d_lifted, d_mixed, d_tail = tail_back(cotangent)
    d_mixed_b = d_mixed.astype(jnp.bfloat16)
    d_attended = contract_cols(d_mixed_b, output_weight).astype(jnp.bfloat16).reshape(attended.shape)
    grad_out = contract_rows(d_mixed_b, flat_attended)
    d_queries, d_keys, d_values = lax.map(window_grads, (queries, keys, values, log_total, d_attended))
    d_queries_b = d_queries.astype(jnp.bfloat16).reshape(-1, query_weight.shape[1])
    d_keys_b = d_keys.astype(jnp.bfloat16).reshape(-1, key_weight.shape[1])
    d_values_b = d_values.astype(jnp.bfloat16).reshape(-1, value_weight.shape[1])
    grad_query = contract_rows(normed, d_queries_b)
    grad_key = contract_rows(normed, d_keys_b)
    grad_value = contract_rows(normed, d_values_b)
    d_normed = contract_cols(d_queries_b, query_weight) + contract_cols(d_keys_b, key_weight) + contract_cols(d_values_b, value_weight)
    d_down, d_gain, d_pooled_path = down_back((d_lifted, d_normed.astype(jnp.bfloat16)))
    d_towered = (d_tail.astype(jnp.float32) + d_pooled_path.astype(jnp.float32)).astype(jnp.bfloat16)
    d_conv, d_padded = conv_back(d_towered)
    d_stem, = stem_back(d_padded[:, DILATION:DILATION + LENGTH])
    return (features, d_stem.astype(jnp.float32), d_conv.astype(jnp.float32), d_down.astype(jnp.float32), d_gain.astype(jnp.float32), d_up.astype(jnp.float32), grad_query, grad_key, grad_value, grad_out)
```

```python
import functools
import math

import jax
import jax.numpy as jnp
from jax import lax
from jax.experimental import pallas as pl
from jax.experimental.pallas import tpu as pltpu
from jax.sharding import PartitionSpec as P

EPSILON = 1e-06
MESH = pl.DeviceIdType.MESH
F32 = jnp.float32
BF16 = jnp.bfloat16
SEQ = 16
BATCH = 8


class OverBatch:
    count = BATCH

    def dst(self, i, s, b):
        j = lax.rem(b + i, BATCH)
        return j, s, j, b

    def src(self, i, s, b):
        j = lax.rem(b + BATCH - i, BATCH)
        return j, s, j

    def same(self, i):
        return i == 0


class OverSeq:
    count = SEQ

    def dst(self, i, s, b):
        j = lax.rem(s + i, SEQ)
        return j, j, b, s

    def src(self, i, s, b):
        j = lax.rem(s + SEQ - i, SEQ)
        return j, j, b

    def same(self, i):
        return i == 0


class Columns:
    count = SEQ

    def dst(self, i, s, b):
        j = lax.rem(s + i, SEQ)
        return j, 2 * b + j // BATCH, lax.rem(j, BATCH), s

    def src(self, i, s, b):
        j = lax.rem(SEQ * BATCH + lax.rem(s, 2) * BATCH + b - i, SEQ)
        return j, j, s // 2

    def same(self, i):
        return None


class Codes:
    count = 2 * BATCH

    def dst(self, i, s, b):
        j = lax.rem(b + i // 2, BATCH)
        return 0, 2 * b + i % 2, j, s

    def src(self, i, s, b):
        return i, i, s // 2

    def same(self, i):
        return None


class ToWorkers:
    count = BATCH

    def dst(self, i, s, b):
        return 0, 2 * b + s // BATCH, lax.rem(s + i, BATCH), lax.rem(s, BATCH)

    def src(self, i, s, b):
        j = lax.rem(b + BATCH - i, BATCH)
        return j, BATCH * lax.rem(s, 2) + j, s // 2

    def same(self, i):
        return None


class ToBlock:
    count = 1

    def dst(self, i, s, b):
        return 0, 2 * b + s // BATCH, lax.rem(s, BATCH), 0

    def src(self, i, s, b):
        return 0, BATCH * lax.rem(s, 2) + b, s // 2

    def same(self, i):
        return None


class ToOwner:
    count = 1

    def dst(self, i, s, b):
        return 0, BATCH * lax.rem(s, 2) + b, s // 2, 0

    def src(self, i, s, b):
        return 0, 2 * b + s // BATCH, lax.rem(s, BATCH)

    def same(self, i):
        return None


def exchange_body(patterns, *refs):
    number = len(patterns)
    sources, results = refs[:number], refs[number : 2 * number]
    sends, receives = refs[2 * number : 3 * number], refs[3 * number :]
    s, b = lax.axis_index("seq"), lax.axis_index("batch")
    barrier = pltpu.get_barrier_semaphore()
    expected = 0
    for pattern in patterns:
        for i in range(pattern.count):
            if pattern.same(i):
                continue
            _, other_s, other_b = pattern.src(i, s, b)
            _, target_s, target_b, _ = pattern.dst(i, s, b)
            if pattern.same(i) is None:
                away = jnp.logical_or(other_s != s, other_b != b)

                @pl.when(away)
                def _():
                    pl.semaphore_signal(
                        barrier, inc=1, device_id=(other_s, other_b), device_id_type=MESH
                    )

                there = jnp.logical_or(target_s != s, target_b != b)
                expected = expected + there.astype(jnp.int32)
            else:
                pl.semaphore_signal(
                    barrier, inc=1, device_id=(other_s, other_b), device_id_type=MESH
                )
                expected = expected + 1
    pl.semaphore_wait(barrier, expected)

    def steps(action):
        for k, pattern in enumerate(patterns):
            for i in range(pattern.count):
                piece, target_s, target_b, slot = pattern.dst(i, s, b)
                near = functools.partial(
                    pltpu.make_async_copy,
                    sources[k].at[piece],
                    results[k].at[slot],
                    sends[k].at[i],
                )
                far = functools.partial(
                    pltpu.make_async_remote_copy,
                    src_ref=sources[k].at[piece],
                    dst_ref=results[k].at[slot],
                    send_sem=sends[k].at[i],
                    recv_sem=receives[k].at[slot],
                    device_id=(target_s, target_b),
                    device_id_type=MESH,
                )
                same = pattern.same(i)
                if same is None:
                    home = jnp.logical_and(target_s == s, target_b == b)
                    pl.when(home)(functools.partial(action, near, None))
                    pl.when(jnp.logical_not(home))(functools.partial(action, None, far))
                elif same:
                    action(near, None)
                else:
                    action(None, far)

    def start(near, far):
        (near if far is None else far)().start()

    def finish(near, far):
        if far is None:
            near().wait()
        else:
            far().wait_send()

    steps(start)
    for k, pattern in enumerate(patterns):
        for i in range(pattern.count):
            slot, other_s, other_b = pattern.src(i, s, b)
            same = pattern.same(i)
            if same:
                continue
            arriving = pltpu.make_async_remote_copy(
                src_ref=sources[k].at[0],
                dst_ref=results[k].at[slot],
                send_sem=sends[k].at[i],
                recv_sem=receives[k].at[slot],
                device_id=(other_s, other_b),
                device_id_type=MESH,
            )
            if same is None:
                away = jnp.logical_or(other_s != s, other_b != b)
                pl.when(away)(arriving.wait_recv)
            else:
                arriving.wait_recv()
    steps(finish)


def exchange(arrays, patterns, slots, collective_id):
    return pl.pallas_call(
        functools.partial(exchange_body, patterns),
        out_shape=[
            jax.ShapeDtypeStruct((slot,) + array.shape[1:], array.dtype)
            for array, slot in zip(arrays, slots)
        ],
        in_specs=[pl.BlockSpec(memory_space=pl.ANY)] * len(arrays),
        out_specs=[pl.BlockSpec(memory_space=pl.ANY)] * len(arrays),
        scratch_shapes=[pltpu.SemaphoreType.DMA((pattern.count,)) for pattern in patterns]
        + [pltpu.SemaphoreType.DMA((slot,)) for slot in slots],
        compiler_params=pltpu.CompilerParams(collective_id=collective_id, has_side_effects=True),
        name="exchange_%d" % collective_id,
    )(*arrays)


def mm(left, right, dims):
    return lax.dot_general(left, right, ((dims[0:1], dims[1:2]), ((), ())), preferred_element_type=F32)


def attention_body(
    q_ref, kv_ref, da_ref, att_ref, dq_ref, dkv_ref,
    other, sent, arrived, own_sum, far_sum, send_sem, recv_sem,
):
    s, b = lax.axis_index("seq"), lax.axis_index("batch")
    peer = (s + 1 - 2 * lax.rem(s, 2), b)
    barrier = pltpu.get_barrier_semaphore()
    pl.semaphore_signal(barrier, inc=1, device_id=peer, device_id_type=MESH)
    pl.semaphore_wait(barrier, 1)
    first = pltpu.make_async_remote_copy(
        src_ref=kv_ref, dst_ref=other, send_sem=send_sem.at[0], recv_sem=recv_sem.at[0],
        device_id=peer, device_id_type=MESH,
    )
    first.start()
    own_sum[...] = jnp.zeros_like(own_sum)
    far_sum[...] = jnp.zeros_like(far_sum)
    first.wait()
    factor = 1.0 / math.sqrt(128)
    rows = 128

    def step(t, carry):
        here = pl.ds(pl.multiple_of(t * rows, rows), rows)
        q, da = q_ref[here, :], da_ref[here, :]
        blocks = ((kv_ref, own_sum), (other, far_sum))
        scores = [mm(q, kv[:, :128], (1, 1)) * factor for kv, _ in blocks]
        total = sum(jnp.sum(jnp.exp(x), axis=1, keepdims=True) for x in scores)
        log_total = jnp.log(total)
        probs = [jnp.exp(x - log_total) for x in scores]
        dprobs = [mm(da, kv[:, 128:], (1, 1)) for kv, _ in blocks]
        inner = sum(jnp.sum(p * d, axis=1, keepdims=True) for p, d in zip(probs, dprobs))
        att = jnp.zeros((rows, 256), F32)
        dq = jnp.zeros((rows, 128), F32)
        for (kv, total_ref), p, d in zip(blocks, probs, dprobs):
            ds = (p * (d - inner)).astype(BF16)
            pb = p.astype(BF16)
            att = att + mm(pb, kv[:, 128:], (1, 0))
            dq = dq + mm(ds, kv[:, :128], (1, 0))
            total_ref[:, :128] += mm(ds, q, (0, 0)) * factor
            total_ref[:, 128:] += mm(pb, da, (0, 0))
        att_ref[here, :] = att.astype(BF16)
        dq_ref[here, :] = (dq * factor).astype(BF16)
        return carry

    lax.fori_loop(0, q_ref.shape[0] // rows, step, 0)
    sent[...] = far_sum[...].astype(BF16)
    second = pltpu.make_async_remote_copy(
        src_ref=sent, dst_ref=arrived, send_sem=send_sem.at[1], recv_sem=recv_sem.at[1],
        device_id=peer, device_id_type=MESH,
    )
    second.start()
    second.wait()
    dkv_ref[...] = (own_sum[...] + arrived[...].astype(F32)).astype(BF16)


def attention(q, kv, da):
    rows = q.shape[0]
    vmem = pl.BlockSpec(memory_space=pltpu.VMEM)
    return pl.pallas_call(
        attention_body,
        out_shape=[
            jax.ShapeDtypeStruct((rows, 256), BF16),
            jax.ShapeDtypeStruct((rows, 128), BF16),
            jax.ShapeDtypeStruct((rows, 384), BF16),
        ],
        in_specs=[vmem] * 3,
        out_specs=[vmem] * 3,
        scratch_shapes=[
            pltpu.VMEM((rows, 384), BF16),
            pltpu.VMEM((rows, 384), BF16),
            pltpu.VMEM((rows, 384), BF16),
            pltpu.VMEM((rows, 384), F32),
            pltpu.VMEM((rows, 384), F32),
            pltpu.SemaphoreType.DMA((2,)),
            pltpu.SemaphoreType.DMA((2,)),
        ],
        compiler_params=pltpu.CompilerParams(
            collective_id=1, has_side_effects=True, vmem_limit_bytes=32 * 1024 * 1024
        ),
        name="attention",
    )(q, kv, da)


def dot(left, right):
    return jnp.dot(left, right, preferred_element_type=F32)


def dot_rows(left, right):
    return lax.dot_general(left, right, (((0,), (0,)), ((), ())), preferred_element_type=F32)


def dot_cols(left, right):
    return lax.dot_general(left, right, (((1,), (1,)), ((), ())), preferred_element_type=F32)


def parity_matrix(size, dtype):
    row = lax.broadcasted_iota(jnp.int32, (size, size), 0)
    column = lax.broadcasted_iota(jnp.int32, (size, size), 1)
    half = size // 2
    return (column == jnp.where(row < half, 2 * row, 2 * (row - half) + 1)).astype(dtype)


def one_hots(even, odd, h):
    pad = jnp.zeros((1, 8), jnp.int32)
    streams = []
    for stream in (even, odd):
        stream = jnp.concatenate([pad, stream, pad], axis=1)
        streams.append(lax.dynamic_slice_in_dim(stream, 512 * h, 528, axis=1))
    e, o = streams
    where = lax.broadcasted_iota(jnp.int32, (1, 520), 1) - 4 + 512 * h
    inside = jnp.logical_and(where >= 0, where < 1024)
    taps = []
    for parity in range(2):
        rows = []
        for tap in range(-7, 8):
            offset = parity + tap
            source, shift = (e, offset // 2) if offset % 2 == 0 else (o, (offset - 1) // 2)
            rows.append(lax.slice_in_dim(source, 4 + shift, 4 + shift + 520, axis=1))
        rows.append(jnp.zeros((1, 520), jnp.int32))
        taps.append(jnp.where(inside, jnp.concatenate(rows, axis=0), 0))
    taps = jnp.stack(taps)
    code = lax.broadcasted_iota(jnp.int32, (1, 4, 1, 1), 1) + 1
    hot = (taps[:, None] == code).astype(BF16).reshape(2, 64, 520)
    return jnp.stack([hot[:, :, 4 + d : 4 + d + 512] for d in (-4, 0, 4)], axis=1)


def gelu_grad(x):
    inner = math.sqrt(2.0 / math.pi) * (x + 0.044715 * x * x * x)
    t = jnp.tanh(inner)
    slope = math.sqrt(2.0 / math.pi) * (1.0 + 3 * 0.044715 * x * x)
    return 0.5 * (1.0 + t) + 0.5 * x * (1.0 - t * t) * slope


def per_device(
    base_codes,
    stem_weight,
    conv_weight,
    down_weight,
    norm_gain,
    query_weight,
    key_weight,
    value_weight,
    output_weight,
    up_weight,
    cotangent,
):
    s, b = lax.axis_index("seq"), lax.axis_index("batch")
    h = lax.rem(s, 2)

    order = parity_matrix(128, BF16)
    cot = dot(order, cotangent[0]).astype(BF16)
    d_low = (cot[:64].astype(F32) + cot[64:].astype(F32)).astype(BF16)
    codes = dot_cols((base_codes + 1).astype(BF16), order).astype(jnp.int32)
    codes = jnp.broadcast_to(codes, (1, 8, 128))
    codes_all, low_half, cot_blk = exchange(
        [codes, d_low[None], cot[None]], [Codes(), ToWorkers(), ToBlock()], [16, 8, 1], 2
    )
    d_low_half = low_half.reshape(512, 768)
    cot_blk = cot_blk[0]

    stem = jnp.pad(stem_weight, ((0, 1), (0, 0), (0, 0))).transpose(1, 0, 2).reshape(64, 768)
    even = codes_all[:, 0, :64].reshape(1, 1024)
    odd = codes_all[:, 0, 64:].reshape(1, 1024)
    hot = one_hots(even, odd, h)
    emb = jnp.concatenate(
        [
            jnp.concatenate([dot_rows(hot[p, d], stem).astype(BF16) for d in range(3)], axis=1)
            for p in range(2)
        ],
        axis=0,
    )
    conv_flat = conv_weight.reshape(2304, 768)
    conv = dot(emb, conv_flat)
    tower = (emb[:, 768:1536].astype(F32) + jax.nn.gelu(conv)).astype(BF16)
    pooled = (0.5 * (tower[:512].astype(F32) + tower[512:].astype(F32))).astype(BF16)
    lifted = dot(pooled, down_weight).astype(BF16)
    lifted_f = lifted.astype(F32)
    factor = lax.rsqrt(jnp.mean(lifted_f * lifted_f, axis=-1, keepdims=True) + EPSILON)
    normed = (lifted_f * factor * norm_gain).astype(BF16)
    value_pad = jnp.pad(value_weight, ((0, 0), (0, 64)))
    output_pad = jnp.pad(output_weight, ((0, 64), (0, 0)))
    kv_weight = jnp.concatenate([key_weight, value_pad], axis=1)
    q = dot(normed, query_weight).astype(BF16)
    kv = dot(normed, kv_weight).astype(BF16)
    d_mixed = dot_cols(d_low_half, up_weight).astype(BF16)
    d_att = dot_cols(d_mixed, output_pad).astype(BF16)

    att, dq, dkv = attention(q, kv, d_att)

    d_normed_part = (dot_cols(dq, query_weight) + dot_cols(dkv, kv_weight)).astype(BF16)
    mixed_part = dot(att, output_pad).astype(BF16)
    grads = jnp.concatenate(
        [
            dot_rows(normed, dq).astype(BF16),
            dot_rows(normed, dkv)[:, :320].astype(BF16),
            dot_rows(d_mixed, att)[:, :192].astype(BF16),
        ],
        axis=1,
    ).reshape(16, 96, 640)
    mixed_all, d_normed_all, grads_all = exchange(
        [mixed_part.reshape(8, 64, 1536), d_normed_part.reshape(8, 64, 1536), grads],
        [OverBatch(), OverBatch(), OverSeq()],
        [8, 8, 16],
        3,
    )

    def block(array, rows):
        return lax.dynamic_slice_in_dim(array, rows, 64, axis=0)

    def both(array):
        return jnp.concatenate([block(array, 64 * b), block(array, 512 + 64 * b)], axis=0)

    mixed = jnp.sum(mixed_all.astype(F32), axis=0)
    d_normed = jnp.sum(d_normed_all.astype(F32), axis=0).astype(BF16).astype(F32)
    tower_b, conv_b = both(tower), both(conv)
    lifted_b, d_updated = block(lifted_f, 64 * b), block(d_mixed, 64 * b)
    factor_b = block(factor, 64 * b)
    updated = (lifted_b + mixed).astype(BF16)
    lowered = dot(updated, up_weight)
    features = (
        tower_b.astype(F32) + jnp.concatenate([lowered, lowered], axis=0)
    ).astype(BF16)
    features = dot_rows(order, features).astype(BF16)

    gained = d_normed * norm_gain
    d_gain = jnp.sum(d_normed * (lifted_b * factor_b), axis=0, keepdims=True)
    shared = jnp.mean(gained * lifted_b, axis=-1, keepdims=True) * (factor_b * factor_b * factor_b)
    d_lifted = (
        (gained * factor_b - lifted_b * shared).astype(BF16).astype(F32) + d_updated.astype(F32)
    ).astype(BF16)
    d_pooled = dot_cols(d_lifted, down_weight) * 0.5
    d_tower = cot_blk.astype(F32) + jnp.concatenate([d_pooled, d_pooled], axis=0)
    d_tower = d_tower.astype(BF16)
    d_conv = (d_tower.astype(F32) * gelu_grad(conv_b)).astype(BF16)
    d_emb = dot_cols(d_conv, conv_flat)
    stem_part = jnp.zeros((64, 768), F32)
    hot_b = lax.dynamic_slice_in_dim(hot, 64 * b, 64, axis=3)
    hot_b = hot_b.transpose(1, 2, 0, 3).reshape(3, 64, 128)
    for d in range(3):
        term = d_emb[:, 768 * d : 768 * (d + 1)]
        if d == 1:
            term = term + d_tower.astype(F32)
        stem_part = stem_part + dot(hot_b[d], term.astype(BF16))

    first = jnp.concatenate(
        [
            jnp.concatenate([d_lifted, jnp.broadcast_to(d_gain, (16, 1536)).astype(BF16)], axis=0)
            .reshape(80, 8, 192)
            .transpose(1, 0, 2),
            jnp.pad(updated, ((0, 16), (0, 0))).reshape(80, 8, 192).transpose(1, 0, 2),
        ],
        axis=2,
    )
    second = (
        jnp.concatenate([d_conv, stem_part.astype(BF16)], axis=0)
        .reshape(192, 8, 96)
        .transpose(1, 0, 2)
    )
    second = jnp.pad(second, ((0, 0), (0, 0), (0, 32)))
    first_all, second_all = exchange([first, second], [OverBatch(), OverBatch()], [8, 8], 4)

    d_lifted_c = first_all[:, :64, :192].reshape(512, 192)
    updated_c = first_all[:, :64, 192:].reshape(512, 192)
    gain_c = jnp.sum(first_all[:, 64, :192].astype(F32), axis=0)
    d_conv_c = (
        second_all[:, :128, :96].reshape(8, 2, 64, 96).transpose(1, 0, 2, 3).reshape(1024, 96)
    )
    stem_c = jnp.sum(second_all[:, 128:, :96].astype(F32), axis=0)
    down_t = dot_rows(d_lifted_c, pooled)
    up_t = dot_rows(d_low_half, updated_c)
    conv_t = dot_rows(d_conv_c, emb)
    flat = jnp.concatenate(
        [
            down_t.astype(BF16).reshape(16, 72, 128),
            conv_t.astype(BF16).reshape(16, 108, 128),
            stem_c.T.astype(BF16).reshape(16, 3, 128),
            jnp.pad(gain_c.astype(BF16).reshape(16, 1, 12), ((0, 0), (0, 8), (0, 116))),
        ],
        axis=1,
    )
    up_pieces = jnp.pad(up_t.astype(BF16).reshape(16, 48, 192), ((0, 0), (0, 0), (0, 64)))
    flat_all, up_all, features = exchange(
        [flat, up_pieces, features[None]], [Columns(), OverSeq(), ToOwner()], [16, 16, 1], 5
    )
    up_sum = jnp.sum(up_all.astype(F32), axis=0)
    up_sum = jnp.pad(up_sum.reshape(8, 6, 256), ((0, 0), (0, 2), (0, 0)))
    (up_final,) = exchange([up_sum], [OverBatch()], [8], 6)
    grad_up = up_final[:, :6, :192].transpose(0, 2, 1).reshape(1536, 6)

    flat_sum = jnp.sum(flat_all.astype(F32), axis=0)
    grad_down = flat_sum[:72].reshape(12, 768).T
    grad_conv = flat_sum[72:180].reshape(6, 3, 768).transpose(1, 2, 0)
    grad_stem = flat_sum[180:183].reshape(6, 4, 16)[:, :, :15].transpose(2, 1, 0)
    grad_gain = flat_sum[183, :12]
    grads_sum = jnp.sum(grads_all.astype(F32), axis=0)
    return (
        features,
        grad_stem,
        grad_conv,
        grad_down,
        grad_gain,
        grad_up,
        grads_sum[:, :128],
        grads_sum[:, 128:256],
        grads_sum[:, 256:448],
        grads_sum[:, 448:],
    )


def solution(mesh):
    placed = (
        P("batch", "seq"),
        P(),
        P(),
        P(),
        P(),
        P(None, "batch"),
        P(None, "batch"),
        P(None, "batch"),
        P("batch", None),
        P(),
        P("batch", "seq", None),
    )
    return jax.shard_map(
        per_device,
        mesh=mesh,
        in_specs=placed,
        out_specs=(
            P("batch", "seq", None),
            P(None, None, ("seq", "batch")),
            P(None, None, ("seq", "batch")),
            P(None, ("seq", "batch")),
            P(("seq", "batch")),
            P(None, ("seq", "batch")),
            P("seq", "batch"),
            P("seq", "batch"),
            P("seq", "batch"),
            P("seq", "batch"),
        ),
        check_vma=False,
    )
```

```python
import functools
import math

import jax
import jax.numpy as jnp
from jax import lax
from jax.experimental import pallas as pl
from jax.experimental.pallas import tpu as pltpu
from jax.sharding import PartitionSpec as P

EPSILON = 1e-06
MESH = pl.DeviceIdType.MESH
F32 = jnp.float32
BF16 = jnp.bfloat16
SEQ = 16
BATCH = 8


class OverBatch:
    count = BATCH

    def dst(self, i, s, b):
        j = lax.rem(b + i, BATCH)
        return j, s, j, b

    def src(self, i, s, b):
        j = lax.rem(b + BATCH - i, BATCH)
        return j, s, j


class OverSeq:
    count = SEQ

    def dst(self, i, s, b):
        j = lax.rem(s + i, SEQ)
        return j, j, b, s

    def src(self, i, s, b):
        j = lax.rem(s + SEQ - i, SEQ)
        return j, j, b


class Columns:
    count = SEQ

    def dst(self, i, s, b):
        j = lax.rem(s + i, SEQ)
        return j, 2 * b + j // BATCH, lax.rem(j, BATCH), s

    def src(self, i, s, b):
        j = lax.rem(SEQ * BATCH + lax.rem(s, 2) * BATCH + b - i, SEQ)
        return j, j, s // 2


class Codes:
    count = 2 * BATCH

    def dst(self, i, s, b):
        j = lax.rem(b + i // 2, BATCH)
        return 0, 2 * b + i % 2, j, s

    def src(self, i, s, b):
        return i, i, s // 2


class ToWorkers:
    count = BATCH

    def dst(self, i, s, b):
        return 0, 2 * b + s // BATCH, lax.rem(s + i, BATCH), lax.rem(s, BATCH)

    def src(self, i, s, b):
        j = lax.rem(b + BATCH - i, BATCH)
        return j, BATCH * lax.rem(s, 2) + j, s // 2


class ToBlock:
    count = 1

    def dst(self, i, s, b):
        return 0, 2 * b + s // BATCH, lax.rem(s, BATCH), 0

    def src(self, i, s, b):
        return 0, BATCH * lax.rem(s, 2) + b, s // 2


class ToOwner:
    count = 1

    def dst(self, i, s, b):
        return 0, BATCH * lax.rem(s, 2) + b, s // 2, 0

    def src(self, i, s, b):
        return 0, 2 * b + s // BATCH, lax.rem(s, BATCH)


class Link:
    def __init__(self, pattern, source, result, sends, receives, s, b):
        self.pattern, self.source, self.result = pattern, source, result
        self.sends, self.receives, self.s, self.b = sends, receives, s, b

    def copy(self, i):
        piece, target_s, target_b, slot = self.pattern.dst(i, self.s, self.b)
        away = jnp.logical_or(target_s != self.s, target_b != self.b)
        return away, pltpu.make_async_remote_copy(
            src_ref=self.source(piece),
            dst_ref=self.result.at[slot],
            send_sem=self.sends.at[i],
            recv_sem=self.receives.at[slot],
            device_id=(target_s, target_b),
            device_id_type=MESH,
        )

    def keep(self, i):
        piece, target_s, target_b, slot = self.pattern.dst(i, self.s, self.b)
        home = jnp.logical_and(target_s == self.s, target_b == self.b)

        @pl.when(home)
        def _():
            self.result[slot] = self.source(piece)[...]

    def each(self, action):
        def step(i, carry):
            action(i)
            return carry

        lax.fori_loop(0, self.pattern.count, step, 0)

    def start_one(self, i):
        away, copy = self.copy(i)
        pl.when(away)(copy.start)

    def start(self):
        self.each(self.start_one)
        self.each(self.keep)

    def receive(self):
        def wait(i):
            slot, other_s, other_b = self.pattern.src(i, self.s, self.b)
            away = jnp.logical_or(other_s != self.s, other_b != self.b)
            copy = pltpu.make_async_remote_copy(
                src_ref=self.result.at[slot],
                dst_ref=self.result.at[slot],
                send_sem=self.sends.at[i],
                recv_sem=self.receives.at[slot],
                device_id=(other_s, other_b),
                device_id_type=MESH,
            )
            pl.when(away)(copy.wait_recv)

        self.each(wait)

    def drain(self):
        def wait(i):
            away, copy = self.copy(i)
            pl.when(away)(copy.wait_send)

        self.each(wait)


def dot(left, right):
    return jnp.dot(left, right, preferred_element_type=F32)


def dot_rows(left, right):
    return lax.dot_general(left, right, (((0,), (0,)), ((), ())), preferred_element_type=F32)


def dot_cols(left, right):
    return lax.dot_general(left, right, (((1,), (1,)), ((), ())), preferred_element_type=F32)


def iota(shape, dim):
    return lax.broadcasted_iota(jnp.int32, shape, dim)


def zero_one(mask):
    return jnp.where(mask, 1.0, 0.0).astype(BF16)


def gelu_grad(x):
    inner = math.sqrt(2.0 / math.pi) * (x + 0.044715 * x * x * x)
    t = jnp.tanh(inner)
    slope = math.sqrt(2.0 / math.pi) * (1.0 + 3 * 0.044715 * x * x)
    return 0.5 * (1.0 + t) + 0.5 * x * (1.0 - t * t) * slope


INPUTS = ["codes", "cot", "gain", "stem", "conv_h", "down_h", "q_h", "k_h", "v_h", "o_h", "up_h"]
OUTPUTS = [
    ("features", (128, 768), BF16),
    ("g_stem", (64, 6), F32),
    ("g_conv", (2304, 6), F32),
    ("g_down", (768, 12), F32),
    ("g_gain", (16, 128), F32),
    ("g_up", (1536, 6), F32),
    ("g_q", (96, 128), F32),
    ("g_k", (96, 128), F32),
    ("g_v", (96, 192), F32),
    ("g_o", (96, 192), F32),
]
SCRATCH = [
    ("conv_w", (2304, 768), BF16),
    ("down_w", (768, 1536), BF16),
    ("q_w", (1536, 128), BF16),
    ("k_w", (1536, 128), BF16),
    ("v_raw", (1536, 192), BF16),
    ("v_w", (1536, 256), BF16),
    ("o_w", (256, 1536), BF16),
    ("up_w", (1536, 768), BF16),
    ("select", (768, 1024), BF16),
    ("codes_s", (1, 8, 128), F32),
    ("codes_r", (16, 8, 128), F32),
    ("low_s", (1, 64, 768), BF16),
    ("low_r", (8, 64, 768), BF16),
    ("blk_s", (1, 128, 768), BF16),
    ("blk_r", (1, 128, 768), BF16),
    ("code", (2, 640, 128), F32),
    ("picked", (2, 528, 128), F32),
    ("emb", (8, 128, 2304), BF16),
    ("conv", (8, 128, 768), F32),
    ("tower", (8, 128, 768), BF16),
    ("pooled", (8, 80, 896), BF16),
    ("lifted", (512, 1536), BF16),
    ("factor", (512, 128), F32),
    ("normed", (512, 1536), BF16),
    ("q", (512, 128), BF16),
    ("kv", (512, 384), BF16),
    ("kv_far", (512, 384), BF16),
    ("d_mixed", (512, 1536), BF16),
    ("d_att", (512, 256), BF16),
    ("att", (512, 256), BF16),
    ("dqkv", (512, 512), BF16),
    ("dkv_own", (512, 384), F32),
    ("dkv_far", (512, 384), F32),
    ("dkv_s", (512, 384), BF16),
    ("dkv_r", (512, 384), BF16),
    ("low_sel", (512, 1024), BF16),
    ("mixed_s", (8, 64, 1536), BF16),
    ("mixed_r", (8, 64, 1536), BF16),
    ("dn_s", (8, 64, 1536), BF16),
    ("dn_r", (8, 64, 1536), BF16),
    ("proj_s", (1536, 640), BF16),
    ("proj_r", (16, 96, 640), BF16),
    ("feat_s", (1, 128, 768), BF16),
    ("feat_r", (1, 128, 768), BF16),
    ("upd_s", (8, 64, 256), BF16),
    ("upd_r", (8, 64, 256), BF16),
    ("dl_s", (8, 80, 256), BF16),
    ("dl_r", (8, 80, 256), BF16),
    ("dc_s", (8, 192, 128), BF16),
    ("dc_r", (8, 192, 128), BF16),
    ("up_s", (16, 64, 256), BF16),
    ("up_r", (16, 64, 256), BF16),
    ("down_s", (16, 16, 896), BF16),
    ("down_r", (16, 16, 896), BF16),
    ("conv_acc", (128, 2304), F32),
    ("conv_s", (16, 16, 1280), BF16),
    ("conv_r", (16, 16, 1280), BF16),
    ("last_s", (8, 8, 256), F32),
    ("last_r", (8, 8, 256), F32),
]
LINKS = [
    ("codes", Codes()),
    ("low", ToWorkers()),
    ("blk", ToBlock()),
    ("mixed", OverBatch()),
    ("dn", OverBatch()),
    ("proj", OverSeq()),
    ("feat", ToOwner()),
    ("upd", OverBatch()),
    ("dl", OverBatch()),
    ("dc", OverBatch()),
    ("up", OverSeq()),
    ("down", Columns()),
    ("conv", Columns()),
    ("last", OverBatch()),
]
WEIGHTS = [
    ("conv_h", "conv_w"),
    ("down_h", "down_w"),
    ("q_h", "q_w"),
    ("k_h", "k_w"),
    ("v_h", "v_raw"),
    ("o_h", "o_w"),
    ("up_h", "up_w"),
]


class Namespace:
    pass


def loop(count, step):
    def body(i, carry):
        step(i)
        return carry

    lax.fori_loop(0, count, body, 0)


def rows_of(i, size):
    return pl.ds(pl.multiple_of(i * size, size), size)


def kernel_body(*refs):
    names = INPUTS + [x[0] for x in OUTPUTS] + [x[0] + "_" for x in SCRATCH]
    n = Namespace()
    for name, ref in zip(names, refs):
        setattr(n, name, ref)
    semaphores = refs[len(names) :]
    weight_sems, swap_send, swap_recv = semaphores[:3]
    s, b = lax.axis_index("seq"), lax.axis_index("batch")
    h = lax.rem(s, 2)
    peer = (s + 1 - 2 * h, b)
    links = {}
    for k, (name, pattern) in enumerate(LINKS):
        sent = getattr(n, name + "_s_")
        if name == "proj":
            source = lambda piece, sent=sent: sent.at[rows_of(piece, 96)]
        else:
            source = lambda piece, sent=sent: sent.at[piece]
        links[name] = Link(
            pattern, source, getattr(n, name + "_r_"), semaphores[3 + 2 * k], semaphores[4 + 2 * k], s, b
        )

    barrier = pltpu.get_barrier_semaphore()
    for name in ("codes", "mixed", "proj", "down", "feat"):
        pattern = links[name].pattern

        def greet(i, pattern=pattern):
            _, other_s, other_b = pattern.src(i, s, b)

            @pl.when(jnp.logical_or(other_s != s, other_b != b))
            def _():
                pl.semaphore_signal(
                    barrier, inc=1, device_id=(other_s, other_b), device_id_type=MESH
                )

        loop(pattern.count, greet)
    own_window = (b == s // 2).astype(jnp.int32)
    own_block = own_window * (s == BATCH * h + b).astype(jnp.int32)
    expected = 16 + 7 + 15 + 16 + 1 - 2 * own_window - own_block

    weights = [
        pltpu.make_async_copy(getattr(n, source), getattr(n, target + "_"), weight_sems.at[k])
        if target != "o_w"
        else pltpu.make_async_copy(n.o_h, n.o_w_.at[pl.ds(0, 192)], weight_sems.at[k])
        for k, (source, target) in enumerate(WEIGHTS)
    ]
    for copy in weights:
        copy.start()

    row, column = iota((128, 128), 0), iota((128, 128), 1)
    order = zero_one(column == jnp.where(row < 64, 2 * row, 2 * row - 127))
    cot = dot(order, n.cot[...])
    n.blk_s_[0] = cot.astype(BF16)
    n.low_s_[0] = (cot[:64] + cot[64:]).astype(BF16)
    codes = jnp.broadcast_to((n.codes[...] + 1).astype(F32), (8, 128)).astype(BF16)
    n.codes_s_[0] = dot_cols(codes, order)

    pl.semaphore_wait(barrier, expected)
    links["codes"].start()
    links["low"].start()
    links["blk"].start()

    def fill(c):
        lane = iota((768, 128), 1) + 128 * c
        wanted = 6 * (lane // 8) + lane % 8
        hit = jnp.logical_and(iota((768, 128), 0) == wanted, lane % 8 < 6)
        n.select_[:, rows_of(c, 128)] = zero_one(hit)

    loop(8, fill)
    n.o_w_[192:, :] = jnp.zeros((64, 1536), BF16)
    gain_row = zero_one(jnp.logical_and(iota((16, 128), 0) == 0, iota((16, 128), 1) == 0))
    for j in range(8):
        n.pooled_[j, :, 768:] = jnp.zeros((80, 128), BF16)
        n.pooled_[j, 64:, :768] = jnp.zeros((16, 768), BF16)
        n.pooled_[j, 64:, 768:] = gain_row

    links["codes"].receive()
    ones = jnp.ones((128, 128), BF16)
    for i in range(10):
        place = BATCH * h + (i - 1)
        inside = jnp.logical_and(place >= 0, place < 16)
        line = n.codes_r_[jnp.clip(place, 0, 15)][0:1]
        line = jnp.where(inside, line, 0.0)
        spread = dot(jnp.where(row == column, line, 0.0).astype(BF16), ones)
        n.code_[0, 64 * i : 64 * i + 64] = spread[:64]
        n.code_[1, 64 * i : 64 * i + 64] = spread[64:]
    lane_tap = iota((1, 128), 1) // 4
    lane_code = (iota((1, 128), 1) % 4 + 1).astype(F32)
    for parity in range(2):
        picked = jnp.zeros((528, 128), F32)
        for tap in range(15):
            offset = parity + tap - 7
            stream, shift = offset % 2, (offset - offset % 2) // 2
            begin = 56 + shift
            picked = jnp.where(lane_tap == tap, n.code_[stream, begin : begin + 528, :], picked)
        where = iota((528, 128), 0) - 8 + 512 * h
        inside = jnp.logical_and(where >= 0, where < 1024)
        n.picked_[parity] = jnp.where(inside, picked, 0.0)

    def one_hots(j):
        found = []
        for parity in range(2):
            near = n.picked_[parity, pl.ds(pl.multiple_of(64 * j, 64), 80), :]
            for step in (-4, 0, 4):
                found.append(zero_one(near[8 + step : 72 + step] == lane_code))
        return found

    def embed(j):
        value = dot(jnp.concatenate(one_hots(j), axis=0), n.stem[...]).astype(BF16)
        for parity in range(2):
            for step in range(3):
                begin = 64 * (3 * parity + step)
                n.emb_[j, 64 * parity : 64 * parity + 64, 768 * step : 768 * step + 768] = value[
                    begin : begin + 64
                ]

    loop(8, embed)
    for copy in weights:
        copy.wait()
    n.v_w_[:, 128:] = jnp.zeros((1536, 128), BF16)
    n.v_w_[:, :192] = n.v_raw_[...]

    def forward(t):
        pair = pl.ds(2 * t, 2)
        here = rows_of(t, 128)
        conv = dot(n.emb_[pair].reshape(256, 2304), n.conv_w_[...])
        n.conv_[pair] = conv.reshape(2, 128, 768)
        center = n.emb_[pair, :, 768:1536].reshape(256, 768).astype(F32)
        tower = (center + jax.nn.gelu(conv)).astype(BF16)
        n.tower_[pair] = tower.reshape(2, 128, 768)
        halves = tower.astype(F32).reshape(2, 2, 64, 768)
        pooled = (0.5 * (halves[:, 0] + halves[:, 1])).astype(BF16)
        n.pooled_[pair, 0:64, 0:768] = pooled
        lifted = dot(pooled.reshape(128, 768), n.down_w_[...]).astype(BF16)
        n.lifted_[here, :] = lifted
        lifted = lifted.astype(F32)
        factor = lax.rsqrt(jnp.mean(lifted * lifted, axis=-1, keepdims=True) + EPSILON)
        n.factor_[here, :] = jnp.broadcast_to(factor, (128, 128))
        normed = (lifted * factor * n.gain[...]).astype(BF16)
        n.normed_[here, :] = normed
        n.q_[here, :] = dot(normed, n.q_w_[...]).astype(BF16)
        n.kv_[here, :128] = dot(normed, n.k_w_[...]).astype(BF16)
        n.kv_[here, 128:] = dot(normed, n.v_w_[...]).astype(BF16)

    loop(4, forward)
    swap = pltpu.make_async_remote_copy(
        src_ref=n.kv_, dst_ref=n.kv_far_, send_sem=swap_send.at[0], recv_sem=swap_recv.at[0],
        device_id=peer, device_id_type=MESH,
    )
    swap.start()
    links["low"].receive()

    def cotangents(t):
        pair, here = pl.ds(2 * t, 2), rows_of(t, 128)
        low = n.low_r_[pair].reshape(128, 768)
        d_mixed = dot_cols(low, n.up_w_[...]).astype(BF16)
        n.d_mixed_[here, :] = d_mixed
        n.d_att_[here, :] = dot_cols(d_mixed, n.o_w_[...]).astype(BF16)
        n.low_sel_[here, :] = dot(low, n.select_[...]).astype(BF16)

    loop(4, cotangents)
    n.dkv_own_[...] = jnp.zeros((512, 384), F32)
    n.dkv_far_[...] = jnp.zeros((512, 384), F32)
    swap.wait()

    scale = 1.0 / math.sqrt(128)

    def send_pair(link, t):
        for j in (2 * t, 2 * t + 1):
            i = lax.rem(j - b + BATCH, BATCH)
            link.start_one(i)

    def attend(t):
        here = rows_of(t, 128)
        q, da = n.q_[here, :], n.d_att_[here, :]
        blocks = ((n.kv_, n.dkv_own_), (n.kv_far_, n.dkv_far_))
        scores = [dot_cols(q, kv[:, :128]) * scale for kv, _ in blocks]
        total = sum(jnp.sum(jnp.exp(x), axis=1, keepdims=True) for x in scores)
        log_total = jnp.log(total)
        probs = [jnp.exp(x - log_total) for x in scores]
        dprobs = [dot_cols(da, kv[:, 128:]) for kv, _ in blocks]
        inner = sum(jnp.sum(p * d, axis=1, keepdims=True) for p, d in zip(probs, dprobs))
        att = jnp.zeros((128, 256), F32)
        dq = jnp.zeros((128, 128), F32)
        for (kv, total_ref), p, d in zip(blocks, probs, dprobs):
            ds = (p * (d - inner)).astype(BF16)
            pb = p.astype(BF16)
            att = att + dot(pb, kv[:, 128:])
            dq = dq + dot(ds, kv[:, :128])
            total_ref[:, :128] += dot_rows(ds, q) * scale
            total_ref[:, 128:] += dot_rows(pb, da)
        att = att.astype(BF16)
        n.att_[here, :] = att
        n.dqkv_[here, :128] = (dq * scale).astype(BF16)
        n.mixed_s_[pl.ds(2 * t, 2)] = dot(att, n.o_w_[...]).astype(BF16).reshape(2, 64, 1536)
        send_pair(links["mixed"], t)

    loop(4, attend)
    n.dkv_s_[...] = n.dkv_far_[...].astype(BF16)
    swap_back = pltpu.make_async_remote_copy(
        src_ref=n.dkv_s_, dst_ref=n.dkv_r_, send_sem=swap_send.at[1], recv_sem=swap_recv.at[1],
        device_id=peer, device_id_type=MESH,
    )
    swap_back.start()
    swap_back.wait()
    n.dqkv_[:, 128:] = (n.dkv_own_[...] + n.dkv_r_[...].astype(F32)).astype(BF16)

    def back_through_projections(t):
        here = rows_of(t, 128)
        d_normed = (
            dot_cols(n.dqkv_[here, :128], n.q_w_[...])
            + dot_cols(n.dqkv_[here, 128:256], n.k_w_[...])
            + dot_cols(n.dqkv_[here, 256:], n.v_w_[...])
        )
        n.dn_s_[pl.ds(2 * t, 2)] = d_normed.astype(BF16).reshape(2, 64, 1536)
        send_pair(links["dn"], t)

    loop(4, back_through_projections)

    def projection_grads(c):
        chunk = rows_of(c, 128)
        first = dot_rows(n.normed_[:, chunk], n.dqkv_[...]).astype(BF16)
        second = dot_rows(n.d_mixed_[:, chunk], n.att_[...]).astype(BF16)
        n.proj_s_[chunk, :] = jnp.concatenate([first[:, :448], second[:, :192]], axis=1)

    loop(12, projection_grads)
    links["proj"].start()

    here = rows_of(b, 64)
    links["mixed"].each(links["mixed"].keep)
    links["dn"].each(links["dn"].keep)
    hots = one_hots(b)
    lifted = n.lifted_[here, :].astype(F32)
    factor = n.factor_[here, 0:1]
    d_updated = n.d_mixed_[here, :].astype(F32)
    links["mixed"].receive()
    mixed = n.mixed_r_[0].astype(F32)
    for j in range(1, 8):
        mixed = mixed + n.mixed_r_[j].astype(F32)
    updated = (lifted + mixed).astype(BF16)

    def select_into(target, value):
        for half in range(2):
            moved = dot(value[:, 768 * half : 768 * half + 768], n.select_[...]).astype(BF16)
            for j in range(4):
                target[4 * half + j] = moved[:, 256 * j : 256 * j + 256]

    select_into(n.upd_s_, updated)
    links["upd"].start()
    lowered = dot(updated, n.up_w_[...])
    features = n.tower_[b].astype(F32) + jnp.concatenate([lowered, lowered], axis=0)
    n.feat_s_[0] = dot_rows(order, features.astype(BF16)).astype(BF16)
    links["feat"].start()

    links["dn"].receive()
    d_normed = n.dn_r_[0].astype(F32)
    for j in range(1, 8):
        d_normed = d_normed + n.dn_r_[j].astype(F32)
    d_normed = d_normed.astype(BF16).astype(F32)
    gained = d_normed * n.gain[...]
    d_gain = jnp.sum(d_normed * (lifted * factor), axis=0, keepdims=True)
    shared = jnp.mean(gained * lifted, axis=-1, keepdims=True) * (factor * factor * factor)
    d_lifted = (gained * factor - lifted * shared).astype(BF16).astype(F32) + d_updated
    d_lifted = d_lifted.astype(BF16)
    select_into(
        n.dl_s_,
        jnp.concatenate([d_lifted, jnp.broadcast_to(d_gain, (16, 1536)).astype(BF16)], axis=0),
    )
    links["dl"].start()
    d_pooled = dot_cols(d_lifted, n.down_w_[...]) * 0.5
    links["blk"].receive()
    d_tower = n.blk_r_[0].astype(F32) + jnp.concatenate([d_pooled, d_pooled], axis=0)
    d_tower = d_tower.astype(BF16)
    d_conv = (d_tower.astype(F32) * gelu_grad(n.conv_[b])).astype(BF16)
    d_stem = jnp.zeros((128, 768), F32)
    for step in range(3):
        d_emb = dot_cols(d_conv, n.conv_w_[768 * step : 768 * step + 768, :])
        if step == 1:
            d_emb = d_emb + d_tower.astype(F32)
        hot = jnp.concatenate([hots[step], hots[3 + step]], axis=0)
        d_stem = d_stem + dot_rows(hot, d_emb.astype(BF16))
    both = jnp.concatenate([d_conv, d_stem[:64].astype(BF16)], axis=0)
    both = dot(both, n.select_[...]).astype(BF16)
    for j in range(8):
        n.dc_s_[j] = both[:, 128 * j : 128 * j + 128]
    links["dc"].start()

    links["upd"].receive()
    updated = n.upd_r_[...].reshape(512, 256)
    n.up_s_[...] = dot_rows(n.low_sel_[...], updated).astype(BF16).reshape(16, 64, 256)
    links["up"].start()
    links["dl"].receive()
    down = dot_rows(n.dl_r_[...].reshape(640, 256), n.pooled_[...].reshape(640, 896))
    n.down_s_[...] = down.astype(BF16).reshape(16, 16, 896)
    links["down"].start()
    n.conv_acc_[...] = jnp.zeros((128, 2304), F32)
    links["dc"].receive()

    def conv_grads(t):
        pair = pl.ds(2 * t, 2)
        left = n.dc_r_[pair, 0:128, :].reshape(256, 128)
        n.conv_acc_[...] += dot_rows(left, n.emb_[pair].reshape(256, 2304))

    loop(4, conv_grads)
    same = zero_one(iota((512, 128), 0) % 64 == iota((512, 128), 1))
    stem = dot_rows(n.dc_r_[:, 128:, :].reshape(512, 128), same)
    n.conv_s_[:, 0:8, :] = n.conv_acc_[:, :1280].reshape(16, 8, 1280).astype(BF16)
    rest = jnp.concatenate([n.conv_acc_[:, 1280:], stem, jnp.zeros((128, 128), F32)], axis=1)
    n.conv_s_[:, 8:16, :] = rest.reshape(16, 8, 1280).astype(BF16)
    links["conv"].start()

    def total(ref, count):
        value = ref[0].astype(F32)
        for j in range(1, count):
            value = value + ref[j].astype(F32)
        return value

    links["up"].receive()
    n.last_s_[...] = total(n.up_r_, 16).reshape(8, 8, 256)
    links["last"].start()
    links["proj"].receive()
    proj = total(n.proj_r_, 16)
    n.g_q[...] = proj[:, :128]
    n.g_k[...] = proj[:, 128:256]
    n.g_v[...] = proj[:, 256:448]
    n.g_o[...] = proj[:, 448:]
    links["feat"].receive()
    n.features[...] = n.feat_r_[0]
    links["down"].receive()
    down = total(n.down_r_, 16)
    n.g_gain[...] = down[:, 768:]
    lane = iota((16, 12), 1)
    twelve = zero_one(iota((16, 12), 0) == 8 * (lane // 6) + lane % 6)
    n.g_down[...] = dot_rows(down[:, :768].astype(BF16), twelve)
    links["last"].receive()
    lane = iota((192, 256), 1)
    tight = jnp.logical_and(iota((192, 256), 0) == 6 * (lane // 8) + lane % 8, lane % 8 < 6)
    tight = zero_one(tight)
    for j in range(8):
        piece = dot_cols(tight, n.last_r_[j].astype(BF16))
        n.g_up[192 * j : 192 * j + 192, :] = piece[:, :6]
    links["conv"].receive()
    conv = total(n.conv_r_, 16).astype(BF16)
    six = zero_one(iota((8, 6), 0) == iota((8, 6), 1))
    n.g_conv[:1280, :] = dot_rows(conv[:8], six)
    n.g_conv[1280:, :] = dot_rows(conv[8:, :1024], six)
    n.g_stem[...] = dot_rows(conv[8:, 1024:1088], six)
    for link in links.values():
        link.drain()


def per_device(
    base_codes,
    stem_weight,
    conv_weight,
    down_weight,
    norm_gain,
    query_weight,
    key_weight,
    value_weight,
    output_weight,
    up_weight,
    cotangent,
):
    vmem, anywhere = pl.BlockSpec(memory_space=pltpu.VMEM), pl.BlockSpec(memory_space=pl.ANY)
    stem = jnp.pad(stem_weight.reshape(60, 768), ((0, 68), (0, 0)))
    semaphores = [pltpu.SemaphoreType.DMA((len(WEIGHTS),))] + [pltpu.SemaphoreType.DMA((2,))] * 2
    for name, pattern in LINKS:
        slots = {x[0]: x[1] for x in SCRATCH}[name + "_r"][0]
        semaphores += [pltpu.SemaphoreType.DMA((pattern.count,)), pltpu.SemaphoreType.DMA((slots,))]
    features, g_stem, g_conv, g_down, g_gain, g_up, g_q, g_k, g_v, g_o = pl.pallas_call(
        kernel_body,
        out_shape=[jax.ShapeDtypeStruct(shape, dtype) for _, shape, dtype in OUTPUTS],
        in_specs=[vmem] * 4 + [anywhere] * 7,
        out_specs=[vmem] * len(OUTPUTS),
        scratch_shapes=[pltpu.VMEM(shape, dtype) for _, shape, dtype in SCRATCH] + semaphores,
        compiler_params=pltpu.CompilerParams(
            collective_id=0, has_side_effects=True, vmem_limit_bytes=60 * 1024 * 1024
        ),
        name="step",
    )(
        base_codes,
        cotangent[0],
        norm_gain.reshape(1, 1536),
        stem,
        conv_weight.reshape(2304, 768),
        down_weight,
        query_weight,
        key_weight,
        value_weight,
        output_weight,
        up_weight,
    )
    return (
        features[None],
        g_stem[:60].reshape(15, 4, 6),
        g_conv.reshape(3, 768, 6),
        g_down,
        jnp.concatenate([g_gain[:6, 0], g_gain[8:14, 0]]),
        g_up,
        g_q,
        g_k,
        g_v,
        g_o,
    )


def solution(mesh):
    placed = (
        P("batch", "seq"),
        P(),
        P(),
        P(),
        P(),
        P(None, "batch"),
        P(None, "batch"),
        P(None, "batch"),
        P("batch", None),
        P(),
        P("batch", "seq", None),
    )
    return jax.shard_map(
        per_device,
        mesh=mesh,
        in_specs=placed,
        out_specs=(
            P("batch", "seq", None),
            P(None, None, ("seq", "batch")),
            P(None, None, ("seq", "batch")),
            P(None, ("seq", "batch")),
            P(("seq", "batch")),
            P(None, ("seq", "batch")),
            P("seq", "batch"),
            P("seq", "batch"),
            P("seq", "batch"),
            P("seq", "batch"),
        ),
        check_vma=False,
    )
```

```python
import functools
import math

import jax
import jax.numpy as jnp
from jax import lax
from jax.experimental import pallas as pl
from jax.experimental.pallas import tpu as pltpu
from jax.sharding import PartitionSpec as P

EPSILON = 1e-06
MESH = pl.DeviceIdType.MESH
F32 = jnp.float32
BF16 = jnp.bfloat16
SEQ = 16
BATCH = 8


class OverBatch:
    count = BATCH

    def dst(self, i, s, b):
        j = lax.rem(b + i, BATCH)
        return j, s, j, b

    def src(self, i, s, b):
        j = lax.rem(b + BATCH - i, BATCH)
        return j, s, j


class Share:
    count = BATCH

    def dst(self, i, s, b):
        return 0, s, lax.rem(b + i, BATCH), b

    def src(self, i, s, b):
        j = lax.rem(b + BATCH - i, BATCH)
        return j, s, j


class OverQuads:
    count = SEQ // 2

    def dst(self, i, s, b):
        j = lax.rem(s // 2 + i, SEQ // 2)
        return j, 2 * j + lax.rem(s, 2), b, s // 2

    def src(self, i, s, b):
        j = lax.rem(s // 2 + SEQ // 2 - i, SEQ // 2)
        return j, 2 * j + lax.rem(s, 2), b


class Core:
    count = 1

    def dst(self, i, s, b):
        other = 1 - lax.rem(s, 2)
        return other, s - lax.rem(s, 2) + other, b, 0

    def src(self, i, s, b):
        return 0, s + 1 - 2 * lax.rem(s, 2), b


class XBlocks:
    count = 8

    def dst(self, i, s, b):
        z, x = b // 4, lax.rem(b, 4)
        to, side = lax.rem(x + i // 2, 4), lax.rem(i, 2)
        return 4 * side + to, s, 4 * z + to, 2 * x + side

    def src(self, i, s, b):
        z, x = b // 4, lax.rem(b, 4)
        at, side = lax.rem(x + 4 - i // 2, 4), lax.rem(i, 2)
        return 2 * at + side, s, 4 * z + at


class ZBlocks:
    count = 4

    def dst(self, i, s, b):
        other = 1 - b // 4
        return 4 * other + i, s, 4 * other + lax.rem(b, 4), i

    def src(self, i, s, b):
        return i, s, 4 * (1 - b // 4) + lax.rem(b, 4)


class ZOne:
    count = 1

    def dst(self, i, s, b):
        return 0, s, 4 * (1 - b // 4) + lax.rem(b, 4), 0

    def src(self, i, s, b):
        return 0, s, 4 * (1 - b // 4) + lax.rem(b, 4)


class XOne:
    count = 4

    def dst(self, i, s, b):
        z, x = b // 4, lax.rem(b, 4)
        to = lax.rem(x + i, 4)
        return to, s, 4 * z + to, x

    def src(self, i, s, b):
        z, x = b // 4, lax.rem(b, 4)
        at = lax.rem(x + 4 - i, 4)
        return at, s, 4 * z + at


class Codes:
    count = 2 * BATCH

    def dst(self, i, s, b):
        return 0, 2 * b + lax.rem(i, 2), lax.rem(b + i // 2, BATCH), s

    def src(self, i, s, b):
        return i, i, s // 2


class ToBlock:
    count = 1

    def dst(self, i, s, b):
        return 0, 2 * b + s // BATCH, lax.rem(s, BATCH), 0

    def src(self, i, s, b):
        return 0, BATCH * lax.rem(s, 2) + b, s // 2


class ToOwner:
    count = 1

    def dst(self, i, s, b):
        return 0, BATCH * lax.rem(s, 2) + b, s // 2, 0

    def src(self, i, s, b):
        return 0, 2 * b + s // BATCH, lax.rem(s, BATCH)


class Link:
    def __init__(self, pattern, source, result, sends, receives, s, b):
        self.pattern, self.source, self.result = pattern, source, result
        self.sends, self.receives, self.s, self.b = sends, receives, s, b

    def copy(self, i):
        piece, target_s, target_b, slot = self.pattern.dst(i, self.s, self.b)
        away = jnp.logical_or(target_s != self.s, target_b != self.b)
        return away, pltpu.make_async_remote_copy(
            src_ref=self.source(piece),
            dst_ref=self.result.at[slot],
            send_sem=self.sends.at[i],
            recv_sem=self.receives.at[slot],
            device_id=(target_s, target_b),
            device_id_type=MESH,
        )

    def keep_one(self, i):
        piece, target_s, target_b, slot = self.pattern.dst(i, self.s, self.b)
        home = jnp.logical_and(target_s == self.s, target_b == self.b)

        @pl.when(home)
        def _():
            self.result[slot] = self.source(piece)[...]

    def each(self, action):
        loop(self.pattern.count, action)

    def start_one(self, i):
        away, copy = self.copy(i)
        pl.when(away)(copy.start)

    def keep(self):
        self.each(self.keep_one)

    def start(self):
        self.each(self.start_one)
        self.keep()

    def receive(self):
        def wait(i):
            slot, other_s, other_b = self.pattern.src(i, self.s, self.b)
            away = jnp.logical_or(other_s != self.s, other_b != self.b)
            copy = pltpu.make_async_remote_copy(
                src_ref=self.result.at[slot],
                dst_ref=self.result.at[slot],
                send_sem=self.sends.at[i],
                recv_sem=self.receives.at[slot],
                device_id=(other_s, other_b),
                device_id_type=MESH,
            )
            pl.when(away)(copy.wait_recv)

        self.each(wait)

    def drain(self):
        def wait(i):
            away, copy = self.copy(i)
            pl.when(away)(copy.wait_send)

        self.each(wait)


def dot(left, right):
    return jnp.dot(left, right, preferred_element_type=F32)


def dot_rows(left, right):
    return lax.dot_general(left, right, (((0,), (0,)), ((), ())), preferred_element_type=F32)


def dot_cols(left, right):
    return lax.dot_general(left, right, (((1,), (1,)), ((), ())), preferred_element_type=F32)


def iota(shape, dim):
    return lax.broadcasted_iota(jnp.int32, shape, dim)


def zero_one(mask):
    return jnp.where(mask, 1.0, 0.0).astype(BF16)


def gelu_grad(x):
    inner = math.sqrt(2.0 / math.pi) * (x + 0.044715 * x * x * x)
    t = jnp.tanh(inner)
    slope = math.sqrt(2.0 / math.pi) * (1.0 + 3 * 0.044715 * x * x)
    return 0.5 * (1.0 + t) + 0.5 * x * (1.0 - t * t) * slope


def total(ref, count):
    value = ref[0].astype(F32)
    for j in range(1, count):
        value = value + ref[j].astype(F32)
    return value


def loop(count, step):
    def body(i, carry):
        step(i)
        return carry

    lax.fori_loop(0, count, body, 0)


def rows_of(i, size):
    return pl.ds(pl.multiple_of(i * size, size), size)


INPUTS = dict(codes=0, cot=0, gain=0, stem=0, conv_h=0, down_h=0, q_h=0, k_h=0, v_h=0, o_h=0, up_h=0)
OUTPUTS = dict(
    features=((128, 768), BF16),
    g_stem=((6, 4, 15), F32),
    g_conv=((3, 6, 768), F32),
    g_down=((12, 768), F32),
    g_gain=((1, 128), F32),
    g_up=((6, 1536), F32),
    g_q=((96, 128), F32),
    g_k=((96, 128), F32),
    g_v=((96, 192), F32),
    g_o=((96, 192), F32),
)
SCRATCH = dict(
    conv_w=((2304, 768), BF16),
    down_w=((768, 1536), BF16),
    in_w=((1536, 512), BF16),
    in_t=((512, 1536), BF16),
    o_w=((256, 1536), BF16),
    o_t=((1536, 256), BF16),
    up_w=((1536, 768), BF16),
    stem_f=((64, 768), F32),
    stem_w=((128, 768), BF16),
    select=((768, 1024), BF16),
    select_conv=((768, 1024), BF16),
    select_down=((768, 1024), BF16),
    codes_s=((1, 8, 128), F32),
    codes_r=((16, 8, 128), F32),
    blk_s=((1, 128, 768), BF16),
    blk_r=((1, 128, 768), BF16),
    low_s=((1, 64, 768), BF16),
    low_r=((8, 64, 768), BF16),
    code=((2, 640, 128), F32),
    picked=((2, 528, 128), F32),
    emb=((8, 128, 2304), BF16),
    conv=((128, 768), F32),
    tower=((128, 768), BF16),
    pooled=((512, 768), BF16),
    lifted=((512, 1536), BF16),
    factor=((512, 128), F32),
    normed=((512, 1536), BF16),
    qkv=((512, 512), BF16),
    kv_far=((512, 384), BF16),
    d_mixed=((512, 1536), BF16),
    d_att=((512, 256), BF16),
    att=((512, 256), BF16),
    dqkv=((512, 512), BF16),
    dkv_own=((512, 384), F32),
    dkv_far=((512, 384), F32),
    dkv_s=((512, 384), BF16),
    dkv_r=((512, 384), BF16),
    low_sel=((512, 1024), BF16),
    conv_acc=((128, 2304), F32),
    mixedA_s=((8, 64, 768), BF16),
    mixedA_r=((8, 64, 768), BF16),
    mixedB_s=((8, 64, 768), BF16),
    mixedB_r=((4, 64, 768), BF16),
    mixedC_s=((1, 64, 768), BF16),
    mixedC_r=((1, 64, 768), BF16),
    mixedD_s=((4, 64, 768), BF16),
    mixedD_r=((4, 64, 768), BF16),
    dnA_s=((8, 64, 768), BF16),
    dnA_r=((8, 64, 768), BF16),
    dnB_s=((8, 64, 768), BF16),
    dnB_r=((4, 64, 768), BF16),
    dnC_s=((1, 64, 768), BF16),
    dnC_r=((1, 64, 768), BF16),
    dnD_s=((4, 64, 768), BF16),
    dnD_r=((4, 64, 768), BF16),
    feat_s=((1, 128, 768), BF16),
    feat_r=((1, 128, 768), BF16),
    upd_s=((8, 64, 256), BF16),
    upd_r=((8, 64, 256), BF16),
    dl_s=((8, 64, 256), BF16),
    dl_r=((8, 64, 256), BF16),
    gain_s=((8, 8, 256), F32),
    gain_r=((8, 8, 256), F32),
    dc_s=((8, 128, 128), BF16),
    dc_r=((8, 128, 128), BF16),
    ds_s=((8, 64, 128), BF16),
    ds_r=((8, 64, 128), BF16),
    proj_c_s=((8, 2, 96, 640), BF16),
    proj_c_r=((1, 8, 96, 640), BF16),
    proj_s=((8, 96, 640), BF16),
    proj_r=((8, 96, 640), BF16),
    up_c_s=((8, 2, 64, 256), BF16),
    up_c_r=((1, 8, 64, 256), BF16),
    up_s=((8, 64, 256), BF16),
    up_r=((8, 64, 256), BF16),
    down_c_s=((8, 2, 16, 896), BF16),
    down_c_r=((1, 8, 16, 896), BF16),
    down_s=((8, 16, 896), BF16),
    down_r=((8, 16, 896), BF16),
    conv_c_s=((8, 2, 16, 1280), BF16),
    conv_c_r=((1, 8, 16, 1280), BF16),
    conv_s=((8, 16, 1280), BF16),
    conv_r=((8, 16, 1280), BF16),
    last_s=((8, 8, 256), F32),
    last_r=((8, 8, 256), F32),
)
LINKS = dict(
    codes=Codes(),
    blk=ToBlock(),
    low=Share(),
    mixedA=XBlocks(),
    mixedB=ZBlocks(),
    mixedC=ZOne(),
    mixedD=XOne(),
    dnA=XBlocks(),
    dnB=ZBlocks(),
    dnC=ZOne(),
    dnD=XOne(),
    feat=ToOwner(),
    upd=OverBatch(),
    dl=OverBatch(),
    gain=OverBatch(),
    dc=OverBatch(),
    ds=OverBatch(),
    proj_c=Core(),
    proj=OverQuads(),
    up_c=Core(),
    up=OverQuads(),
    down_c=Core(),
    down=OverQuads(),
    conv_c=Core(),
    conv=OverQuads(),
    last=OverBatch(),
)


class Namespace:
    pass


def kernel_body(*refs):
    names = list(INPUTS) + list(OUTPUTS) + [x + "_" for x in SCRATCH]
    n = Namespace()
    for name, ref in zip(names, refs):
        setattr(n, name, ref)
    semaphores = refs[len(names) :]
    weight_sems, swap_send, swap_recv = semaphores[:3]
    s, b = lax.axis_index("seq"), lax.axis_index("batch")
    h = lax.rem(s, 2)
    z = b // 4
    peer = (s + 1 - 2 * h, b)
    links = Namespace()
    for k, (name, pattern) in enumerate(LINKS.items()):
        sent = getattr(n, name + "_s_")
        if name.endswith("_c"):
            source = lambda piece, sent=sent: sent.at[:, piece]
        else:
            source = lambda piece, sent=sent: sent.at[piece]
        result = getattr(n, name + "_r_")
        link = Link(pattern, source, result, semaphores[3 + 2 * k], semaphores[4 + 2 * k], s, b)
        setattr(links, name, link)

    barrier = pltpu.get_barrier_semaphore()
    for link in (links.codes, links.low, links.proj, links.up_c, links.feat):
        pattern = link.pattern

        def greet(i, pattern=pattern):
            _, other_s, other_b = pattern.src(i, s, b)

            @pl.when(jnp.logical_or(other_s != s, other_b != b))
            def _():
                pl.semaphore_signal(
                    barrier, inc=1, device_id=(other_s, other_b), device_id_type=MESH
                )

        loop(pattern.count, greet)
    own_window = (b == s // 2).astype(jnp.int32)
    own_block = own_window * (s == BATCH * h + b).astype(jnp.int32)
    expected = 16 + 7 + 7 + 1 + 1 - own_window - own_block

    weights = [
        pltpu.make_async_copy(source, target, weight_sems.at[k])
        for k, (source, target) in enumerate(
            [
                (n.q_h, n.in_w_.at[:, pl.ds(0, 128)]),
                (n.k_h, n.in_w_.at[:, pl.ds(128, 128)]),
                (n.v_h, n.in_t_.at[pl.ds(256, 192)]),
                (n.o_h, n.o_w_.at[pl.ds(0, 192)]),
                (n.conv_h, n.conv_w_),
                (n.down_h, n.down_w_),
                (n.up_h, n.up_w_),
            ]
        )
    ]
    for copy in weights:
        copy.start()

    row, column = iota((128, 128), 0), iota((128, 128), 1)
    order = zero_one(column == jnp.where(row < 64, 2 * row, 2 * row - 127))
    codes = jnp.broadcast_to((n.codes[...] + 1).astype(F32), (8, 128)).astype(BF16)
    n.codes_s_[0] = dot_cols(codes, order)
    n.blk_s_[0] = dot(order, n.cot[...]).astype(BF16)

    pl.semaphore_wait(barrier, expected)
    links.codes.start()
    links.blk.start()

    def fill(c):
        within = iota((1, 128), 1)
        i, m = lax.rem(within, 8), within // 8
        good = i < 6
        rows = iota((768, 128), 0)
        place = rows_of(c, 128)
        n.select_[:, place] = zero_one(rows == jnp.where(good, 6 * (m + 16 * c) + i, -1))
        n.select_conv_[:, place] = zero_one(rows == jnp.where(good, 6 * (8 * m + c) + i, -1))
        wanted = 12 * (8 * (m // 2) + c) + 6 * lax.rem(m, 2) + i
        n.select_down_[:, place] = zero_one(rows == jnp.where(good, wanted, -1))

    loop(8, fill)
    for t in range(15):
        n.stem_f_[4 * t : 4 * t + 4, :] = n.stem[t].astype(F32)
    n.stem_f_[60:, :] = jnp.zeros((4, 768), F32)
    n.stem_w_[:64, :] = n.stem_f_[...].astype(BF16)
    n.stem_w_[64:, :] = jnp.zeros((64, 768), BF16)
    for copy in weights[:4]:
        copy.wait()
    n.o_w_[192:, :] = jnp.zeros((64, 1536), BF16)
    n.in_t_[448:, :] = jnp.zeros((64, 1536), BF16)
    eye, eye2 = zero_one(row == column), zero_one(iota((256, 256), 0) == iota((256, 256), 1))
    n.in_t_[:128, :] = dot_cols(eye, n.in_w_[:, :128]).astype(BF16)
    n.in_t_[128:256, :] = dot_cols(eye, n.in_w_[:, 128:256]).astype(BF16)
    n.in_w_[:, 256:] = dot_rows(n.in_t_[256:, :], eye2).astype(BF16)
    n.o_t_[...] = dot_rows(n.o_w_[...], eye2).astype(BF16)

    links.codes.receive()
    ones = jnp.ones((128, 128), BF16)
    for i in range(10):
        place = BATCH * h + (i - 1)
        inside = jnp.logical_and(place >= 0, place < 16)
        line = n.codes_r_[jnp.clip(place, 0, 15)][0:1]
        line = jnp.where(inside, line, 0.0)
        spread = dot(jnp.where(row == column, line, 0.0).astype(BF16), ones)
        n.code_[0, 64 * i : 64 * i + 64] = spread[:64]
        n.code_[1, 64 * i : 64 * i + 64] = spread[64:]
    lane_tap = iota((1, 128), 1) // 4
    lane_code = (iota((1, 128), 1) % 4 + 1).astype(F32)
    for parity in range(2):
        picked = jnp.zeros((528, 128), F32)
        for tap in range(15):
            offset = parity + tap - 7
            stream, shift = offset % 2, (offset - offset % 2) // 2
            begin = 56 + shift
            picked = jnp.where(lane_tap == tap, n.code_[stream, begin : begin + 528, :], picked)
        where = iota((528, 128), 0) - 8 + 512 * h
        inside = jnp.logical_and(where >= 0, where < 1024)
        n.picked_[parity] = jnp.where(inside, picked, 0.0)

    links.blk.receive()
    pairs = n.blk_r_[0].astype(F32)
    n.low_s_[0] = (pairs[:64] + pairs[64:]).astype(BF16)
    links.low.start()

    def one_hots(j):
        found = []
        for parity in range(2):
            near = n.picked_[parity, pl.ds(pl.multiple_of(64 * j, 64), 80), :]
            for step in (-4, 0, 4):
                found.append(zero_one(near[8 + step : 72 + step] == lane_code))
        return found

    def embed(j):
        value = dot(jnp.concatenate(one_hots(j), axis=0), n.stem_w_[...]).astype(BF16)
        for parity in range(2):
            for step in range(3):
                begin = 64 * (3 * parity + step)
                n.emb_[j, 64 * parity : 64 * parity + 64, 768 * step : 768 * step + 768] = value[
                    begin : begin + 64
                ]

    loop(8, embed)
    for copy in weights[4:]:
        copy.wait()
    gain = n.gain[...].reshape(1, 1536)

    def forward(t):
        pair = pl.ds(2 * t, 2)
        here = rows_of(t, 128)
        conv = dot(n.emb_[pair].reshape(256, 2304), n.conv_w_[...])
        center = n.emb_[pair, :, 768:1536].reshape(256, 768).astype(F32)
        tower = (center + jax.nn.gelu(conv)).astype(BF16)
        halves = tower.astype(F32).reshape(2, 2, 64, 768)
        pooled = (0.5 * (halves[:, 0] + halves[:, 1])).astype(BF16).reshape(128, 768)
        n.pooled_[here, :] = pooled
        lifted = dot(pooled, n.down_w_[...]).astype(BF16)
        n.lifted_[here, :] = lifted
        lifted = lifted.astype(F32)
        factor = lax.rsqrt(jnp.mean(lifted * lifted, axis=-1, keepdims=True) + EPSILON)
        n.factor_[here, :] = jnp.broadcast_to(factor, (128, 128))
        normed = (lifted * factor * gain).astype(BF16)
        n.normed_[here, :] = normed
        n.qkv_[here, :] = dot(normed, n.in_w_[...]).astype(BF16)

    loop(4, forward)
    swap = pltpu.make_async_remote_copy(
        src_ref=n.qkv_.at[:, pl.ds(128, 384)], dst_ref=n.kv_far_,
        send_sem=swap_send.at[0], recv_sem=swap_recv.at[0], device_id=peer, device_id_type=MESH,
    )
    swap.start()
    links.low.receive()

    def cotangent_of_mixed(c):
        low = n.low_r_[...].reshape(512, 768)
        chunk = rows_of(c, 256)
        n.d_mixed_[:, chunk] = dot_cols(low, n.up_w_[chunk, :]).astype(BF16)

    loop(6, cotangent_of_mixed)
    n.d_att_[...] = dot(n.d_mixed_[...], n.o_t_[...]).astype(BF16)
    n.dkv_own_[...] = jnp.zeros((512, 384), F32)
    n.dkv_far_[...] = jnp.zeros((512, 384), F32)
    swap.wait()

    scale = 1.0 / math.sqrt(128)

    def send_pair(name, t, value):
        half = value.astype(BF16)
        getattr(n, name + "A_s_")[pl.ds(2 * t, 2)] = half[:, :768].reshape(2, 64, 768)
        getattr(n, name + "B_s_")[pl.ds(2 * t, 2)] = half[:, 768:].reshape(2, 64, 768)
        for j in (2 * t, 2 * t + 1):
            to, side = lax.rem(j, 4), j // 4
            getattr(links, name + "A").start_one(2 * lax.rem(to - lax.rem(b, 4) + 4, 4) + side)

            @pl.when(side != z)
            def _():
                getattr(links, name + "B").start_one(to)

    def attend(t):
        here = rows_of(t, 128)
        q, da = n.qkv_[here, :128], n.d_att_[here, :]
        blocks = (
            (n.qkv_[:, 128:256], n.qkv_[:, 256:], n.dkv_own_),
            (n.kv_far_[:, :128], n.kv_far_[:, 128:], n.dkv_far_),
        )
        scores = [dot_cols(q, k) * scale for k, _, _ in blocks]
        sums = sum(jnp.sum(jnp.exp(x), axis=1, keepdims=True) for x in scores)
        log_total = jnp.log(sums)
        probs = [jnp.exp(x - log_total) for x in scores]
        dprobs = [dot_cols(da, v) for _, v, _ in blocks]
        inner = sum(jnp.sum(p * d, axis=1, keepdims=True) for p, d in zip(probs, dprobs))
        att = jnp.zeros((128, 256), F32)
        dq = jnp.zeros((128, 128), F32)
        for (k, v, total_ref), p, d in zip(blocks, probs, dprobs):
            ds = (p * (d - inner)).astype(BF16)
            pb = p.astype(BF16)
            att = att + dot(pb, v)
            dq = dq + dot(ds, k)
            total_ref[:, :128] += dot_rows(ds, q) * scale
            total_ref[:, 128:] += dot_rows(pb, da)
        att = att.astype(BF16)
        n.att_[here, :] = att
        n.dqkv_[here, :128] = (dq * scale).astype(BF16)
        send_pair("mixed", t, dot(att, n.o_w_[...]))

    loop(4, attend)
    n.dkv_s_[...] = n.dkv_far_[...].astype(BF16)
    swap_back = pltpu.make_async_remote_copy(
        src_ref=n.dkv_s_, dst_ref=n.dkv_r_, send_sem=swap_send.at[1], recv_sem=swap_recv.at[1],
        device_id=peer, device_id_type=MESH,
    )
    swap_back.start()
    swap_back.wait()
    n.dqkv_[:, 128:] = (n.dkv_own_[...] + n.dkv_r_[...].astype(F32)).astype(BF16)

    def back_through_projections(t):
        send_pair("dn", t, dot(n.dqkv_[rows_of(t, 128), :], n.in_t_[...]))

    loop(4, back_through_projections)

    def first_hop(name):
        over_x, over_z = getattr(links, name + "A"), getattr(links, name + "B")
        over_x.keep()
        over_x.receive()
        there = 1 - z
        value = over_x.result[there].astype(F32)
        for j in range(1, 4):
            value = value + over_x.result[2 * j + there].astype(F32)
        getattr(n, name + "C_s_")[0] = value.astype(BF16)
        getattr(links, name + "C").start()
        over_z.receive()
        value = getattr(n, name + "B_s_")[pl.ds(4 * z, 4)].astype(F32)
        value = value + over_z.result[...].astype(F32)
        getattr(n, name + "D_s_")[...] = value.astype(BF16)
        getattr(links, name + "D").start()

    def second_hop(name):
        getattr(links, name + "C").receive()
        left = getattr(links, name + "C").result[0].astype(F32)
        for j in range(4):
            left = left + getattr(links, name + "A").result[2 * j + z].astype(F32)
        getattr(links, name + "D").receive()
        return jnp.concatenate([left, total(getattr(links, name + "D").result, 4)], axis=1)

    first_hop("mixed")

    def projection_grads(c):
        chunk = rows_of(c, 384)
        first = dot_rows(n.normed_[:, chunk], n.dqkv_[...]).astype(BF16)
        second = dot_rows(n.d_mixed_[:, chunk], n.att_[...]).astype(BF16)
        both = jnp.concatenate([first[:, :448], second[:, :192]], axis=1)
        n.proj_c_s_[pl.ds(2 * c, 2)] = both.reshape(2, 2, 96, 640)

    loop(4, projection_grads)
    links.proj_c.start()

    here = rows_of(b, 64)
    n.conv_[...] = dot(n.emb_[b], n.conv_w_[...])
    center = n.emb_[b, :, 768:1536].astype(F32)
    n.tower_[...] = (center + jax.nn.gelu(n.conv_[...])).astype(BF16)
    lifted = n.lifted_[here, :].astype(F32)
    factor = n.factor_[here, 0:1]
    first_hop("dn")
    updated = (lifted + second_hop("mixed")).astype(BF16)

    def select_into(target, value, matrix):
        for half in range(2):
            moved = dot(value[:, 768 * half : 768 * half + 768], matrix[...]).astype(BF16)
            for j in range(4):
                target[4 * half + j] = moved[:, 256 * j : 256 * j + 256]

    select_into(n.upd_s_, updated, n.select_)
    lowered = dot(updated, n.up_w_[...])
    features = n.tower_[...].astype(F32) + jnp.concatenate([lowered, lowered], axis=0)
    n.feat_s_[0] = dot_rows(order, features.astype(BF16)).astype(BF16)
    links.feat.start()

    def core_sum(name):
        getattr(links, name + "_c").receive()
        mine = getattr(n, name + "_c_s_")
        far = getattr(n, name + "_c_r_")
        target = getattr(n, name + "_s_")

        def add(j):
            target[j] = (mine[j, h].astype(F32) + far[0, j].astype(F32)).astype(BF16)

        loop(8, add)
        getattr(links, name).start()

    d_normed = second_hop("dn").astype(BF16).astype(F32)
    d_updated = n.d_mixed_[here, :].astype(F32)
    gained = d_normed * gain
    shared = jnp.mean(gained * lifted, axis=-1, keepdims=True) * (factor * factor * factor)
    d_lifted = (gained * factor - lifted * shared).astype(BF16).astype(F32) + d_updated
    d_lifted = d_lifted.astype(BF16)
    for half in range(2):
        moved = dot(d_lifted[:, 768 * half : 768 * half + 768], n.select_down_[...]).astype(BF16)
        for j in range(8):
            n.dl_s_[j, :, 128 * half : 128 * half + 128] = moved[:, 128 * j : 128 * j + 128]
    links.dl.start()
    d_pooled = dot_cols(d_lifted, n.down_w_[...]) * 0.5
    d_tower = n.blk_r_[0].astype(F32) + jnp.concatenate([d_pooled, d_pooled], axis=0)
    d_tower = d_tower.astype(BF16)
    d_conv = (d_tower.astype(F32) * gelu_grad(n.conv_[...])).astype(BF16)
    moved = dot(d_conv, n.select_conv_[...]).astype(BF16)
    for j in range(8):
        n.dc_s_[j] = moved[:, 128 * j : 128 * j + 128]
    links.dc.start()
    links.upd.start()
    hots = one_hots(b)
    d_stem = jnp.zeros((128, 768), F32)
    for step in range(3):
        d_emb = dot_cols(d_conv, n.conv_w_[768 * step : 768 * step + 768, :])
        if step == 1:
            d_emb = d_emb + d_tower.astype(F32)
        hot = jnp.concatenate([hots[step], hots[3 + step]], axis=0)
        d_stem = d_stem + dot_rows(hot, d_emb.astype(BF16))
    moved = dot(d_stem[:64].astype(BF16), n.select_conv_[...]).astype(BF16)
    for j in range(8):
        n.ds_s_[j] = moved[:, 128 * j : 128 * j + 128]
    links.ds.start()
    d_gain = jnp.sum(d_normed * (lifted * factor), axis=0, keepdims=True).astype(BF16)
    d_gain = jnp.broadcast_to(d_gain, (16, 1536))
    for half in range(2):
        moved = dot(d_gain[:, 768 * half : 768 * half + 768], n.select_down_[...])
        for j in range(8):
            n.gain_s_[j, :, 128 * half : 128 * half + 128] = moved[:8, 128 * j : 128 * j + 128]
    links.gain.start()
    core_sum("proj")

    def select_low(t):
        rows = rows_of(t, 128)
        low = n.low_r_[pl.ds(2 * t, 2)].reshape(128, 768)
        n.low_sel_[rows, :] = dot(low, n.select_[...]).astype(BF16)

    loop(4, select_low)

    links.dl.receive()
    down = dot_rows(n.dl_r_[...].reshape(512, 256), n.pooled_[...]).astype(BF16)
    n.down_c_s_[:, :, :, :768] = down.reshape(8, 2, 16, 768)
    links.gain.receive()
    first_row = jnp.logical_and(iota((64, 128), 0) % 8 == 0, iota((64, 128), 1) == 0)
    gains = dot_rows(n.gain_r_[...].reshape(64, 256).astype(BF16), zero_one(first_row)).astype(BF16)
    n.down_c_s_[:, :, :, 768:] = gains.reshape(8, 2, 16, 128)
    links.down_c.start()
    n.conv_acc_[...] = jnp.zeros((128, 2304), F32)
    links.dc.receive()

    def conv_grads(t):
        pair = pl.ds(2 * t, 2)
        left = n.dc_r_[pair].reshape(256, 128)
        n.conv_acc_[...] += dot_rows(left, n.emb_[pair].reshape(256, 2304))

    loop(4, conv_grads)
    core_sum("down")
    links.ds.receive()
    same = zero_one(iota((512, 128), 0) % 64 == iota((512, 128), 1))
    stem = dot_rows(n.ds_r_[...].reshape(512, 128), same)
    n.conv_c_s_[:, :, 0:8, :] = n.conv_acc_[:, :1280].reshape(8, 2, 8, 1280).astype(BF16)
    rest = jnp.concatenate([n.conv_acc_[:, 1280:], stem, jnp.zeros((128, 128), F32)], axis=1)
    n.conv_c_s_[:, :, 8:16, :] = rest.reshape(8, 2, 8, 1280).astype(BF16)
    links.conv_c.start()
    links.upd.receive()
    up = dot_rows(n.low_sel_[...], n.upd_r_[...].reshape(512, 256)).astype(BF16)
    n.up_c_s_[...] = up.reshape(8, 2, 64, 256)
    links.up_c.start()
    core_sum("conv")
    core_sum("up")

    links.proj.receive()
    proj = total(n.proj_r_, 8)
    n.g_q[...] = proj[:, :128]
    n.g_k[...] = proj[:, 128:256]
    n.g_v[...] = proj[:, 256:448]
    n.g_o[...] = proj[:, 448:]
    links.feat.receive()
    n.features[...] = n.feat_r_[0]
    links.down.receive()
    down = total(n.down_r_, 8)
    n.g_down[0:6, :] = down[0:6, :768]
    n.g_down[6:12, :] = down[8:14, :768]
    lane = iota((16, 128), 1)
    wanted = jnp.where(lane < 6, lane, lane + 2)
    hit = jnp.logical_and(iota((16, 128), 0) == wanted, lane < 12)
    n.g_gain[...] = jnp.sum(jnp.where(hit, down[:, 768:769], 0.0), axis=0, keepdims=True)
    links.up.receive()
    n.last_s_[...] = total(n.up_r_, 8).reshape(8, 8, 256)
    links.last.start()
    links.conv.receive()
    conv = total(n.conv_r_, 8)
    n.g_conv[0] = conv[0:6, :768]
    n.g_conv[1] = jnp.concatenate([conv[0:6, 768:], conv[8:14, :256]], axis=1)
    n.g_conv[2] = conv[8:14, 256:1024]
    stem = conv[8:16, 1024:1152].astype(BF16)
    for code in range(4):
        taps = iota((128, 15), 0) == 4 * iota((128, 15), 1) + code
        n.g_stem[:, code, :] = dot(stem, zero_one(taps))[:6]
    lane = iota((192, 256), 1)
    tight = jnp.logical_and(iota((192, 256), 0) == 6 * (lane // 8) + lane % 8, lane % 8 < 6)
    tight = zero_one(tight)
    links.last.receive()
    for j in range(4):
        pieces = [dot_cols(n.last_r_[2 * j + k].astype(BF16), tight) for k in range(2)]
        n.g_up[:, 384 * j : 384 * j + 384] = jnp.concatenate(pieces, axis=1)[:6]
    for link in vars(links).values():
        link.drain()


def finish_body(*refs):
    number = len(OUTPUTS)
    copies = [
        pltpu.make_async_copy(source, target, refs[-1].at[k])
        for k, (source, target) in enumerate(zip(refs[:number], refs[number : 2 * number]))
    ]
    for copy in copies:
        copy.start()
    for copy in copies:
        copy.wait()


def per_device(
    base_codes,
    stem_weight,
    conv_weight,
    down_weight,
    norm_gain,
    query_weight,
    key_weight,
    value_weight,
    output_weight,
    up_weight,
    cotangent,
):
    vmem, anywhere = pl.BlockSpec(memory_space=pltpu.VMEM), pl.BlockSpec(memory_space=pl.ANY)
    semaphores = [pltpu.SemaphoreType.DMA((7,))] + [pltpu.SemaphoreType.DMA((2,))] * 2
    shapes = {name: x[0] for name, x in SCRATCH.items()}
    for name, pattern in LINKS.items():
        semaphores += [
            pltpu.SemaphoreType.DMA((pattern.count,)),
            pltpu.SemaphoreType.DMA((shapes[name + "_r"][0],)),
        ]
    out_shape = [jax.ShapeDtypeStruct(shape, dtype) for shape, dtype in OUTPUTS.values()]
    results = pl.pallas_call(
        kernel_body,
        out_shape=out_shape,
        in_specs=[vmem] * 4 + [anywhere] * 7,
        out_specs=[vmem] * len(OUTPUTS),
        scratch_shapes=[pltpu.VMEM(shape, dtype) for shape, dtype in SCRATCH.values()] + semaphores,
        compiler_params=pltpu.CompilerParams(
            collective_id=0, has_side_effects=True, vmem_limit_bytes=60 * 1024 * 1024
        ),
        name="step",
    )(
        base_codes,
        cotangent[0],
        norm_gain,
        stem_weight,
        conv_weight.reshape(2304, 768),
        down_weight,
        query_weight,
        key_weight,
        value_weight.T,
        output_weight,
        up_weight,
    )
    features, g_stem, g_conv, g_down, g_gain, g_up, g_q, g_k, g_v, g_o = pl.pallas_call(
        finish_body,
        out_shape=out_shape,
        in_specs=[anywhere] * len(OUTPUTS),
        out_specs=[anywhere] * len(OUTPUTS),
        scratch_shapes=[pltpu.SemaphoreType.DMA((len(OUTPUTS),))],
        name="finish",
    )(*results)
    return (
        features[None],
        g_stem.transpose(2, 1, 0),
        g_conv.transpose(0, 2, 1),
        g_down.T,
        g_gain[0, :12],
        g_up.T,
        g_q,
        g_k,
        g_v,
        g_o,
    )


def solution(mesh):
    placed = (
        P("batch", "seq"),
        P(),
        P(),
        P(),
        P(),
        P(None, "batch"),
        P(None, "batch"),
        P(None, "batch"),
        P("batch", None),
        P(),
        P("batch", "seq", None),
    )
    return jax.shard_map(
        per_device,
        mesh=mesh,
        in_specs=placed,
        out_specs=(
            P("batch", "seq", None),
            P(None, None, ("seq", "batch")),
            P(None, None, ("seq", "batch")),
            P(None, ("seq", "batch")),
            P(("seq", "batch")),
            P(None, ("seq", "batch")),
            P("seq", "batch"),
            P("seq", "batch"),
            P("seq", "batch"),
            P("seq", "batch"),
        ),
        check_vma=False,
    )
```

```python
import functools
import math

import jax
import jax.numpy as jnp
from jax import lax
from jax.experimental import pallas as pl
from jax.experimental.pallas import tpu as pltpu
from jax.sharding import PartitionSpec as P

EPSILON = 1e-06
MESH = pl.DeviceIdType.MESH
F32 = jnp.float32
BF16 = jnp.bfloat16
SEQ = 16
BATCH = 8


class OverBatch:
    count = BATCH

    def dst(self, i, s, b):
        j = lax.rem(b + i, BATCH)
        return j, s, j, b

    def src(self, i, s, b):
        j = lax.rem(b + BATCH - i, BATCH)
        return j, s, j


class Share:
    count = BATCH

    def dst(self, i, s, b):
        return 0, s, lax.rem(b + i, BATCH), b

    def src(self, i, s, b):
        j = lax.rem(b + BATCH - i, BATCH)
        return j, s, j


class OverQuads:
    count = SEQ // 2

    def dst(self, i, s, b):
        j = lax.rem(s // 2 + i, SEQ // 2)
        return j, 2 * j + lax.rem(s, 2), b, s // 2

    def src(self, i, s, b):
        j = lax.rem(s // 2 + SEQ // 2 - i, SEQ // 2)
        return j, 2 * j + lax.rem(s, 2), b


class QuadShare:
    count = SEQ // 2

    def dst(self, i, s, b):
        j = lax.rem(s // 2 + i, SEQ // 2)
        return 0, 2 * j + lax.rem(s, 2), b, s // 2

    def src(self, i, s, b):
        j = lax.rem(s // 2 + SEQ // 2 - i, SEQ // 2)
        return j, 2 * j + lax.rem(s, 2), b


class Core:
    count = 1

    def dst(self, i, s, b):
        other = 1 - lax.rem(s, 2)
        return other, s - lax.rem(s, 2) + other, b, 0

    def src(self, i, s, b):
        return 0, s + 1 - 2 * lax.rem(s, 2), b


class XBlocks:
    count = 8

    def dst(self, i, s, b):
        z, x = b // 4, lax.rem(b, 4)
        to, side = lax.rem(x + i // 2, 4), lax.rem(i, 2)
        return 4 * side + to, s, 4 * z + to, 2 * x + side

    def src(self, i, s, b):
        z, x = b // 4, lax.rem(b, 4)
        at, side = lax.rem(x + 4 - i // 2, 4), lax.rem(i, 2)
        return 2 * at + side, s, 4 * z + at


class ZBlocks:
    count = 4

    def dst(self, i, s, b):
        other = 1 - b // 4
        return 4 * other + i, s, 4 * other + lax.rem(b, 4), i

    def src(self, i, s, b):
        return i, s, 4 * (1 - b // 4) + lax.rem(b, 4)


class ZOne:
    count = 1

    def dst(self, i, s, b):
        return 0, s, 4 * (1 - b // 4) + lax.rem(b, 4), 0

    def src(self, i, s, b):
        return 0, s, 4 * (1 - b // 4) + lax.rem(b, 4)


class XOne:
    count = 4

    def dst(self, i, s, b):
        z, x = b // 4, lax.rem(b, 4)
        to = lax.rem(x + i, 4)
        return to, s, 4 * z + to, x

    def src(self, i, s, b):
        z, x = b // 4, lax.rem(b, 4)
        at = lax.rem(x + 4 - i, 4)
        return at, s, 4 * z + at


class Codes:
    count = 2 * BATCH

    def dst(self, i, s, b):
        return 0, 2 * b + lax.rem(i, 2), lax.rem(b + i // 2, BATCH), s

    def src(self, i, s, b):
        return i, i, s // 2


class ToBlock:
    count = 1

    def dst(self, i, s, b):
        return 0, 2 * b + s // BATCH, lax.rem(s, BATCH), 0

    def src(self, i, s, b):
        return 0, BATCH * lax.rem(s, 2) + b, s // 2


class ToOwner:
    count = 1

    def dst(self, i, s, b):
        return 0, BATCH * lax.rem(s, 2) + b, s // 2, 0

    def src(self, i, s, b):
        return 0, 2 * b + s // BATCH, lax.rem(s, BATCH)


class Link:
    def __init__(self, pattern, source, result, sends, receives, s, b):
        self.pattern, self.source, self.result = pattern, source, result
        self.sends, self.receives, self.s, self.b = sends, receives, s, b

    def copy(self, i):
        piece, target_s, target_b, slot = self.pattern.dst(i, self.s, self.b)
        away = jnp.logical_or(target_s != self.s, target_b != self.b)
        return away, pltpu.make_async_remote_copy(
            src_ref=self.source(piece),
            dst_ref=self.result.at[slot],
            send_sem=self.sends.at[i],
            recv_sem=self.receives.at[slot],
            device_id=(target_s, target_b),
            device_id_type=MESH,
        )

    def keep_one(self, i):
        piece, target_s, target_b, slot = self.pattern.dst(i, self.s, self.b)
        home = jnp.logical_and(target_s == self.s, target_b == self.b)

        @pl.when(home)
        def _():
            self.result[slot] = self.source(piece)[...]

    def each(self, action):
        loop(self.pattern.count, action)

    def start_one(self, i):
        away, copy = self.copy(i)
        pl.when(away)(copy.start)

    def keep(self):
        self.each(self.keep_one)

    def start(self):
        self.each(self.start_one)
        self.keep()

    def receive(self):
        def wait(i):
            slot, other_s, other_b = self.pattern.src(i, self.s, self.b)
            away = jnp.logical_or(other_s != self.s, other_b != self.b)
            copy = pltpu.make_async_remote_copy(
                src_ref=self.result.at[slot],
                dst_ref=self.result.at[slot],
                send_sem=self.sends.at[i],
                recv_sem=self.receives.at[slot],
                device_id=(other_s, other_b),
                device_id_type=MESH,
            )
            pl.when(away)(copy.wait_recv)

        self.each(wait)

    def drain(self):
        def wait(i):
            away, copy = self.copy(i)
            pl.when(away)(copy.wait_send)

        self.each(wait)


def dot(left, right):
    return jnp.dot(left, right, preferred_element_type=F32)


def dot_rows(left, right):
    return lax.dot_general(left, right, (((0,), (0,)), ((), ())), preferred_element_type=F32)


def dot_cols(left, right):
    return lax.dot_general(left, right, (((1,), (1,)), ((), ())), preferred_element_type=F32)


def iota(shape, dim):
    return lax.broadcasted_iota(jnp.int32, shape, dim)


def zero_one(mask):
    return jnp.where(mask, 1.0, 0.0).astype(BF16)


def gelu_grad(x):
    inner = math.sqrt(2.0 / math.pi) * (x + 0.044715 * x * x * x)
    t = jnp.tanh(inner)
    slope = math.sqrt(2.0 / math.pi) * (1.0 + 3 * 0.044715 * x * x)
    return 0.5 * (1.0 + t) + 0.5 * x * (1.0 - t * t) * slope


def total(ref, count):
    value = ref[0].astype(F32)
    for j in range(1, count):
        value = value + ref[j].astype(F32)
    return value


def loop(count, step):
    def body(i, carry):
        step(i)
        return carry

    lax.fori_loop(0, count, body, 0)


def rows_of(i, size):
    return pl.ds(pl.multiple_of(i * size, size), size)


INPUTS = dict(codes=0, cot=0, gain=0, stem=0, conv_h=0, down_h=0, q_h=0, k_h=0, v_h=0, o_h=0, up_h=0)
OUTPUTS = dict(
    features=((128, 768), BF16),
    g_stem=((6, 4, 15), F32),
    g_conv=((3, 6, 768), F32),
    g_down=((12, 768), F32),
    g_gain=((1, 128), F32),
    g_up=((6, 1536), F32),
    g_q=((96, 128), F32),
    g_k=((96, 128), F32),
    g_v=((96, 192), F32),
    g_o=((96, 192), F32),
)
SCRATCH = dict(
    conv_w=((2304, 768), BF16),
    down_w=((768, 1536), BF16),
    in_w=((1536, 512), BF16),
    in_t=((512, 1536), BF16),
    o_w=((256, 1536), BF16),
    o_t=((1536, 256), BF16),
    up_w=((1536, 768), BF16),
    stem_f=((64, 768), F32),
    stem_w=((128, 768), BF16),
    select_conv=((768, 1024), BF16),
    select_down=((768, 1024), BF16),
    codes_s=((1, 8, 128), F32),
    codes_r=((16, 8, 128), F32),
    blk_s=((1, 128, 768), BF16),
    blk_r=((1, 128, 768), BF16),
    low_s=((1, 64, 768), BF16),
    low_r=((8, 64, 768), BF16),
    code=((2, 640, 128), F32),
    picked=((2, 528, 128), F32),
    emb=((8, 128, 2304), BF16),
    conv=((128, 768), F32),
    tower=((128, 768), BF16),
    pooled=((512, 768), BF16),
    lifted=((512, 1536), BF16),
    factor=((512, 128), F32),
    normed=((512, 1536), BF16),
    qkv=((512, 512), BF16),
    kv_far=((512, 384), BF16),
    d_mixed=((512, 1536), BF16),
    d_att=((512, 256), BF16),
    att=((512, 256), BF16),
    dqkv=((512, 512), BF16),
    dkv_own=((512, 384), F32),
    dkv_far=((512, 384), F32),
    dkv_s=((512, 384), BF16),
    dkv_r=((512, 384), BF16),
    conv_acc=((128, 2304), F32),
    w_up=((256, 768), BF16),
    w_down=((512, 768), BF16),
    pick_in=((128, 512), BF16),
    pick_down=((128, 768), BF16),
    lpA_s=((8, 64, 384), BF16),
    lpA_r=((8, 64, 384), BF16),
    lpB_s=((8, 64, 384), BF16),
    lpB_r=((4, 64, 384), BF16),
    lpC_s=((1, 64, 384), BF16),
    lpC_r=((1, 64, 384), BF16),
    lpD_s=((4, 64, 384), BF16),
    lpD_r=((4, 64, 384), BF16),
    pdA_s=((8, 64, 384), BF16),
    pdA_r=((8, 64, 384), BF16),
    pdB_s=((8, 64, 384), BF16),
    pdB_r=((4, 64, 384), BF16),
    pdC_s=((1, 64, 384), BF16),
    pdC_r=((1, 64, 384), BF16),
    pdD_s=((4, 64, 384), BF16),
    pdD_r=((4, 64, 384), BF16),
    feat_s=((1, 128, 768), BF16),
    feat_r=((1, 128, 768), BF16),
    mean_s=((1, 8, 128), F32),
    mean_r=((8, 8, 128), F32),
    gain_s=((1, 8, 128), F32),
    gain_r=((8, 8, 128), F32),
    dc_s=((8, 128, 128), BF16),
    dc_r=((8, 128, 128), BF16),
    ds_s=((8, 64, 128), BF16),
    ds_r=((8, 64, 128), BF16),
    up_s=((8, 16, 768), BF16),
    up_r=((8, 16, 768), BF16),
    first_s=((8, 16, 768), BF16),
    first_r=((8, 16, 768), BF16),
    mnl_c_s=((8, 2, 48, 1024), BF16),
    mnl_c_r=((1, 8, 48, 1024), BF16),
    mnl_s=((8, 48, 1024), BF16),
    mnl_r=((8, 48, 1024), BF16),
    mn_s=((1, 48, 768), BF16),
    mn_r=((8, 48, 768), BF16),
    full_r=((1, 8, 48, 768), BF16),
    summed=((768, 768), BF16),
    slices=((512, 512), BF16),
    rest=((512, 256), BF16),
    down_c_s=((8, 2, 16, 768), BF16),
    down_c_r=((1, 8, 16, 768), BF16),
    down_s=((8, 16, 768), BF16),
    down_r=((8, 16, 768), BF16),
    conv_c_s=((8, 2, 16, 1280), BF16),
    conv_c_r=((1, 8, 16, 1280), BF16),
    conv_s=((8, 16, 1280), BF16),
    conv_r=((8, 16, 1280), BF16),
)
LINKS = dict(
    codes=Codes(),
    blk=ToBlock(),
    low=Share(),
    lpA=XBlocks(),
    lpB=ZBlocks(),
    lpC=ZOne(),
    lpD=XOne(),
    pdA=XBlocks(),
    pdB=ZBlocks(),
    pdC=ZOne(),
    pdD=XOne(),
    feat=ToOwner(),
    mean=Share(),
    gain=Share(),
    dc=OverBatch(),
    ds=OverBatch(),
    up=OverBatch(),
    first=OverBatch(),
    mnl_c=Core(),
    mnl=OverQuads(),
    mn=QuadShare(),
    full=Core(),
    down_c=Core(),
    down=OverQuads(),
    conv_c=Core(),
    conv=OverQuads(),
)


class Namespace:
    pass


def kernel_body(*refs):
    names = list(INPUTS) + list(OUTPUTS) + [x + "_" for x in SCRATCH]
    n = Namespace()
    for name, ref in zip(names, refs):
        setattr(n, name, ref)
    semaphores = refs[len(names) :]
    weight_sems, swap_send, swap_recv = semaphores[:3]
    s, b = lax.axis_index("seq"), lax.axis_index("batch")
    h = lax.rem(s, 2)
    z = b // 4
    peer = (s + 1 - 2 * h, b)
    links = Namespace()
    for k, (name, pattern) in enumerate(LINKS.items()):
        sent = n.mn_r_ if name == "full" else getattr(n, name + "_s_")
        if name == "full":
            source = lambda piece, sent=sent: sent
        elif name.endswith("_c"):
            source = lambda piece, sent=sent: sent.at[:, piece]
        else:
            source = lambda piece, sent=sent: sent.at[piece]
        result = getattr(n, name + "_r_")
        link = Link(pattern, source, result, semaphores[3 + 2 * k], semaphores[4 + 2 * k], s, b)
        setattr(links, name, link)

    barrier = pltpu.get_barrier_semaphore()
    for link in (links.codes, links.low, links.mnl, links.mnl_c, links.feat):
        pattern = link.pattern

        def greet(i, pattern=pattern):
            _, other_s, other_b = pattern.src(i, s, b)

            @pl.when(jnp.logical_or(other_s != s, other_b != b))
            def _():
                pl.semaphore_signal(
                    barrier, inc=1, device_id=(other_s, other_b), device_id_type=MESH
                )

        loop(pattern.count, greet)
    own_window = (b == s // 2).astype(jnp.int32)
    own_block = own_window * (s == BATCH * h + b).astype(jnp.int32)
    expected = 16 + 7 + 7 + 1 + 1 - own_window - own_block

    weights = [
        pltpu.make_async_copy(source, target, weight_sems.at[k])
        for k, (source, target) in enumerate(
            [
                (n.q_h, n.in_w_.at[:, pl.ds(0, 128)]),
                (n.k_h, n.in_w_.at[:, pl.ds(128, 128)]),
                (n.v_h, n.in_t_.at[pl.ds(256, 192)]),
                (n.o_h, n.o_w_.at[pl.ds(0, 192)]),
                (n.conv_h, n.conv_w_),
                (n.down_h, n.down_w_),
                (n.up_h, n.up_w_),
            ]
        )
    ]
    for copy in weights:
        copy.start()

    row, column = iota((128, 128), 0), iota((128, 128), 1)
    order = zero_one(column == jnp.where(row < 64, 2 * row, 2 * row - 127))
    codes = jnp.broadcast_to((n.codes[...] + 1).astype(F32), (8, 128)).astype(BF16)
    n.codes_s_[0] = dot_cols(codes, order)
    n.blk_s_[0] = dot(order, n.cot[...]).astype(BF16)

    pl.semaphore_wait(barrier, expected)
    links.codes.start()
    links.blk.start()

    def fill(c):
        within = iota((1, 128), 1)
        i, m = lax.rem(within, 8), within // 8
        good = i < 6
        rows = iota((768, 128), 0)
        place = rows_of(c, 128)
        n.select_conv_[:, place] = zero_one(rows == jnp.where(good, 6 * (8 * m + c) + i, -1))
        wanted = 12 * (8 * (m // 2) + c) + 6 * lax.rem(m, 2) + i
        n.select_down_[:, place] = zero_one(rows == jnp.where(good, wanted, -1))

    loop(8, fill)
    for t in range(15):
        n.stem_f_[4 * t : 4 * t + 4, :] = n.stem[t].astype(F32)
    n.stem_f_[60:, :] = jnp.zeros((4, 768), F32)
    n.stem_w_[:64, :] = n.stem_f_[...].astype(BF16)
    n.stem_w_[64:, :] = jnp.zeros((64, 768), BF16)
    for copy in weights[:4]:
        copy.wait()
    n.o_w_[192:, :] = jnp.zeros((64, 1536), BF16)
    n.in_t_[448:, :] = jnp.zeros((64, 1536), BF16)
    eye, eye2 = zero_one(row == column), zero_one(iota((256, 256), 0) == iota((256, 256), 1))
    n.in_t_[:128, :] = dot_cols(eye, n.in_w_[:, :128]).astype(BF16)
    n.in_t_[128:256, :] = dot_cols(eye, n.in_w_[:, 128:256]).astype(BF16)
    n.in_w_[:, 256:] = dot_rows(n.in_t_[256:, :], eye2).astype(BF16)
    n.o_t_[...] = dot_rows(n.o_w_[...], eye2).astype(BF16)

    links.codes.receive()
    ones = jnp.ones((128, 128), BF16)
    for i in range(10):
        place = BATCH * h + (i - 1)
        inside = jnp.logical_and(place >= 0, place < 16)
        line = n.codes_r_[jnp.clip(place, 0, 15)][0:1]
        line = jnp.where(inside, line, 0.0)
        spread = dot(jnp.where(row == column, line, 0.0).astype(BF16), ones)
        n.code_[0, 64 * i : 64 * i + 64] = spread[:64]
        n.code_[1, 64 * i : 64 * i + 64] = spread[64:]
    lane_tap = iota((1, 128), 1) // 4
    lane_code = (iota((1, 128), 1) % 4 + 1).astype(F32)
    for parity in range(2):
        picked = jnp.zeros((528, 128), F32)
        for tap in range(15):
            offset = parity + tap - 7
            stream, shift = offset % 2, (offset - offset % 2) // 2
            begin = 56 + shift
            picked = jnp.where(lane_tap == tap, n.code_[stream, begin : begin + 528, :], picked)
        where = iota((528, 128), 0) - 8 + 512 * h
        inside = jnp.logical_and(where >= 0, where < 1024)
        n.picked_[parity] = jnp.where(inside, picked, 0.0)

    links.blk.receive()
    pairs = n.blk_r_[0].astype(F32)
    n.low_s_[0] = (pairs[:64] + pairs[64:]).astype(BF16)
    links.low.start()

    def one_hots(j):
        found = []
        for parity in range(2):
            near = n.picked_[parity, pl.ds(pl.multiple_of(64 * j, 64), 80), :]
            for step in (-4, 0, 4):
                found.append(zero_one(near[8 + step : 72 + step] == lane_code))
        return found

    def embed(j):
        value = dot(jnp.concatenate(one_hots(j), axis=0), n.stem_w_[...]).astype(BF16)
        for parity in range(2):
            for step in range(3):
                begin = 64 * (3 * parity + step)
                n.emb_[j, 64 * parity : 64 * parity + 64, 768 * step : 768 * step + 768] = value[
                    begin : begin + 64
                ]

    loop(8, embed)
    for copy in weights[4:]:
        copy.wait()
    gain = n.gain[...].reshape(1, 1536)

    def forward(t):
        pair = pl.ds(2 * t, 2)
        here = rows_of(t, 128)
        conv = dot(n.emb_[pair].reshape(256, 2304), n.conv_w_[...])
        center = n.emb_[pair, :, 768:1536].reshape(256, 768).astype(F32)
        tower = (center + jax.nn.gelu(conv)).astype(BF16)
        halves = tower.astype(F32).reshape(2, 2, 64, 768)
        pooled = (0.5 * (halves[:, 0] + halves[:, 1])).astype(BF16).reshape(128, 768)
        n.pooled_[here, :] = pooled
        lifted = dot(pooled, n.down_w_[...]).astype(BF16)
        n.lifted_[here, :] = lifted
        lifted = lifted.astype(F32)
        factor = lax.rsqrt(jnp.mean(lifted * lifted, axis=-1, keepdims=True) + EPSILON)
        n.factor_[here, :] = jnp.broadcast_to(factor, (128, 128))
        normed = (lifted * factor * gain).astype(BF16)
        n.normed_[here, :] = normed
        n.qkv_[here, :] = dot(normed, n.in_w_[...]).astype(BF16)

    loop(4, forward)
    swap = pltpu.make_async_remote_copy(
        src_ref=n.qkv_.at[:, pl.ds(128, 384)], dst_ref=n.kv_far_,
        send_sem=swap_send.at[0], recv_sem=swap_recv.at[0], device_id=peer, device_id_type=MESH,
    )
    swap.start()
    n.w_up_[...] = dot(n.o_w_[...], n.up_w_[...]).astype(BF16)
    gained = (n.in_t_[...].astype(F32) * gain).astype(BF16)
    n.w_down_[...] = dot_cols(gained, n.down_w_[...]).astype(BF16)
    links.low.receive()

    def cotangent_of_mixed(c):
        low = n.low_r_[...].reshape(512, 768)
        chunk = rows_of(c, 256)
        n.d_mixed_[:, chunk] = dot_cols(low, n.up_w_[chunk, :]).astype(BF16)

    loop(6, cotangent_of_mixed)
    n.d_att_[...] = dot(n.d_mixed_[...], n.o_t_[...]).astype(BF16)
    n.dkv_own_[...] = jnp.zeros((512, 384), F32)
    n.dkv_far_[...] = jnp.zeros((512, 384), F32)
    swap.wait()

    scale = 1.0 / math.sqrt(128)

    def send_pair(name, t, value):
        half = value.astype(BF16)
        getattr(n, name + "A_s_")[pl.ds(2 * t, 2)] = half[:, :384].reshape(2, 64, 384)
        getattr(n, name + "B_s_")[pl.ds(2 * t, 2)] = half[:, 384:].reshape(2, 64, 384)
        for j in (2 * t, 2 * t + 1):
            to, side = lax.rem(j, 4), j // 4
            getattr(links, name + "A").start_one(2 * lax.rem(to - lax.rem(b, 4) + 4, 4) + side)

            @pl.when(side != z)
            def _():
                getattr(links, name + "B").start_one(to)

    def attend(t):
        here = rows_of(t, 128)
        q, da = n.qkv_[here, :128], n.d_att_[here, :]
        blocks = (
            (n.qkv_[:, 128:256], n.qkv_[:, 256:], n.dkv_own_),
            (n.kv_far_[:, :128], n.kv_far_[:, 128:], n.dkv_far_),
        )
        scores = [dot_cols(q, k) * scale for k, _, _ in blocks]
        sums = sum(jnp.sum(jnp.exp(x), axis=1, keepdims=True) for x in scores)
        log_total = jnp.log(sums)
        probs = [jnp.exp(x - log_total) for x in scores]
        dprobs = [dot_cols(da, v) for _, v, _ in blocks]
        inner = sum(jnp.sum(p * d, axis=1, keepdims=True) for p, d in zip(probs, dprobs))
        att = jnp.zeros((128, 256), F32)
        dq = jnp.zeros((128, 128), F32)
        for (k, v, total_ref), p, d in zip(blocks, probs, dprobs):
            ds = (p * (d - inner)).astype(BF16)
            pb = p.astype(BF16)
            att = att + dot(pb, v)
            dq = dq + dot(ds, k)
            total_ref[:, :128] += dot_rows(ds, q) * scale
            total_ref[:, 128:] += dot_rows(pb, da)
        att = att.astype(BF16)
        n.att_[here, :] = att
        n.dqkv_[here, :128] = (dq * scale).astype(BF16)
        send_pair("lp", t, dot(att, n.w_up_[...]))

    loop(4, attend)
    n.dkv_s_[...] = n.dkv_far_[...].astype(BF16)
    swap_back = pltpu.make_async_remote_copy(
        src_ref=n.dkv_s_, dst_ref=n.dkv_r_, send_sem=swap_send.at[1], recv_sem=swap_recv.at[1],
        device_id=peer, device_id_type=MESH,
    )
    swap_back.start()
    low = n.low_r_[...].reshape(512, 768)
    pick = n.select_down_[:, rows_of(b, 128)]
    for half in range(2):
        wide = slice(768 * half, 768 * half + 768)
        n.slices_[:, 128 * half : 128 * half + 128] = dot(n.lifted_[:, wide], pick).astype(BF16)
    swap_back.wait()
    n.dqkv_[:, 128:] = (n.dkv_own_[...] + n.dkv_r_[...].astype(F32)).astype(BF16)

    def back_through_projections(t):
        send_pair("pd", t, dot(n.dqkv_[rows_of(t, 128), :], n.w_down_[...]))

    loop(4, back_through_projections)

    scaled = (n.pooled_[...].astype(F32) * n.factor_[:, 0:1]).astype(BF16)
    n.mnl_c_s_[:, :, :, :512] = dot_rows(scaled, n.dqkv_[...]).astype(BF16).reshape(8, 2, 48, 512)
    n.mnl_c_s_[:, :, :, 512:768] = dot_rows(low, n.att_[...]).astype(BF16).reshape(8, 2, 48, 256)
    n.mnl_c_s_[:, :, :, 768:] = (
        dot_rows(low, n.slices_[:, :256]).astype(BF16).reshape(8, 2, 48, 256)
    )
    links.mnl_c.start()

    def first_hop(name):
        over_x, over_z = getattr(links, name + "A"), getattr(links, name + "B")
        over_x.keep()
        over_x.receive()
        there = 1 - z
        value = over_x.result[there].astype(F32)
        for j in range(1, 4):
            value = value + over_x.result[2 * j + there].astype(F32)
        getattr(n, name + "C_s_")[0] = value.astype(BF16)
        getattr(links, name + "C").start()
        over_z.receive()
        value = getattr(n, name + "B_s_")[pl.ds(4 * z, 4)].astype(F32)
        value = value + over_z.result[...].astype(F32)
        getattr(n, name + "D_s_")[...] = value.astype(BF16)
        getattr(links, name + "D").start()

    def second_hop(name):
        getattr(links, name + "C").receive()
        left = getattr(links, name + "C").result[0].astype(F32)
        for j in range(4):
            left = left + getattr(links, name + "A").result[2 * j + z].astype(F32)
        getattr(links, name + "D").receive()
        return jnp.concatenate([left, total(getattr(links, name + "D").result, 4)], axis=1)

    def core_sum(name):
        getattr(links, name + "_c").receive()
        mine = getattr(n, name + "_c_s_")
        far = getattr(n, name + "_c_r_")
        target = getattr(n, name + "_s_")

        def add(j):
            target[j] = (mine[j, h].astype(F32) + far[0, j].astype(F32)).astype(BF16)

        loop(8, add)
        getattr(links, name).start()

    first_hop("lp")
    core_sum("mnl")

    here = rows_of(b, 64)
    n.conv_[...] = dot(n.emb_[b], n.conv_w_[...])
    center = n.emb_[b, :, 768:1536].astype(F32)
    n.tower_[...] = (center + jax.nn.gelu(n.conv_[...])).astype(BF16)
    lifted = n.lifted_[here, :]
    factor = n.factor_[here, 0:1]
    cube = factor * factor * factor
    first_hop("pd")
    behind = dot_cols(jnp.concatenate([lifted, n.d_mixed_[here, :]], axis=0), n.down_w_[...])
    lowered = dot(lifted, n.up_w_[...])
    slope = gelu_grad(n.conv_[...])
    straight = second_hop("pd")
    mean = jnp.sum(straight * n.pooled_[here, :].astype(F32), axis=-1, keepdims=True) / 1536.0
    d_pooled = 0.5 * (factor * straight - cube * mean * behind[:64] + behind[64:])
    d_tower = n.blk_r_[0].astype(F32) + jnp.concatenate([d_pooled, d_pooled], axis=0)
    d_tower = d_tower.astype(BF16)
    d_conv = (d_tower.astype(F32) * slope).astype(BF16)
    moved = dot(d_conv, n.select_conv_[...]).astype(BF16)
    for j in range(8):
        n.dc_s_[j] = moved[:, 128 * j : 128 * j + 128]
    links.dc.start()
    diagonal = iota((64, 128), 0) == iota((64, 128), 1)
    line = jnp.sum(jnp.where(diagonal, mean, 0.0), axis=0, keepdims=True)
    n.mean_s_[0] = jnp.broadcast_to(line, (8, 128))
    links.mean.start()
    hots = one_hots(b)
    d_stem = jnp.zeros((128, 768), F32)
    for step in range(3):
        d_emb = dot_cols(d_conv, n.conv_w_[768 * step : 768 * step + 768, :])
        if step == 1:
            d_emb = d_emb + d_tower.astype(F32)
        hot = jnp.concatenate([hots[step], hots[3 + step]], axis=0)
        d_stem = d_stem + dot_rows(hot, d_emb.astype(BF16))
    moved = dot(d_stem[:64].astype(BF16), n.select_conv_[...]).astype(BF16)
    for j in range(8):
        n.ds_s_[j] = moved[:, 128 * j : 128 * j + 128]
    links.ds.start()

    lowered = lowered + second_hop("lp")
    features = n.tower_[...].astype(F32) + jnp.concatenate([lowered, lowered], axis=0)
    n.feat_s_[0] = dot_rows(order, features.astype(BF16)).astype(BF16)
    links.feat.start()

    links.mnl.receive()
    summed = total(n.mnl_r_, 8)
    n.mn_s_[0] = summed[:, :768].astype(BF16)
    links.mn.start()
    wide = dot(summed[:, 512:768].astype(BF16), n.o_w_[...])
    sides = [
        dot_cols(summed[:, 768 + 128 * half : 896 + 128 * half].astype(BF16), pick)
        for half in range(2)
    ]
    wide = (wide + jnp.concatenate(sides, axis=1)).astype(BF16)
    groups = iota((64, 48), 0)
    groups = jnp.where(groups % 8 < 6, 6 * (groups // 8) + groups % 8, -1)
    wide = dot(zero_one(iota((64, 48), 1) == groups), wide)
    n.up_s_[:, 0:8, :] = wide[:, :768].reshape(8, 8, 768).astype(BF16)
    n.up_s_[:, 8:16, :] = wide[:, 768:].reshape(8, 8, 768).astype(BF16)
    links.up.start()

    for half in range(2):
        wide = slice(768 * half, 768 * half + 768)
        n.slices_[:, 256 + 128 * half : 384 + 128 * half] = dot(n.d_mixed_[:, wide], pick).astype(BF16)
    links.mean.receive()

    def remainder(j):
        rows = rows_of(j, 64)
        mean = jnp.sum(jnp.where(diagonal, n.mean_r_[j][0:1], 0.0), axis=1, keepdims=True)
        factor = n.factor_[rows, 0:1]
        part = factor * factor * factor * mean * n.slices_[rows, :256].astype(F32)
        n.rest_[rows, :] = (n.slices_[rows, 256:].astype(F32) - part).astype(BF16)

    loop(8, remainder)
    n.down_c_s_[...] = dot_rows(n.rest_[...], n.pooled_[...]).astype(BF16).reshape(8, 2, 16, 768)
    links.down_c.start()

    n.conv_acc_[...] = jnp.zeros((128, 2304), F32)
    links.dc.receive()

    def conv_grads(t):
        pair = pl.ds(2 * t, 2)
        left = n.dc_r_[pair].reshape(256, 128)
        n.conv_acc_[...] += dot_rows(left, n.emb_[pair].reshape(256, 2304))

    loop(4, conv_grads)
    links.ds.receive()
    same = zero_one(iota((512, 128), 0) % 64 == iota((512, 128), 1))
    stem = dot_rows(n.ds_r_[...].reshape(512, 128), same)
    n.conv_c_s_[:, :, 0:8, :] = n.conv_acc_[:, :1280].reshape(8, 2, 8, 1280).astype(BF16)
    rest = jnp.concatenate([n.conv_acc_[:, 1280:], stem, jnp.zeros((128, 128), F32)], axis=1)
    n.conv_c_s_[:, :, 8:16, :] = rest.reshape(8, 2, 8, 1280).astype(BF16)
    links.conv_c.start()
    links.mn.receive()
    links.full.start()
    core_sum("conv")
    core_sum("down")

    lane, channel = iota((128, 1536), 0), iota((128, 1536), 1)
    wanted = jnp.where(lane < 96, 96 * s + lane, -1)
    hit = channel == wanted
    gain_here = jnp.sum(jnp.where(hit, gain, 0.0), axis=1, keepdims=True)[:96]
    n.pick_down_[...] = dot_cols(zero_one(hit), n.down_w_[...]).astype(BF16)
    wanted = 96 * s + 12 * (lane // 16) + 6 * (lane % 16 // 8) + lane % 8
    hit = jnp.logical_and(channel == wanted, lane % 8 < 6)
    gained = (n.in_t_[...].astype(F32) * gain).astype(BF16)
    n.pick_in_[...] = dot_cols(zero_one(hit), gained).astype(BF16)
    links.full.receive()

    def assemble(q):
        near = pl.ds(pl.multiple_of(96 * q + 48 * h, 16), 48)
        far = pl.ds(pl.multiple_of(96 * q + 48 * (1 - h), 16), 48)
        n.summed_[near, :] = n.mn_r_[q]
        n.summed_[far, :] = n.full_r_[0, q]

    loop(8, assemble)
    first = dot_cols(n.pick_in_[...], n.summed_[:, :512])
    n.first_s_[...] = first.astype(BF16).reshape(8, 16, 768)
    links.first.start()
    inner = dot(n.pick_down_[...], n.summed_[:, :512])[:96]
    rows = pl.ds(pl.multiple_of(96 * s, 16), 96)
    part = jnp.sum(inner * n.in_w_[rows, :].astype(F32), axis=1, keepdims=True)
    diagonal = iota((96, 128), 0) == iota((96, 128), 1)
    line = jnp.sum(jnp.where(diagonal, part, 0.0), axis=0, keepdims=True)
    n.gain_s_[0] = jnp.broadcast_to(line, (8, 128))
    links.gain.start()
    inner = inner * gain_here
    n.g_q[...] = inner[:, :128]
    n.g_k[...] = inner[:, 128:256]
    n.g_v[...] = inner[:, 256:448]
    n.g_o[...] = dot(n.up_w_[rows, :], n.summed_[:, 512:])[:, :192]

    links.feat.receive()
    n.features[...] = n.feat_r_[0]
    links.up.receive()
    up = total(n.up_r_, 8)
    n.g_up[:, :768] = up[0:6]
    n.g_up[:, 768:] = up[8:14]
    links.conv.receive()
    conv = total(n.conv_r_, 8)
    n.g_conv[0] = conv[0:6, :768]
    n.g_conv[1] = jnp.concatenate([conv[0:6, 768:], conv[8:14, :256]], axis=1)
    n.g_conv[2] = conv[8:14, 256:1024]
    stem = conv[8:16, 1024:1152].astype(BF16)
    for code in range(4):
        taps = iota((128, 15), 0) == 4 * iota((128, 15), 1) + code
        n.g_stem[:, code, :] = dot(stem, zero_one(taps))[:6]
    links.down.receive()
    links.first.receive()
    down = total(n.down_r_, 8) + total(n.first_r_, 8)
    n.g_down[0:6, :] = down[0:6]
    n.g_down[6:12, :] = down[8:14]
    links.gain.receive()
    gains = total(n.gain_r_, 8)
    high = gains.astype(BF16)
    low = (gains - high.astype(F32)).astype(BF16)
    shift = zero_one(jnp.logical_and(row == column + 12 * b, column < 12))
    n.g_gain[...] = (dot(high, shift) + dot(low, shift))[0:1]
    for link in vars(links).values():
        link.drain()


def finish_body(*refs):
    number = len(OUTPUTS)
    for source, target in zip(refs[:number], refs[number:]):
        target[...] = source[...]


def per_device(
    base_codes,
    stem_weight,
    conv_weight,
    down_weight,
    norm_gain,
    query_weight,
    key_weight,
    value_weight,
    output_weight,
    up_weight,
    cotangent,
):
    vmem, anywhere = pl.BlockSpec(memory_space=pltpu.VMEM), pl.BlockSpec(memory_space=pl.ANY)
    semaphores = [pltpu.SemaphoreType.DMA((7,))] + [pltpu.SemaphoreType.DMA((2,))] * 2
    shapes = {name: x[0] for name, x in SCRATCH.items()}
    for name, pattern in LINKS.items():
        semaphores += [
            pltpu.SemaphoreType.DMA((pattern.count,)),
            pltpu.SemaphoreType.DMA((shapes[name + "_r"][0],)),
        ]
    out_shape = [jax.ShapeDtypeStruct(shape, dtype) for shape, dtype in OUTPUTS.values()]
    results = pl.pallas_call(
        kernel_body,
        out_shape=out_shape,
        in_specs=[vmem] * 4 + [anywhere] * 7,
        out_specs=[vmem] * len(OUTPUTS),
        scratch_shapes=[pltpu.VMEM(shape, dtype) for shape, dtype in SCRATCH.values()] + semaphores,
        compiler_params=pltpu.CompilerParams(
            collective_id=0, has_side_effects=True, vmem_limit_bytes=60 * 1024 * 1024
        ),
        name="step",
    )(
        base_codes,
        cotangent[0],
        norm_gain,
        stem_weight,
        conv_weight.reshape(2304, 768),
        down_weight,
        query_weight,
        key_weight,
        value_weight.T,
        output_weight,
        up_weight,
    )
    features, g_stem, g_conv, g_down, g_gain, g_up, g_q, g_k, g_v, g_o = pl.pallas_call(
        finish_body,
        out_shape=out_shape,
        in_specs=[vmem] * len(OUTPUTS),
        out_specs=[vmem] * len(OUTPUTS),
        name="finish",
    )(*results)
    return (
        features[None],
        g_stem.transpose(2, 1, 0),
        g_conv.transpose(0, 2, 1),
        g_down.T,
        g_gain[0, :12],
        g_up.T,
        g_q,
        g_k,
        g_v,
        g_o,
    )


def solution(mesh):
    placed = (
        P("batch", "seq"),
        P(),
        P(),
        P(),
        P(),
        P(None, "batch"),
        P(None, "batch"),
        P(None, "batch"),
        P("batch", None),
        P(),
        P("batch", "seq", None),
    )
    return jax.shard_map(
        per_device,
        mesh=mesh,
        in_specs=placed,
        out_specs=(
            P("batch", "seq", None),
            P(None, None, ("seq", "batch")),
            P(None, None, ("seq", "batch")),
            P(None, ("seq", "batch")),
            P(("seq", "batch")),
            P(None, ("seq", "batch")),
            P("seq", "batch"),
            P("seq", "batch"),
            P("seq", "batch"),
            P("seq", "batch"),
        ),
        check_vma=False,
    )
```

```python
import functools
import math

import jax
import jax.numpy as jnp
from jax import lax
from jax.experimental import pallas as pl
from jax.experimental.pallas import tpu as pltpu
from jax.sharding import PartitionSpec as P

EPSILON = 1e-06
MESH = pl.DeviceIdType.MESH
F32 = jnp.float32
BF16 = jnp.bfloat16
SEQ = 16
BATCH = 8


class OverBatch:
    count = BATCH

    def dst(self, i, s, b):
        j = lax.rem(b + i, BATCH)
        return j, s, j, b

    def src(self, i, s, b):
        j = lax.rem(b + BATCH - i, BATCH)
        return j, s, j


class Share:
    count = BATCH

    def dst(self, i, s, b):
        return 0, s, lax.rem(b + i, BATCH), b

    def src(self, i, s, b):
        j = lax.rem(b + BATCH - i, BATCH)
        return j, s, j


class OverQuads:
    count = SEQ // 2

    def dst(self, i, s, b):
        j = lax.rem(s // 2 + i, SEQ // 2)
        return j, 2 * j + lax.rem(s, 2), b, s // 2

    def src(self, i, s, b):
        j = lax.rem(s // 2 + SEQ // 2 - i, SEQ // 2)
        return j, 2 * j + lax.rem(s, 2), b


class QuadShare:
    count = SEQ // 2

    def dst(self, i, s, b):
        j = lax.rem(s // 2 + i, SEQ // 2)
        return 0, 2 * j + lax.rem(s, 2), b, s // 2

    def src(self, i, s, b):
        j = lax.rem(s // 2 + SEQ // 2 - i, SEQ // 2)
        return j, 2 * j + lax.rem(s, 2), b


class Core:
    count = 1

    def dst(self, i, s, b):
        other = 1 - lax.rem(s, 2)
        return other, s - lax.rem(s, 2) + other, b, 0

    def src(self, i, s, b):
        return 0, s + 1 - 2 * lax.rem(s, 2), b


class XBlocks:
    count = 8

    def dst(self, i, s, b):
        z, x = b // 4, lax.rem(b, 4)
        to, side = lax.rem(x + i // 2, 4), lax.rem(i, 2)
        return 4 * side + to, s, 4 * z + to, 2 * x + side

    def src(self, i, s, b):
        z, x = b // 4, lax.rem(b, 4)
        at, side = lax.rem(x + 4 - i // 2, 4), lax.rem(i, 2)
        return 2 * at + side, s, 4 * z + at


class ZBlocks:
    count = 4

    def dst(self, i, s, b):
        other = 1 - b // 4
        return 4 * other + i, s, 4 * other + lax.rem(b, 4), i

    def src(self, i, s, b):
        return i, s, 4 * (1 - b // 4) + lax.rem(b, 4)


class ZOne:
    count = 1

    def dst(self, i, s, b):
        return 0, s, 4 * (1 - b // 4) + lax.rem(b, 4), 0

    def src(self, i, s, b):
        return 0, s, 4 * (1 - b // 4) + lax.rem(b, 4)


class XOne:
    count = 4

    def dst(self, i, s, b):
        z, x = b // 4, lax.rem(b, 4)
        to = lax.rem(x + i, 4)
        return to, s, 4 * z + to, x

    def src(self, i, s, b):
        z, x = b // 4, lax.rem(b, 4)
        at = lax.rem(x + 4 - i, 4)
        return at, s, 4 * z + at


class Codes:
    count = 2 * BATCH

    def dst(self, i, s, b):
        return 0, 2 * b + lax.rem(i, 2), lax.rem(b + i // 2, BATCH), s

    def src(self, i, s, b):
        return i, i, s // 2


class ToBlock:
    count = 1

    def dst(self, i, s, b):
        return 0, 2 * b + s // BATCH, lax.rem(s, BATCH), 0

    def src(self, i, s, b):
        return 0, BATCH * lax.rem(s, 2) + b, s // 2


class ToOwner:
    count = 1

    def dst(self, i, s, b):
        return 0, BATCH * lax.rem(s, 2) + b, s // 2, 0

    def src(self, i, s, b):
        return 0, 2 * b + s // BATCH, lax.rem(s, BATCH)


class Link:
    def __init__(self, pattern, source, result, sends, receives, s, b):
        self.pattern, self.source, self.result = pattern, source, result
        self.sends, self.receives, self.s, self.b = sends, receives, s, b

    def copy(self, i):
        piece, target_s, target_b, slot = self.pattern.dst(i, self.s, self.b)
        away = jnp.logical_or(target_s != self.s, target_b != self.b)
        return away, pltpu.make_async_remote_copy(
            src_ref=self.source(piece),
            dst_ref=self.result.at[slot],
            send_sem=self.sends.at[i],
            recv_sem=self.receives.at[slot],
            device_id=(target_s, target_b),
            device_id_type=MESH,
        )

    def keep_one(self, i):
        piece, target_s, target_b, slot = self.pattern.dst(i, self.s, self.b)
        home = jnp.logical_and(target_s == self.s, target_b == self.b)

        @pl.when(home)
        def _():
            self.result[slot] = self.source(piece)[...]

    def each(self, action):
        loop(self.pattern.count, action)

    def start_one(self, i):
        away, copy = self.copy(i)
        pl.when(away)(copy.start)

    def keep(self):
        self.each(self.keep_one)

    def start(self):
        self.each(self.start_one)
        self.keep()

    def receive(self):
        def wait(i):
            slot, other_s, other_b = self.pattern.src(i, self.s, self.b)
            away = jnp.logical_or(other_s != self.s, other_b != self.b)
            copy = pltpu.make_async_remote_copy(
                src_ref=self.result.at[slot],
                dst_ref=self.result.at[slot],
                send_sem=self.sends.at[i],
                recv_sem=self.receives.at[slot],
                device_id=(other_s, other_b),
                device_id_type=MESH,
            )
            pl.when(away)(copy.wait_recv)

        self.each(wait)

    def drain(self):
        def wait(i):
            away, copy = self.copy(i)
            pl.when(away)(copy.wait_send)

        self.each(wait)


def dot(left, right):
    return jnp.dot(left, right, preferred_element_type=F32)


def dot_rows(left, right):
    return lax.dot_general(left, right, (((0,), (0,)), ((), ())), preferred_element_type=F32)


def dot_cols(left, right):
    return lax.dot_general(left, right, (((1,), (1,)), ((), ())), preferred_element_type=F32)


def iota(shape, dim):
    return lax.broadcasted_iota(jnp.int32, shape, dim)


def zero_one(mask):
    return jnp.where(mask, 1.0, 0.0).astype(BF16)


def gelu_grad(x):
    inner = math.sqrt(2.0 / math.pi) * (x + 0.044715 * x * x * x)
    t = jnp.tanh(inner)
    slope = math.sqrt(2.0 / math.pi) * (1.0 + 3 * 0.044715 * x * x)
    return 0.5 * (1.0 + t) + 0.5 * x * (1.0 - t * t) * slope


def total(ref, count):
    value = ref[0].astype(F32)
    for j in range(1, count):
        value = value + ref[j].astype(F32)
    return value


def loop(count, step):
    def body(i, carry):
        step(i)
        return carry

    lax.fori_loop(0, count, body, 0)


def rows_of(i, size):
    return pl.ds(pl.multiple_of(i * size, size), size)


INPUTS = dict(codes=0, cot=0, gain=0, stem=0, conv_h=0, down_h=0, q_h=0, k_h=0, v_h=0, o_h=0, up_h=0)
OUTPUTS = dict(
    features=((128, 768), BF16),
    g_stem=((6, 4, 15), F32),
    g_conv=((3, 6, 768), F32),
    g_down=((12, 768), F32),
    g_gain=((1, 128), F32),
    g_up=((6, 1536), F32),
    g_q=((96, 128), F32),
    g_k=((96, 128), F32),
    g_v=((96, 192), F32),
    g_o=((96, 192), F32),
)
SCRATCH = dict(
    conv_w=((2304, 768), BF16),
    down_w=((768, 1536), BF16),
    in_w=((1536, 512), BF16),
    in_t=((512, 1536), BF16),
    o_w=((256, 1536), BF16),
    up_w=((1536, 768), BF16),
    stem_f=((64, 768), F32),
    stem_w=((128, 768), BF16),
    select_conv=((768, 1024), BF16),
    select_down=((768, 1024), BF16),
    codes_s=((1, 8, 128), F32),
    codes_r=((16, 8, 128), F32),
    blk_s=((1, 128, 768), BF16),
    blk_r=((1, 128, 768), BF16),
    own_s=((1, 64, 768), BF16),
    own_r=((1, 64, 768), BF16),
    low_r=((8, 64, 768), BF16),
    code=((2, 640, 128), F32),
    picked=((2, 528, 128), F32),
    emb=((8, 128, 2304), BF16),
    conv=((128, 768), F32),
    tower=((128, 768), BF16),
    pooled=((512, 768), BF16),
    lifted=((512, 1536), BF16),
    factor=((512, 128), F32),
    normed=((512, 1536), BF16),
    qkv=((512, 512), BF16),
    kv_far=((512, 384), BF16),
    d_att=((512, 256), BF16),
    att=((512, 256), BF16),
    dqkv=((512, 512), BF16),
    dkv_own=((512, 384), F32),
    dkv_far=((512, 384), F32),
    dkv_s=((512, 384), BF16),
    dkv_r=((512, 384), BF16),
    conv_acc=((128, 2304), F32),
    w_up=((256, 768), BF16),
    w_down=((512, 768), BF16),
    pick_in=((128, 512), BF16),
    pick_down=((128, 768), BF16),
    lpA_s=((8, 64, 384), BF16),
    lpA_r=((8, 64, 384), BF16),
    lpB_s=((8, 64, 384), BF16),
    lpB_r=((4, 64, 384), BF16),
    lpC_s=((1, 64, 384), BF16),
    lpC_r=((1, 64, 384), BF16),
    lpD_s=((4, 64, 384), BF16),
    lpD_r=((4, 64, 384), BF16),
    pdA_s=((8, 64, 384), BF16),
    pdA_r=((8, 64, 384), BF16),
    pdB_s=((8, 64, 384), BF16),
    pdB_r=((4, 64, 384), BF16),
    pdC_s=((1, 64, 384), BF16),
    pdC_r=((1, 64, 384), BF16),
    pdD_s=((4, 64, 384), BF16),
    pdD_r=((4, 64, 384), BF16),
    feat_s=((1, 128, 768), BF16),
    feat_r=((1, 128, 768), BF16),
    mean_s=((1, 8, 128), F32),
    mean_r=((8, 8, 128), F32),
    gain_s=((1, 8, 128), F32),
    gain_r=((8, 8, 128), F32),
    dc_s=((8, 128, 128), BF16),
    dc_r=((8, 128, 128), BF16),
    ds_s=((8, 64, 128), BF16),
    ds_r=((8, 64, 128), BF16),
    up_s=((8, 16, 768), BF16),
    up_r=((8, 16, 768), BF16),
    first_s=((8, 16, 768), BF16),
    first_r=((8, 16, 768), BF16),
    mnl_c_s=((8, 2, 48, 1024), BF16),
    mnl_c_r=((1, 8, 48, 1024), BF16),
    mnl_s=((8, 48, 1024), BF16),
    mnl_r=((8, 48, 1024), BF16),
    mn_s=((1, 48, 768), BF16),
    mn_r=((8, 48, 768), BF16),
    full_r=((1, 8, 48, 768), BF16),
    summed=((768, 768), BF16),
    slices=((512, 512), BF16),
    rest=((512, 256), BF16),
    down_c_s=((8, 2, 16, 768), BF16),
    down_c_r=((1, 8, 16, 768), BF16),
    down_s=((8, 16, 768), BF16),
    down_r=((8, 16, 768), BF16),
    conv_c_s=((8, 2, 16, 1280), BF16),
    conv_c_r=((1, 8, 16, 1280), BF16),
    conv_s=((8, 16, 1280), BF16),
    conv_r=((8, 16, 1280), BF16),
)
LINKS = dict(
    codes=Codes(),
    own=ToBlock(),
    blk=ToBlock(),
    low=Share(),
    lpA=XBlocks(),
    lpB=ZBlocks(),
    lpC=ZOne(),
    lpD=XOne(),
    pdA=XBlocks(),
    pdB=ZBlocks(),
    pdC=ZOne(),
    pdD=XOne(),
    feat=ToOwner(),
    mean=Share(),
    gain=Share(),
    dc=OverBatch(),
    ds=OverBatch(),
    up=OverBatch(),
    first=OverBatch(),
    mnl_c=Core(),
    mnl=OverQuads(),
    mn=QuadShare(),
    full=Core(),
    down_c=Core(),
    down=OverQuads(),
    conv_c=Core(),
    conv=OverQuads(),
)


FORWARDED = dict(low="own_r", full="mn_r")


class Namespace:
    pass


def kernel_body(*refs):
    names = list(INPUTS) + list(OUTPUTS) + [x + "_" for x in SCRATCH]
    n = Namespace()
    for name, ref in zip(names, refs):
        setattr(n, name, ref)
    semaphores = refs[len(names) :]
    weight_sems, swap_send, swap_recv = semaphores[:3]
    s, b = lax.axis_index("seq"), lax.axis_index("batch")
    h = lax.rem(s, 2)
    z = b // 4
    peer = (s + 1 - 2 * h, b)
    links = Namespace()
    for k, (name, pattern) in enumerate(LINKS.items()):
        sent = getattr(n, FORWARDED.get(name, name + "_s") + "_")
        if name == "full":
            source = lambda piece, sent=sent: sent
        elif name.endswith("_c"):
            source = lambda piece, sent=sent: sent.at[:, piece]
        else:
            source = lambda piece, sent=sent: sent.at[piece]
        result = getattr(n, name + "_r_")
        link = Link(pattern, source, result, semaphores[3 + 2 * k], semaphores[4 + 2 * k], s, b)
        setattr(links, name, link)

    barrier = pltpu.get_barrier_semaphore()
    for link in (links.codes, links.low, links.mnl, links.mnl_c, links.feat):
        pattern = link.pattern

        def greet(i, pattern=pattern):
            _, other_s, other_b = pattern.src(i, s, b)

            @pl.when(jnp.logical_or(other_s != s, other_b != b))
            def _():
                pl.semaphore_signal(
                    barrier, inc=1, device_id=(other_s, other_b), device_id_type=MESH
                )

        loop(pattern.count, greet)
    own_window = (b == s // 2).astype(jnp.int32)
    own_block = own_window * (s == BATCH * h + b).astype(jnp.int32)
    expected = 16 + 7 + 7 + 1 + 1 - own_window - own_block

    weights = [
        pltpu.make_async_copy(source, target, weight_sems.at[k])
        for k, (source, target) in enumerate(
            [
                (n.q_h, n.in_w_.at[:, pl.ds(0, 128)]),
                (n.k_h, n.in_w_.at[:, pl.ds(128, 128)]),
                (n.v_h, n.in_t_.at[pl.ds(256, 192)]),
                (n.o_h, n.o_w_.at[pl.ds(0, 192)]),
                (n.conv_h, n.conv_w_),
                (n.down_h, n.down_w_),
                (n.up_h, n.up_w_),
            ]
        )
    ]
    for copy in weights:
        copy.start()

    row, column = iota((128, 128), 0), iota((128, 128), 1)
    order = zero_one(column == jnp.where(row < 64, 2 * row, 2 * row - 127))
    codes = jnp.broadcast_to((n.codes[...] + 1).astype(F32), (8, 128)).astype(BF16)
    n.codes_s_[0] = dot_cols(codes, order)
    cot = dot(order, n.cot[...])
    n.own_s_[0] = (cot[:64] + cot[64:]).astype(BF16)
    n.blk_s_[0] = cot.astype(BF16)

    pl.semaphore_wait(barrier, expected)
    links.codes.start()
    links.own.start()

    def fill(c):
        within = iota((1, 128), 1)
        i, m = lax.rem(within, 8), within // 8
        good = i < 6
        rows = iota((768, 128), 0)
        place = rows_of(c, 128)
        n.select_conv_[:, place] = zero_one(rows == jnp.where(good, 6 * (8 * m + c) + i, -1))
        wanted = 12 * (8 * (m // 2) + c) + 6 * lax.rem(m, 2) + i
        n.select_down_[:, place] = zero_one(rows == jnp.where(good, wanted, -1))

    loop(8, fill)
    for t in range(15):
        n.stem_f_[4 * t : 4 * t + 4, :] = n.stem[t].astype(F32)
    n.stem_f_[60:, :] = jnp.zeros((4, 768), F32)
    n.stem_w_[:64, :] = n.stem_f_[...].astype(BF16)
    n.stem_w_[64:, :] = jnp.zeros((64, 768), BF16)
    for copy in weights[:4]:
        copy.wait()
    n.o_w_[192:, :] = jnp.zeros((64, 1536), BF16)
    n.in_t_[448:, :] = jnp.zeros((64, 1536), BF16)
    eye, eye2 = zero_one(row == column), zero_one(iota((256, 256), 0) == iota((256, 256), 1))
    n.in_t_[:128, :] = dot_cols(eye, n.in_w_[:, :128]).astype(BF16)
    n.in_t_[128:256, :] = dot_cols(eye, n.in_w_[:, 128:256]).astype(BF16)
    n.in_w_[:, 256:] = dot_rows(n.in_t_[256:, :], eye2).astype(BF16)

    links.codes.receive()
    ones = jnp.ones((128, 128), BF16)
    for i in range(10):
        place = BATCH * h + (i - 1)
        inside = jnp.logical_and(place >= 0, place < 16)
        line = n.codes_r_[jnp.clip(place, 0, 15)][0:1]
        line = jnp.where(inside, line, 0.0)
        spread = dot(jnp.where(row == column, line, 0.0).astype(BF16), ones)
        n.code_[0, 64 * i : 64 * i + 64] = spread[:64]
        n.code_[1, 64 * i : 64 * i + 64] = spread[64:]
    lane_tap = iota((1, 128), 1) // 4
    lane_code = (iota((1, 128), 1) % 4 + 1).astype(F32)
    for parity in range(2):
        picked = jnp.zeros((528, 128), F32)
        for tap in range(15):
            offset = parity + tap - 7
            stream, shift = offset % 2, (offset - offset % 2) // 2
            begin = 56 + shift
            picked = jnp.where(lane_tap == tap, n.code_[stream, begin : begin + 528, :], picked)
        where = iota((528, 128), 0) - 8 + 512 * h
        inside = jnp.logical_and(where >= 0, where < 1024)
        n.picked_[parity] = jnp.where(inside, picked, 0.0)

    links.own.receive()
    links.low.start()
    links.blk.start()

    def one_hots(j):
        found = []
        for parity in range(2):
            near = n.picked_[parity, pl.ds(pl.multiple_of(64 * j, 64), 80), :]
            for step in (-4, 0, 4):
                found.append(zero_one(near[8 + step : 72 + step] == lane_code))
        return found

    def embed(j):
        value = dot(jnp.concatenate(one_hots(j), axis=0), n.stem_w_[...]).astype(BF16)
        for parity in range(2):
            for step in range(3):
                begin = 64 * (3 * parity + step)
                n.emb_[j, 64 * parity : 64 * parity + 64, 768 * step : 768 * step + 768] = value[
                    begin : begin + 64
                ]

    loop(8, embed)
    for copy in weights[4:]:
        copy.wait()
    gain = n.gain[...].reshape(1, 1536)

    def forward(t):
        pair = pl.ds(2 * t, 2)
        here = rows_of(t, 128)
        conv = dot(n.emb_[pair].reshape(256, 2304), n.conv_w_[...])
        center = n.emb_[pair, :, 768:1536].reshape(256, 768).astype(F32)
        tower = (center + jax.nn.gelu(conv)).astype(BF16)
        halves = tower.astype(F32).reshape(2, 2, 64, 768)
        pooled = (0.5 * (halves[:, 0] + halves[:, 1])).astype(BF16).reshape(128, 768)
        n.pooled_[here, :] = pooled
        lifted = dot(pooled, n.down_w_[...]).astype(BF16)
        n.lifted_[here, :] = lifted
        lifted = lifted.astype(F32)
        factor = lax.rsqrt(jnp.mean(lifted * lifted, axis=-1, keepdims=True) + EPSILON)
        n.factor_[here, :] = jnp.broadcast_to(factor, (128, 128))
        normed = (lifted * factor * gain).astype(BF16)
        n.normed_[here, :] = normed
        n.qkv_[here, :] = dot(normed, n.in_w_[...]).astype(BF16)

    loop(4, forward)
    swap = pltpu.make_async_remote_copy(
        src_ref=n.qkv_.at[:, pl.ds(128, 384)], dst_ref=n.kv_far_,
        send_sem=swap_send.at[0], recv_sem=swap_recv.at[0], device_id=peer, device_id_type=MESH,
    )
    swap.start()
    n.w_up_[...] = dot(n.o_w_[...], n.up_w_[...]).astype(BF16)
    links.low.receive()

    def low():
        return n.low_r_[...].reshape(512, 768)

    n.d_att_[...] = dot_cols(low(), n.w_up_[...]).astype(BF16)
    n.dkv_own_[...] = jnp.zeros((512, 384), F32)
    n.dkv_far_[...] = jnp.zeros((512, 384), F32)
    swap.wait()

    scale = 1.0 / math.sqrt(128)

    def send_pair(name, t, value):
        half = value.astype(BF16)
        getattr(n, name + "A_s_")[pl.ds(2 * t, 2)] = half[:, :384].reshape(2, 64, 384)
        getattr(n, name + "B_s_")[pl.ds(2 * t, 2)] = half[:, 384:].reshape(2, 64, 384)
        for j in (2 * t, 2 * t + 1):
            to, side = lax.rem(j, 4), j // 4
            getattr(links, name + "A").start_one(2 * lax.rem(to - lax.rem(b, 4) + 4, 4) + side)

            @pl.when(side != z)
            def _():
                getattr(links, name + "B").start_one(to)

    def attend(t):
        here = rows_of(t, 128)
        q, da = n.qkv_[here, :128], n.d_att_[here, :]
        blocks = (
            (n.qkv_[:, 128:256], n.qkv_[:, 256:], n.dkv_own_),
            (n.kv_far_[:, :128], n.kv_far_[:, 128:], n.dkv_far_),
        )
        scores = [dot_cols(q, k) * scale for k, _, _ in blocks]
        sums = sum(jnp.sum(jnp.exp(x), axis=1, keepdims=True) for x in scores)
        log_total = jnp.log(sums)
        probs = [jnp.exp(x - log_total) for x in scores]
        dprobs = [dot_cols(da, v) for _, v, _ in blocks]
        inner = sum(jnp.sum(p * d, axis=1, keepdims=True) for p, d in zip(probs, dprobs))
        att = jnp.zeros((128, 256), F32)
        dq = jnp.zeros((128, 128), F32)
        for (k, v, total_ref), p, d in zip(blocks, probs, dprobs):
            ds = (p * (d - inner)).astype(BF16)
            pb = p.astype(BF16)
            att = att + dot(pb, v)
            dq = dq + dot(ds, k)
            total_ref[:, :128] += dot_rows(ds, q) * scale
            total_ref[:, 128:] += dot_rows(pb, da)
        att = att.astype(BF16)
        n.att_[here, :] = att
        n.dqkv_[here, :128] = (dq * scale).astype(BF16)
        send_pair("lp", t, dot(att, n.w_up_[...]))

    loop(4, attend)
    n.dkv_s_[...] = n.dkv_far_[...].astype(BF16)
    swap_back = pltpu.make_async_remote_copy(
        src_ref=n.dkv_s_, dst_ref=n.dkv_r_, send_sem=swap_send.at[1], recv_sem=swap_recv.at[1],
        device_id=peer, device_id_type=MESH,
    )
    swap_back.start()
    gained = (n.in_t_[...].astype(F32) * gain).astype(BF16)
    n.w_down_[...] = dot_cols(gained, n.down_w_[...]).astype(BF16)
    swap_back.wait()
    n.dqkv_[:, 128:] = (n.dkv_own_[...] + n.dkv_r_[...].astype(F32)).astype(BF16)

    def back_through_projections(t):
        send_pair("pd", t, dot(n.dqkv_[rows_of(t, 128), :], n.w_down_[...]))

    loop(4, back_through_projections)

    pick = n.select_down_[:, rows_of(b, 128)]
    for half in range(2):
        wide = slice(768 * half, 768 * half + 768)
        n.slices_[:, 128 * half : 128 * half + 128] = dot(n.lifted_[:, wide], pick).astype(BF16)

    scaled = (n.pooled_[...].astype(F32) * n.factor_[:, 0:1]).astype(BF16)
    n.mnl_c_s_[:, :, :, :512] = dot_rows(scaled, n.dqkv_[...]).astype(BF16).reshape(8, 2, 48, 512)
    n.mnl_c_s_[:, :, :, 512:768] = dot_rows(low(), n.att_[...]).astype(BF16).reshape(8, 2, 48, 256)
    n.mnl_c_s_[:, :, :, 768:] = (
        dot_rows(low(), n.slices_[:, :256]).astype(BF16).reshape(8, 2, 48, 256)
    )
    links.mnl_c.start()

    def first_hop(name):
        over_x, over_z = getattr(links, name + "A"), getattr(links, name + "B")
        over_x.keep()
        over_x.receive()
        there = 1 - z
        value = over_x.result[there].astype(F32)
        for j in range(1, 4):
            value = value + over_x.result[2 * j + there].astype(F32)
        getattr(n, name + "C_s_")[0] = value.astype(BF16)
        getattr(links, name + "C").start()
        over_z.receive()
        value = getattr(n, name + "B_s_")[pl.ds(4 * z, 4)].astype(F32)
        value = value + over_z.result[...].astype(F32)
        getattr(n, name + "D_s_")[...] = value.astype(BF16)
        getattr(links, name + "D").start()

    def second_hop(name):
        getattr(links, name + "C").receive()
        left = getattr(links, name + "C").result[0].astype(F32)
        for j in range(4):
            left = left + getattr(links, name + "A").result[2 * j + z].astype(F32)
        getattr(links, name + "D").receive()
        return jnp.concatenate([left, total(getattr(links, name + "D").result, 4)], axis=1)

    def core_sum(name):
        getattr(links, name + "_c").receive()
        mine = getattr(n, name + "_c_s_")
        far = getattr(n, name + "_c_r_")
        target = getattr(n, name + "_s_")

        def add(j):
            target[j] = (mine[j, h].astype(F32) + far[0, j].astype(F32)).astype(BF16)

        loop(8, add)
        getattr(links, name).start()

    first_hop("lp")
    core_sum("mnl")

    here = rows_of(b, 64)
    n.conv_[...] = dot(n.emb_[b], n.conv_w_[...])
    center = n.emb_[b, :, 768:1536].astype(F32)
    n.tower_[...] = (center + jax.nn.gelu(n.conv_[...])).astype(BF16)
    lifted = n.lifted_[here, :]
    factor = n.factor_[here, 0:1]
    cube = factor * factor * factor
    d_updated = dot_cols(n.own_r_[0], n.up_w_[...]).astype(BF16)
    behind = dot_cols(jnp.concatenate([lifted, d_updated], axis=0), n.down_w_[...])
    lowered = dot(lifted, n.up_w_[...])
    slope = gelu_grad(n.conv_[...])
    first_hop("pd")
    lowered = lowered + second_hop("lp")
    features = n.tower_[...].astype(F32) + jnp.concatenate([lowered, lowered], axis=0)
    n.feat_s_[0] = dot_rows(order, features.astype(BF16)).astype(BF16)
    links.feat.start()

    lane, channel = iota((128, 1536), 0), iota((128, 1536), 1)
    wanted = jnp.where(lane < 96, 96 * s + lane, -1)
    hit = channel == wanted
    gain_here = jnp.sum(jnp.where(hit, gain, 0.0), axis=1, keepdims=True)[:96]
    n.pick_down_[...] = dot_cols(zero_one(hit), n.down_w_[...]).astype(BF16)
    wanted = 96 * s + 12 * (lane // 16) + 6 * (lane % 16 // 8) + lane % 8
    hit = jnp.logical_and(channel == wanted, lane % 8 < 6)
    gained = (n.in_t_[...].astype(F32) * gain).astype(BF16)
    n.pick_in_[...] = dot_cols(zero_one(hit), gained).astype(BF16)
    straight = second_hop("pd")
    mean = jnp.sum(straight * n.pooled_[here, :].astype(F32), axis=-1, keepdims=True) / 1536.0
    d_pooled = 0.5 * (factor * straight - cube * mean * behind[:64] + behind[64:])
    links.blk.receive()
    d_tower = n.blk_r_[0].astype(F32) + jnp.concatenate([d_pooled, d_pooled], axis=0)
    d_tower = d_tower.astype(BF16)
    d_conv = (d_tower.astype(F32) * slope).astype(BF16)
    moved = dot(d_conv, n.select_conv_[...]).astype(BF16)
    for j in range(8):
        n.dc_s_[j] = moved[:, 128 * j : 128 * j + 128]
    links.dc.start()
    diagonal = iota((64, 128), 0) == iota((64, 128), 1)
    line = jnp.sum(jnp.where(diagonal, mean, 0.0), axis=0, keepdims=True)
    n.mean_s_[0] = jnp.broadcast_to(line, (8, 128))
    links.mean.start()

    links.mnl.receive()
    summed = total(n.mnl_r_, 8)
    n.mn_s_[0] = summed[:, :768].astype(BF16)
    links.mn.start()

    hots = one_hots(b)
    d_stem = jnp.zeros((128, 768), F32)
    for step in range(3):
        d_emb = dot_cols(d_conv, n.conv_w_[768 * step : 768 * step + 768, :])
        if step == 1:
            d_emb = d_emb + d_tower.astype(F32)
        hot = jnp.concatenate([hots[step], hots[3 + step]], axis=0)
        d_stem = d_stem + dot_rows(hot, d_emb.astype(BF16))
    moved = dot(d_stem[:64].astype(BF16), n.select_conv_[...]).astype(BF16)
    for j in range(8):
        n.ds_s_[j] = moved[:, 128 * j : 128 * j + 128]
    links.ds.start()

    wide = dot(summed[:, 512:768].astype(BF16), n.o_w_[...])
    sides = [
        dot_cols(summed[:, 768 + 128 * half : 896 + 128 * half].astype(BF16), pick)
        for half in range(2)
    ]
    wide = (wide + jnp.concatenate(sides, axis=1)).astype(BF16)
    groups = iota((64, 48), 0)
    groups = jnp.where(groups % 8 < 6, 6 * (groups // 8) + groups % 8, -1)
    wide = dot(zero_one(iota((64, 48), 1) == groups), wide)
    n.up_s_[:, 0:8, :] = wide[:, :768].reshape(8, 8, 768).astype(BF16)
    n.up_s_[:, 8:16, :] = wide[:, 768:].reshape(8, 8, 768).astype(BF16)
    links.up.start()

    for half in range(2):
        wide = slice(768 * half, 768 * half + 768)
        part = dot_rows(pick, n.up_w_[wide, :]).astype(BF16)
        n.slices_[:, 256 + 128 * half : 384 + 128 * half] = dot_cols(low(), part).astype(BF16)
    n.conv_acc_[...] = jnp.zeros((128, 2304), F32)
    links.dc.receive()

    def conv_grads(t):
        pair = pl.ds(2 * t, 2)
        left = n.dc_r_[pair].reshape(256, 128)
        n.conv_acc_[...] += dot_rows(left, n.emb_[pair].reshape(256, 2304))

    loop(4, conv_grads)
    links.ds.receive()
    same = zero_one(iota((512, 128), 0) % 64 == iota((512, 128), 1))
    stem = dot_rows(n.ds_r_[...].reshape(512, 128), same)
    n.conv_c_s_[:, :, 0:8, :] = n.conv_acc_[:, :1280].reshape(8, 2, 8, 1280).astype(BF16)
    rest = jnp.concatenate([n.conv_acc_[:, 1280:], stem, jnp.zeros((128, 128), F32)], axis=1)
    n.conv_c_s_[:, :, 8:16, :] = rest.reshape(8, 2, 8, 1280).astype(BF16)
    links.conv_c.start()

    links.mean.receive()

    def remainder(j):
        rows = rows_of(j, 64)
        mean = jnp.sum(jnp.where(diagonal, n.mean_r_[j][0:1], 0.0), axis=1, keepdims=True)
        factor = n.factor_[rows, 0:1]
        part = factor * factor * factor * mean * n.slices_[rows, :256].astype(F32)
        n.rest_[rows, :] = (n.slices_[rows, 256:].astype(F32) - part).astype(BF16)

    loop(8, remainder)
    n.down_c_s_[...] = dot_rows(n.rest_[...], n.pooled_[...]).astype(BF16).reshape(8, 2, 16, 768)
    links.down_c.start()

    core_sum("conv")
    links.mn.receive()
    links.full.start()
    core_sum("down")

    links.full.receive()

    def assemble(q):
        near = pl.ds(pl.multiple_of(96 * q + 48 * h, 16), 48)
        far = pl.ds(pl.multiple_of(96 * q + 48 * (1 - h), 16), 48)
        n.summed_[near, :] = n.mn_r_[q]
        n.summed_[far, :] = n.full_r_[0, q]

    loop(8, assemble)
    first = dot_cols(n.pick_in_[...], n.summed_[:, :512])
    n.first_s_[...] = first.astype(BF16).reshape(8, 16, 768)
    links.first.start()
    inner = dot(n.pick_down_[...], n.summed_[:, :512])[:96]
    rows = pl.ds(pl.multiple_of(96 * s, 16), 96)
    part = jnp.sum(inner * n.in_w_[rows, :].astype(F32), axis=1, keepdims=True)
    diagonal = iota((96, 128), 0) == iota((96, 128), 1)
    line = jnp.sum(jnp.where(diagonal, part, 0.0), axis=0, keepdims=True)
    n.gain_s_[0] = jnp.broadcast_to(line, (8, 128))
    links.gain.start()
    inner = inner * gain_here
    n.g_q[...] = inner[:, :128]
    n.g_k[...] = inner[:, 128:256]
    n.g_v[...] = inner[:, 256:448]
    n.g_o[...] = dot(n.up_w_[rows, :], n.summed_[:, 512:])[:, :192]

    links.feat.receive()
    n.features[...] = n.feat_r_[0]
    links.up.receive()
    up = total(n.up_r_, 8)
    n.g_up[:, :768] = up[0:6]
    n.g_up[:, 768:] = up[8:14]
    links.conv.receive()
    conv = total(n.conv_r_, 8)
    n.g_conv[0] = conv[0:6, :768]
    n.g_conv[1] = jnp.concatenate([conv[0:6, 768:], conv[8:14, :256]], axis=1)
    n.g_conv[2] = conv[8:14, 256:1024]
    stem = conv[8:16, 1024:1152].astype(BF16)
    for code in range(4):
        taps = iota((128, 15), 0) == 4 * iota((128, 15), 1) + code
        n.g_stem[:, code, :] = dot(stem, zero_one(taps))[:6]
    links.down.receive()
    links.first.receive()
    down = total(n.down_r_, 8) + total(n.first_r_, 8)
    n.g_down[0:6, :] = down[0:6]
    n.g_down[6:12, :] = down[8:14]
    links.gain.receive()
    gains = total(n.gain_r_, 8)
    high = gains.astype(BF16)
    fine = (gains - high.astype(F32)).astype(BF16)
    shift = zero_one(jnp.logical_and(row == column + 12 * b, column < 12))
    n.g_gain[...] = (dot(high, shift) + dot(fine, shift))[0:1]
    for link in vars(links).values():
        link.drain()


def finish_body(*refs):
    number = len(OUTPUTS)
    for source, target in zip(refs[:number], refs[number:]):
        target[...] = source[...]


def per_device(
    base_codes,
    stem_weight,
    conv_weight,
    down_weight,
    norm_gain,
    query_weight,
    key_weight,
    value_weight,
    output_weight,
    up_weight,
    cotangent,
):
    vmem, anywhere = pl.BlockSpec(memory_space=pltpu.VMEM), pl.BlockSpec(memory_space=pl.ANY)
    semaphores = [pltpu.SemaphoreType.DMA((7,))] + [pltpu.SemaphoreType.DMA((2,))] * 2
    shapes = {name: x[0] for name, x in SCRATCH.items()}
    for name, pattern in LINKS.items():
        semaphores += [
            pltpu.SemaphoreType.DMA((pattern.count,)),
            pltpu.SemaphoreType.DMA((shapes[name + "_r"][0],)),
        ]
    out_shape = [jax.ShapeDtypeStruct(shape, dtype) for shape, dtype in OUTPUTS.values()]
    results = pl.pallas_call(
        kernel_body,
        out_shape=out_shape,
        in_specs=[vmem] * 4 + [anywhere] * 7,
        out_specs=[vmem] * len(OUTPUTS),
        scratch_shapes=[pltpu.VMEM(shape, dtype) for shape, dtype in SCRATCH.values()] + semaphores,
        compiler_params=pltpu.CompilerParams(
            collective_id=0, has_side_effects=True, vmem_limit_bytes=60 * 1024 * 1024
        ),
        name="step",
    )(
        base_codes,
        cotangent[0],
        norm_gain,
        stem_weight,
        conv_weight.reshape(2304, 768),
        down_weight,
        query_weight,
        key_weight,
        value_weight.T,
        output_weight,
        up_weight,
    )
    features, g_stem, g_conv, g_down, g_gain, g_up, g_q, g_k, g_v, g_o = pl.pallas_call(
        finish_body,
        out_shape=out_shape,
        in_specs=[vmem] * len(OUTPUTS),
        out_specs=[vmem] * len(OUTPUTS),
        name="finish",
    )(*results)
    return (
        features[None],
        g_stem.transpose(2, 1, 0),
        g_conv.transpose(0, 2, 1),
        g_down.T,
        g_gain[0, :12],
        g_up.T,
        g_q,
        g_k,
        g_v,
        g_o,
    )


def solution(mesh):
    placed = (
        P("batch", "seq"),
        P(),
        P(),
        P(),
        P(),
        P(None, "batch"),
        P(None, "batch"),
        P(None, "batch"),
        P("batch", None),
        P(),
        P("batch", "seq", None),
    )
    return jax.shard_map(
        per_device,
        mesh=mesh,
        in_specs=placed,
        out_specs=(
            P("batch", "seq", None),
            P(None, None, ("seq", "batch")),
            P(None, None, ("seq", "batch")),
            P(None, ("seq", "batch")),
            P(("seq", "batch")),
            P(None, ("seq", "batch")),
            P("seq", "batch"),
            P("seq", "batch"),
            P("seq", "batch"),
            P("seq", "batch"),
        ),
        check_vma=False,
    )
```

```python
import functools
import math

import jax
import jax.numpy as jnp
from jax import lax
from jax.experimental import pallas as pl
from jax.experimental.pallas import tpu as pltpu
from jax.sharding import PartitionSpec as P

EPSILON = 1e-06
MESH = pl.DeviceIdType.MESH
F32 = jnp.float32
BF16 = jnp.bfloat16
SEQ = 16
BATCH = 8


class OverBatch:
    count = BATCH

    def dst(self, i, s, b):
        j = lax.rem(b + i, BATCH)
        return j, s, j, b

    def src(self, i, s, b):
        j = lax.rem(b + BATCH - i, BATCH)
        return j, s, j


class Share:
    count = BATCH

    def dst(self, i, s, b):
        return 0, s, lax.rem(b + i, BATCH), b

    def src(self, i, s, b):
        j = lax.rem(b + BATCH - i, BATCH)
        return j, s, j


class OverQuads:
    count = SEQ // 2

    def dst(self, i, s, b):
        j = lax.rem(s // 2 + i, SEQ // 2)
        return j, 2 * j + lax.rem(s, 2), b, s // 2

    def src(self, i, s, b):
        j = lax.rem(s // 2 + SEQ // 2 - i, SEQ // 2)
        return j, 2 * j + lax.rem(s, 2), b


class QuadShare:
    count = SEQ // 2

    def dst(self, i, s, b):
        j = lax.rem(s // 2 + i, SEQ // 2)
        return 0, 2 * j + lax.rem(s, 2), b, s // 2

    def src(self, i, s, b):
        j = lax.rem(s // 2 + SEQ // 2 - i, SEQ // 2)
        return j, 2 * j + lax.rem(s, 2), b


class Core:
    count = 1

    def dst(self, i, s, b):
        other = 1 - lax.rem(s, 2)
        return other, s - lax.rem(s, 2) + other, b, 0

    def src(self, i, s, b):
        return 0, s + 1 - 2 * lax.rem(s, 2), b


class XBlocks:
    count = 8

    def dst(self, i, s, b):
        z, x = b // 4, lax.rem(b, 4)
        to, side = lax.rem(x + i // 2, 4), lax.rem(i, 2)
        return 4 * side + to, s, 4 * z + to, 2 * x + side

    def src(self, i, s, b):
        z, x = b // 4, lax.rem(b, 4)
        at, side = lax.rem(x + 4 - i // 2, 4), lax.rem(i, 2)
        return 2 * at + side, s, 4 * z + at


class ZBlocks:
    count = 4

    def dst(self, i, s, b):
        other = 1 - b // 4
        return 4 * other + i, s, 4 * other + lax.rem(b, 4), i

    def src(self, i, s, b):
        return i, s, 4 * (1 - b // 4) + lax.rem(b, 4)


class ZOne:
    count = 1

    def dst(self, i, s, b):
        return 0, s, 4 * (1 - b // 4) + lax.rem(b, 4), 0

    def src(self, i, s, b):
        return 0, s, 4 * (1 - b // 4) + lax.rem(b, 4)


class XOne:
    count = 4

    def dst(self, i, s, b):
        z, x = b // 4, lax.rem(b, 4)
        to = lax.rem(x + i, 4)
        return to, s, 4 * z + to, x

    def src(self, i, s, b):
        z, x = b // 4, lax.rem(b, 4)
        at = lax.rem(x + 4 - i, 4)
        return at, s, 4 * z + at


class Codes:
    count = 2 * BATCH

    def dst(self, i, s, b):
        return 0, 2 * b + lax.rem(i, 2), lax.rem(b + i // 2, BATCH), s

    def src(self, i, s, b):
        return i, i, s // 2


class ToBlock:
    count = 1

    def dst(self, i, s, b):
        return 0, 2 * b + s // BATCH, lax.rem(s, BATCH), 0

    def src(self, i, s, b):
        return 0, BATCH * lax.rem(s, 2) + b, s // 2


class ToOwner:
    count = 1

    def dst(self, i, s, b):
        return 0, BATCH * lax.rem(s, 2) + b, s // 2, 0

    def src(self, i, s, b):
        return 0, 2 * b + s // BATCH, lax.rem(s, BATCH)


class Link:
    def __init__(self, pattern, source, result, sends, receives, s, b):
        self.pattern, self.source, self.result = pattern, source, result
        self.sends, self.receives, self.s, self.b = sends, receives, s, b

    def copy(self, i):
        piece, target_s, target_b, slot = self.pattern.dst(i, self.s, self.b)
        away = jnp.logical_or(target_s != self.s, target_b != self.b)
        return away, pltpu.make_async_remote_copy(
            src_ref=self.source(piece),
            dst_ref=self.result.at[slot],
            send_sem=self.sends.at[i],
            recv_sem=self.receives.at[slot],
            device_id=(target_s, target_b),
            device_id_type=MESH,
        )

    def keep_one(self, i):
        piece, target_s, target_b, slot = self.pattern.dst(i, self.s, self.b)
        home = jnp.logical_and(target_s == self.s, target_b == self.b)

        @pl.when(home)
        def _():
            self.result[slot] = self.source(piece)[...]

    def each(self, action):
        loop(self.pattern.count, action)

    def start_one(self, i):
        away, copy = self.copy(i)
        pl.when(away)(copy.start)

    def keep(self):
        self.each(self.keep_one)

    def start(self):
        self.each(self.start_one)
        self.keep()

    def receive(self):
        def wait(i):
            slot, other_s, other_b = self.pattern.src(i, self.s, self.b)
            away = jnp.logical_or(other_s != self.s, other_b != self.b)
            copy = pltpu.make_async_remote_copy(
                src_ref=self.result.at[slot],
                dst_ref=self.result.at[slot],
                send_sem=self.sends.at[i],
                recv_sem=self.receives.at[slot],
                device_id=(other_s, other_b),
                device_id_type=MESH,
            )
            pl.when(away)(copy.wait_recv)

        self.each(wait)

    def drain(self):
        def wait(i):
            away, copy = self.copy(i)
            pl.when(away)(copy.wait_send)

        self.each(wait)


def dot(left, right):
    return jnp.dot(left, right, preferred_element_type=F32)


def dot_rows(left, right):
    return lax.dot_general(left, right, (((0,), (0,)), ((), ())), preferred_element_type=F32)


def dot_cols(left, right):
    return lax.dot_general(left, right, (((1,), (1,)), ((), ())), preferred_element_type=F32)


def iota(shape, dim):
    return lax.broadcasted_iota(jnp.int32, shape, dim)


def zero_one(mask):
    return jnp.where(mask, 1.0, 0.0).astype(BF16)


def gelu_grad(x):
    inner = math.sqrt(2.0 / math.pi) * (x + 0.044715 * x * x * x)
    t = jnp.tanh(inner)
    slope = math.sqrt(2.0 / math.pi) * (1.0 + 3 * 0.044715 * x * x)
    return 0.5 * (1.0 + t) + 0.5 * x * (1.0 - t * t) * slope


def total(ref, count):
    value = ref[0].astype(F32)
    for j in range(1, count):
        value = value + ref[j].astype(F32)
    return value


def loop(count, step):
    def body(i, carry):
        step(i)
        return carry

    lax.fori_loop(0, count, body, 0)


def rows_of(i, size):
    return pl.ds(pl.multiple_of(i * size, size), size)


INPUTS = dict(codes=0, cot=0, gain=0, stem=0, conv_h=0, down_h=0, q_h=0, k_h=0, v_h=0, o_h=0, up_h=0)
OUTPUTS = dict(
    features=((128, 768), BF16),
    g_stem=((6, 4, 15), F32),
    g_conv=((3, 6, 768), F32),
    g_down=((12, 768), F32),
    g_gain=((1, 128), F32),
    g_up=((6, 1536), F32),
    g_q=((96, 128), F32),
    g_k=((96, 128), F32),
    g_v=((96, 192), F32),
    g_o=((96, 192), F32),
)
SCRATCH = dict(
    conv_w=((2304, 768), BF16),
    down_w=((768, 1536), BF16),
    in_w=((1536, 512), BF16),
    in_t=((512, 1536), BF16),
    o_w=((256, 1536), BF16),
    up_w=((1536, 768), BF16),
    stem_f=((64, 768), F32),
    stem_w=((128, 768), BF16),
    select_conv=((768, 1024), BF16),
    select_down=((768, 1024), BF16),
    codes_s=((1, 8, 128), F32),
    codes_r=((16, 8, 128), F32),
    blk_s=((1, 128, 768), BF16),
    blk_r=((1, 128, 768), BF16),
    own_s=((1, 64, 768), BF16),
    own_r=((1, 64, 768), BF16),
    low_r=((8, 64, 768), BF16),
    code=((2, 640, 128), F32),
    picked=((2, 528, 128), F32),
    emb=((8, 128, 2304), BF16),
    conv=((128, 768), F32),
    tower=((128, 768), BF16),
    pooled=((512, 768), BF16),
    lifted=((512, 1536), BF16),
    factor=((512, 128), F32),
    qkv=((512, 512), BF16),
    kv_far=((512, 384), BF16),
    d_att=((512, 256), BF16),
    att=((512, 256), BF16),
    dqkv=((512, 512), BF16),
    dkv_own=((512, 384), F32),
    dkv_far=((512, 384), F32),
    dkv_s=((512, 384), BF16),
    dkv_r=((512, 384), BF16),
    conv_acc=((128, 2304), F32),
    w_up=((256, 768), BF16),
    w_down=((512, 768), BF16),
    pick_in=((128, 512), BF16),
    pick_down=((128, 768), BF16),
    lpA_s=((8, 64, 384), BF16),
    lpA_r=((8, 64, 384), BF16),
    lpB_s=((8, 64, 384), BF16),
    lpB_r=((4, 64, 384), BF16),
    lpC_s=((1, 64, 384), BF16),
    lpC_r=((1, 64, 384), BF16),
    lpD_s=((4, 64, 384), BF16),
    lpD_r=((4, 64, 384), BF16),
    pdA_s=((8, 64, 384), BF16),
    pdA_r=((8, 64, 384), BF16),
    pdB_s=((8, 64, 384), BF16),
    pdB_r=((4, 64, 384), BF16),
    pdC_s=((1, 64, 384), BF16),
    pdC_r=((1, 64, 384), BF16),
    pdD_s=((4, 64, 384), BF16),
    pdD_r=((4, 64, 384), BF16),
    feat_s=((1, 128, 768), BF16),
    feat_r=((1, 128, 768), BF16),
    mean_s=((1, 8, 128), F32),
    mean_r=((8, 8, 128), F32),
    gain_s=((1, 8, 128), F32),
    gain_r=((8, 8, 128), F32),
    dc_s=((8, 128, 128), BF16),
    dc_r=((8, 128, 128), BF16),
    ds_s=((8, 64, 128), BF16),
    ds_r=((8, 64, 128), BF16),
    up_s=((8, 16, 768), BF16),
    up_r=((8, 16, 768), BF16),
    first_s=((8, 16, 768), BF16),
    first_r=((8, 16, 768), BF16),
    rows_c_s=((8, 2, 48, 640), BF16),
    rows_c_r=((1, 8, 48, 640), BF16),
    rows_s=((8, 48, 640), BF16),
    rows_r=((8, 48, 640), BF16),
    side_c_s=((8, 2, 48, 256), BF16),
    side_c_r=((1, 8, 48, 256), BF16),
    side_s=((8, 48, 256), BF16),
    side_r=((8, 48, 256), BF16),
    mn_s=((1, 48, 640), BF16),
    mn_r=((8, 48, 640), BF16),
    full_r=((1, 8, 48, 640), BF16),
    summed=((768, 640), BF16),
    slices=((512, 512), BF16),
    rest=((512, 256), BF16),
    down_c_s=((8, 2, 16, 768), BF16),
    down_c_r=((1, 8, 16, 768), BF16),
    down_s=((8, 16, 768), BF16),
    down_r=((8, 16, 768), BF16),
    conv_c_s=((8, 2, 16, 1280), BF16),
    conv_c_r=((1, 8, 16, 1280), BF16),
    conv_s=((8, 16, 1280), BF16),
    conv_r=((8, 16, 1280), BF16),
)
LINKS = dict(
    codes=Codes(),
    own=ToBlock(),
    blk=ToBlock(),
    low=Share(),
    lpA=XBlocks(),
    lpB=ZBlocks(),
    lpC=ZOne(),
    lpD=XOne(),
    pdA=XBlocks(),
    pdB=ZBlocks(),
    pdC=ZOne(),
    pdD=XOne(),
    feat=ToOwner(),
    mean=Share(),
    gain=Share(),
    dc=OverBatch(),
    ds=OverBatch(),
    up=OverBatch(),
    first=OverBatch(),
    rows_c=Core(),
    rows=OverQuads(),
    side_c=Core(),
    side=OverQuads(),
    mn=QuadShare(),
    full=Core(),
    down_c=Core(),
    down=OverQuads(),
    conv_c=Core(),
    conv=OverQuads(),
)


FORWARDED = dict(low="own_r", full="mn_r")


class Namespace:
    pass


def kernel_body(*refs):
    names = list(INPUTS) + list(OUTPUTS) + [x + "_" for x in SCRATCH]
    n = Namespace()
    for name, ref in zip(names, refs):
        setattr(n, name, ref)
    semaphores = refs[len(names) :]
    weight_sems, swap_send, swap_recv = semaphores[:3]
    s, b = lax.axis_index("seq"), lax.axis_index("batch")
    h = lax.rem(s, 2)
    z = b // 4
    peer = (s + 1 - 2 * h, b)
    links = Namespace()
    for k, (name, pattern) in enumerate(LINKS.items()):
        sent = getattr(n, FORWARDED.get(name, name + "_s") + "_")
        if name == "full":
            source = lambda piece, sent=sent: sent
        elif name.endswith("_c"):
            source = lambda piece, sent=sent: sent.at[:, piece]
        else:
            source = lambda piece, sent=sent: sent.at[piece]
        result = getattr(n, name + "_r_")
        link = Link(pattern, source, result, semaphores[3 + 2 * k], semaphores[4 + 2 * k], s, b)
        setattr(links, name, link)

    barrier = pltpu.get_barrier_semaphore()
    for link in (links.codes, links.low, links.rows, links.rows_c, links.feat):
        pattern = link.pattern

        def greet(i, pattern=pattern):
            _, other_s, other_b = pattern.src(i, s, b)

            @pl.when(jnp.logical_or(other_s != s, other_b != b))
            def _():
                pl.semaphore_signal(
                    barrier, inc=1, device_id=(other_s, other_b), device_id_type=MESH
                )

        loop(pattern.count, greet)
    own_window = (b == s // 2).astype(jnp.int32)
    own_block = own_window * (s == BATCH * h + b).astype(jnp.int32)
    expected = 16 + 7 + 7 + 1 + 1 - own_window - own_block

    weights = [
        pltpu.make_async_copy(source, target, weight_sems.at[k])
        for k, (source, target) in enumerate(
            [
                (n.q_h, n.in_w_.at[:, pl.ds(0, 128)]),
                (n.k_h, n.in_w_.at[:, pl.ds(128, 128)]),
                (n.v_h, n.in_t_.at[pl.ds(256, 192)]),
                (n.o_h, n.o_w_.at[pl.ds(0, 192)]),
                (n.conv_h, n.conv_w_),
                (n.down_h, n.down_w_),
                (n.up_h, n.up_w_),
            ]
        )
    ]
    for copy in weights:
        copy.start()

    row, column = iota((128, 128), 0), iota((128, 128), 1)
    order = zero_one(column == jnp.where(row < 64, 2 * row, 2 * row - 127))
    codes = jnp.broadcast_to((n.codes[...] + 1).astype(F32), (8, 128)).astype(BF16)
    n.codes_s_[0] = dot_cols(codes, order)
    cot = dot(order, n.cot[...])
    n.own_s_[0] = (cot[:64] + cot[64:]).astype(BF16)
    n.blk_s_[0] = cot.astype(BF16)

    pl.semaphore_wait(barrier, expected)
    links.codes.start()
    links.own.start()

    def fill(c):
        within = iota((1, 128), 1)
        i, m = lax.rem(within, 8), within // 8
        good = i < 6
        rows = iota((768, 128), 0)
        place = rows_of(c, 128)
        n.select_conv_[:, place] = zero_one(rows == jnp.where(good, 6 * (8 * m + c) + i, -1))
        wanted = 12 * (8 * (m // 2) + c) + 6 * lax.rem(m, 2) + i
        n.select_down_[:, place] = zero_one(rows == jnp.where(good, wanted, -1))

    loop(8, fill)
    for t in range(15):
        n.stem_f_[4 * t : 4 * t + 4, :] = n.stem[t].astype(F32)
    n.stem_f_[60:, :] = jnp.zeros((4, 768), F32)
    n.stem_w_[:64, :] = n.stem_f_[...].astype(BF16)
    n.stem_w_[64:, :] = jnp.zeros((64, 768), BF16)
    for copy in weights[:4]:
        copy.wait()
    n.o_w_[192:, :] = jnp.zeros((64, 1536), BF16)
    n.in_t_[448:, :] = jnp.zeros((64, 1536), BF16)
    eye, eye2 = zero_one(row == column), zero_one(iota((256, 256), 0) == iota((256, 256), 1))
    n.in_t_[:128, :] = dot_cols(eye, n.in_w_[:, :128]).astype(BF16)
    n.in_t_[128:256, :] = dot_cols(eye, n.in_w_[:, 128:256]).astype(BF16)
    n.in_w_[:, 256:] = dot_rows(n.in_t_[256:, :], eye2).astype(BF16)

    links.codes.receive()
    ones = jnp.ones((128, 128), BF16)
    for i in range(10):
        place = BATCH * h + (i - 1)
        inside = jnp.logical_and(place >= 0, place < 16)
        line = n.codes_r_[jnp.clip(place, 0, 15)][0:1]
        line = jnp.where(inside, line, 0.0)
        spread = dot(jnp.where(row == column, line, 0.0).astype(BF16), ones)
        n.code_[0, 64 * i : 64 * i + 64] = spread[:64]
        n.code_[1, 64 * i : 64 * i + 64] = spread[64:]
    lane_tap = iota((1, 128), 1) // 4
    lane_code = (iota((1, 128), 1) % 4 + 1).astype(F32)
    for parity in range(2):
        picked = jnp.zeros((528, 128), F32)
        for tap in range(15):
            offset = parity + tap - 7
            stream, shift = offset % 2, (offset - offset % 2) // 2
            begin = 56 + shift
            picked = jnp.where(lane_tap == tap, n.code_[stream, begin : begin + 528, :], picked)
        where = iota((528, 128), 0) - 8 + 512 * h
        inside = jnp.logical_and(where >= 0, where < 1024)
        n.picked_[parity] = jnp.where(inside, picked, 0.0)

    links.own.receive()
    links.low.start()
    links.blk.start()

    def one_hots(j):
        found = []
        for parity in range(2):
            near = n.picked_[parity, pl.ds(pl.multiple_of(64 * j, 64), 80), :]
            for step in (-4, 0, 4):
                found.append(zero_one(near[8 + step : 72 + step] == lane_code))
        return found

    def embed(j):
        value = dot(jnp.concatenate(one_hots(j), axis=0), n.stem_w_[...]).astype(BF16)
        for parity in range(2):
            for step in range(3):
                begin = 64 * (3 * parity + step)
                n.emb_[j, 64 * parity : 64 * parity + 64, 768 * step : 768 * step + 768] = value[
                    begin : begin + 64
                ]

    loop(8, embed)
    for copy in weights[4:]:
        copy.wait()
    gain = n.gain[...].reshape(1, 1536)

    def forward(t):
        four = pl.ds(4 * t, 4)
        here = rows_of(t, 256)
        conv = dot(n.emb_[four].reshape(512, 2304), n.conv_w_[...])
        center = n.emb_[four, :, 768:1536].reshape(512, 768).astype(F32)
        tower = (center + jax.nn.gelu(conv)).astype(BF16)
        halves = tower.astype(F32).reshape(4, 2, 64, 768)
        pooled = (0.5 * (halves[:, 0] + halves[:, 1])).astype(BF16).reshape(256, 768)
        n.pooled_[here, :] = pooled
        lifted = dot(pooled, n.down_w_[...]).astype(BF16)
        n.lifted_[here, :] = lifted
        lifted = lifted.astype(F32)
        factor = lax.rsqrt(jnp.mean(lifted * lifted, axis=-1, keepdims=True) + EPSILON)
        n.factor_[here, :] = jnp.broadcast_to(factor, (256, 128))
        normed = (lifted * factor * gain).astype(BF16)
        n.qkv_[here, :] = dot(normed, n.in_w_[...]).astype(BF16)

    loop(2, forward)
    swap = pltpu.make_async_remote_copy(
        src_ref=n.qkv_.at[:, pl.ds(128, 384)], dst_ref=n.kv_far_,
        send_sem=swap_send.at[0], recv_sem=swap_recv.at[0], device_id=peer, device_id_type=MESH,
    )
    swap.start()
    n.w_up_[...] = dot(n.o_w_[...], n.up_w_[...]).astype(BF16)
    links.low.receive()

    def low():
        return n.low_r_[...].reshape(512, 768)

    n.d_att_[...] = dot_cols(low(), n.w_up_[...]).astype(BF16)
    n.dkv_own_[...] = jnp.zeros((512, 384), F32)
    n.dkv_far_[...] = jnp.zeros((512, 384), F32)
    swap.wait()

    scale = 1.0 / math.sqrt(128)

    def send_pair(name, t, value):
        half = value.astype(BF16)
        getattr(n, name + "A_s_")[pl.ds(2 * t, 2)] = half[:, :384].reshape(2, 64, 384)
        getattr(n, name + "B_s_")[pl.ds(2 * t, 2)] = half[:, 384:].reshape(2, 64, 384)
        for j in (2 * t, 2 * t + 1):
            to, side = lax.rem(j, 4), j // 4
            getattr(links, name + "A").start_one(2 * lax.rem(to - lax.rem(b, 4) + 4, 4) + side)

            @pl.when(side != z)
            def _():
                getattr(links, name + "B").start_one(to)

    def attend(t):
        here = rows_of(t, 128)
        q, da = n.qkv_[here, :128], n.d_att_[here, :]
        blocks = (
            (n.qkv_[:, 128:256], n.qkv_[:, 256:], n.dkv_own_),
            (n.kv_far_[:, :128], n.kv_far_[:, 128:], n.dkv_far_),
        )
        scores = [dot_cols(q, k) * scale for k, _, _ in blocks]
        sums = sum(jnp.sum(jnp.exp(x), axis=1, keepdims=True) for x in scores)
        log_total = jnp.log(sums)
        probs = [jnp.exp(x - log_total) for x in scores]
        dprobs = [dot_cols(da, v) for _, v, _ in blocks]
        inner = sum(jnp.sum(p * d, axis=1, keepdims=True) for p, d in zip(probs, dprobs))
        att = jnp.zeros((128, 256), F32)
        dq = jnp.zeros((128, 128), F32)
        for (k, v, total_ref), p, d in zip(blocks, probs, dprobs):
            ds = (p * (d - inner)).astype(BF16)
            pb = p.astype(BF16)
            att = att + dot(pb, v)
            dq = dq + dot(ds, k)
            total_ref[:, :128] += dot_rows(ds, q) * scale
            total_ref[:, 128:] += dot_rows(pb, da)
        att = att.astype(BF16)
        n.att_[here, :] = att
        n.dqkv_[here, :128] = (dq * scale).astype(BF16)
        send_pair("lp", t, dot(att, n.w_up_[...]))

    loop(4, attend)
    n.dkv_s_[...] = n.dkv_far_[...].astype(BF16)
    swap_back = pltpu.make_async_remote_copy(
        src_ref=n.dkv_s_, dst_ref=n.dkv_r_, send_sem=swap_send.at[1], recv_sem=swap_recv.at[1],
        device_id=peer, device_id_type=MESH,
    )
    swap_back.start()
    gained = (n.in_t_[...].astype(F32) * gain).astype(BF16)
    n.w_down_[...] = dot_cols(gained, n.down_w_[...]).astype(BF16)
    pieces = dot_rows(low(), n.att_[...])[:, :192].astype(BF16)
    n.rows_c_s_[:, :, :, 448:] = pieces.reshape(8, 2, 48, 192)
    scaled = (n.pooled_[...].astype(F32) * n.factor_[:, 0:1]).astype(BF16)
    swap_back.wait()
    n.dqkv_[:, 128:] = (n.dkv_own_[...] + n.dkv_r_[...].astype(F32)).astype(BF16)

    pieces = dot_rows(scaled, n.dqkv_[...])[:, :448].astype(BF16)
    n.rows_c_s_[:, :, :, :448] = pieces.reshape(8, 2, 48, 448)
    links.rows_c.start()

    def back_through_projections(t):
        send_pair("pd", t, dot(n.dqkv_[rows_of(t, 128), :], n.w_down_[...]))

    loop(4, back_through_projections)

    def core_sum(name):
        getattr(links, name + "_c").receive()
        mine = getattr(n, name + "_c_s_")
        far = getattr(n, name + "_c_r_")
        target = getattr(n, name + "_s_")

        def add(j):
            target[j] = (mine[j, h].astype(F32) + far[0, j].astype(F32)).astype(BF16)

        loop(8, add)
        getattr(links, name).start()

    def first_hop(name):
        over_x, over_z = getattr(links, name + "A"), getattr(links, name + "B")
        over_x.keep()
        over_x.receive()
        there = 1 - z
        value = over_x.result[there].astype(F32)
        for j in range(1, 4):
            value = value + over_x.result[2 * j + there].astype(F32)
        getattr(n, name + "C_s_")[0] = value.astype(BF16)
        getattr(links, name + "C").start()
        over_z.receive()
        value = getattr(n, name + "B_s_")[pl.ds(4 * z, 4)].astype(F32)
        value = value + over_z.result[...].astype(F32)
        getattr(n, name + "D_s_")[...] = value.astype(BF16)
        getattr(links, name + "D").start()

    def second_hop(name):
        getattr(links, name + "C").receive()
        left = getattr(links, name + "C").result[0].astype(F32)
        for j in range(4):
            left = left + getattr(links, name + "A").result[2 * j + z].astype(F32)
        getattr(links, name + "D").receive()
        return jnp.concatenate([left, total(getattr(links, name + "D").result, 4)], axis=1)

    pick = n.select_down_[:, rows_of(b, 128)]
    for half in range(2):
        wide = slice(768 * half, 768 * half + 768)
        n.slices_[:, 128 * half : 128 * half + 128] = dot(n.lifted_[:, wide], pick).astype(BF16)
    core_sum("rows")
    n.side_c_s_[...] = dot_rows(low(), n.slices_[:, :256]).astype(BF16).reshape(8, 2, 48, 256)
    links.side_c.start()
    first_hop("lp")
    first_hop("pd")
    core_sum("side")

    here = rows_of(b, 64)
    n.conv_[...] = dot(n.emb_[b], n.conv_w_[...])
    center = n.emb_[b, :, 768:1536].astype(F32)
    n.tower_[...] = (center + jax.nn.gelu(n.conv_[...])).astype(BF16)
    lifted = n.lifted_[here, :]
    factor = n.factor_[here, 0:1]
    cube = factor * factor * factor
    d_updated = dot_cols(n.own_r_[0], n.up_w_[...]).astype(BF16)
    behind = dot_cols(jnp.concatenate([lifted, d_updated], axis=0), n.down_w_[...])
    lowered = dot(lifted, n.up_w_[...])
    slope = gelu_grad(n.conv_[...])
    lowered = lowered + second_hop("lp")
    features = n.tower_[...].astype(F32) + jnp.concatenate([lowered, lowered], axis=0)
    n.feat_s_[0] = dot_rows(order, features.astype(BF16)).astype(BF16)
    links.feat.start()

    lane, channel = iota((128, 1536), 0), iota((128, 1536), 1)
    wanted = jnp.where(lane < 96, 96 * s + lane, -1)
    hit = channel == wanted
    gain_here = jnp.sum(jnp.where(hit, gain, 0.0), axis=1, keepdims=True)[:96]
    n.pick_down_[...] = dot_cols(zero_one(hit), n.down_w_[...]).astype(BF16)
    wanted = 96 * s + 12 * (lane // 16) + 6 * (lane % 16 // 8) + lane % 8
    hit = jnp.logical_and(channel == wanted, lane % 8 < 6)
    gained = (n.in_t_[...].astype(F32) * gain).astype(BF16)
    n.pick_in_[...] = dot_cols(zero_one(hit), gained).astype(BF16)
    straight = second_hop("pd")
    mean = jnp.sum(straight * n.pooled_[here, :].astype(F32), axis=-1, keepdims=True) / 1536.0
    d_pooled = 0.5 * (factor * straight - cube * mean * behind[:64] + behind[64:])
    links.blk.receive()
    d_tower = n.blk_r_[0].astype(F32) + jnp.concatenate([d_pooled, d_pooled], axis=0)
    d_tower = d_tower.astype(BF16)
    d_conv = (d_tower.astype(F32) * slope).astype(BF16)
    moved = dot(d_conv, n.select_conv_[...]).astype(BF16)
    for j in range(8):
        n.dc_s_[j] = moved[:, 128 * j : 128 * j + 128]
    links.dc.start()
    diagonal = iota((64, 128), 0) == iota((64, 128), 1)
    line = jnp.sum(jnp.where(diagonal, mean, 0.0), axis=0, keepdims=True)
    n.mean_s_[0] = jnp.broadcast_to(line, (8, 128))
    links.mean.start()

    links.rows.receive()
    summed = total(n.rows_r_, 8).astype(BF16)
    n.mn_s_[0] = summed
    links.mn.start()

    hots = one_hots(b)
    d_stem = jnp.zeros((128, 768), F32)
    for step in range(3):
        d_emb = dot_cols(d_conv, n.conv_w_[768 * step : 768 * step + 768, :])
        if step == 1:
            d_emb = d_emb + d_tower.astype(F32)
        hot = jnp.concatenate([hots[step], hots[3 + step]], axis=0)
        d_stem = d_stem + dot_rows(hot, d_emb.astype(BF16))
    moved = dot(d_stem[:64].astype(BF16), n.select_conv_[...]).astype(BF16)
    for j in range(8):
        n.ds_s_[j] = moved[:, 128 * j : 128 * j + 128]
    links.ds.start()

    own = jnp.concatenate([summed[:, 448:], jnp.zeros((48, 64), BF16)], axis=1)
    wide = dot(own, n.o_w_[...])
    links.side.receive()
    sides = total(n.side_r_, 8).astype(BF16)
    sides = [dot_cols(sides[:, 128 * half : 128 * half + 128], pick) for half in range(2)]
    wide = (wide + jnp.concatenate(sides, axis=1)).astype(BF16)
    groups = iota((64, 48), 0)
    groups = jnp.where(groups % 8 < 6, 6 * (groups // 8) + groups % 8, -1)
    wide = dot(zero_one(iota((64, 48), 1) == groups), wide)
    n.up_s_[:, 0:8, :] = wide[:, :768].reshape(8, 8, 768).astype(BF16)
    n.up_s_[:, 8:16, :] = wide[:, 768:].reshape(8, 8, 768).astype(BF16)
    links.up.start()

    for half in range(2):
        wide = slice(768 * half, 768 * half + 768)
        part = dot_rows(pick, n.up_w_[wide, :]).astype(BF16)
        n.slices_[:, 256 + 128 * half : 384 + 128 * half] = dot_cols(low(), part).astype(BF16)
    n.conv_acc_[...] = jnp.zeros((128, 2304), F32)
    links.dc.receive()

    def conv_grads(t):
        pair = pl.ds(2 * t, 2)
        left = n.dc_r_[pair].reshape(256, 128)
        n.conv_acc_[...] += dot_rows(left, n.emb_[pair].reshape(256, 2304))

    loop(4, conv_grads)
    links.ds.receive()
    same = zero_one(iota((512, 128), 0) % 64 == iota((512, 128), 1))
    stem = dot_rows(n.ds_r_[...].reshape(512, 128), same)
    n.conv_c_s_[:, :, 0:8, :] = n.conv_acc_[:, :1280].reshape(8, 2, 8, 1280).astype(BF16)
    rest = jnp.concatenate([n.conv_acc_[:, 1280:], stem, jnp.zeros((128, 128), F32)], axis=1)
    n.conv_c_s_[:, :, 8:16, :] = rest.reshape(8, 2, 8, 1280).astype(BF16)
    links.conv_c.start()

    links.mean.receive()

    def remainder(j):
        rows = rows_of(j, 64)
        mean = jnp.sum(jnp.where(diagonal, n.mean_r_[j][0:1], 0.0), axis=1, keepdims=True)
        factor = n.factor_[rows, 0:1]
        part = factor * factor * factor * mean * n.slices_[rows, :256].astype(F32)
        n.rest_[rows, :] = (n.slices_[rows, 256:].astype(F32) - part).astype(BF16)

    loop(8, remainder)
    n.down_c_s_[...] = dot_rows(n.rest_[...], n.pooled_[...]).astype(BF16).reshape(8, 2, 16, 768)
    links.down_c.start()

    core_sum("conv")
    links.mn.receive()
    links.full.start()
    core_sum("down")

    links.full.receive()

    def assemble(q):
        near = pl.ds(pl.multiple_of(96 * q + 48 * h, 16), 48)
        far = pl.ds(pl.multiple_of(96 * q + 48 * (1 - h), 16), 48)
        n.summed_[near, :] = n.mn_r_[q]
        n.summed_[far, :] = n.full_r_[0, q]

    loop(8, assemble)
    first = dot_cols(n.pick_in_[...], n.summed_[:, :512])
    n.first_s_[...] = first.astype(BF16).reshape(8, 16, 768)
    links.first.start()
    inner = dot(n.pick_down_[...], n.summed_[:, :512])[:96]
    rows = pl.ds(pl.multiple_of(96 * s, 16), 96)
    part = jnp.sum(inner * n.in_w_[rows, :].astype(F32), axis=1, keepdims=True)
    diagonal = iota((96, 128), 0) == iota((96, 128), 1)
    line = jnp.sum(jnp.where(diagonal, part, 0.0), axis=0, keepdims=True)
    n.gain_s_[0] = jnp.broadcast_to(line, (8, 128))
    links.gain.start()
    inner = inner * gain_here
    n.g_q[...] = inner[:, :128]
    n.g_k[...] = inner[:, 128:256]
    n.g_v[...] = inner[:, 256:448]
    n.g_o[...] = dot(n.up_w_[rows, :], n.summed_[:, 384:])[:, 64:]

    links.feat.receive()
    n.features[...] = n.feat_r_[0]
    links.up.receive()
    up = total(n.up_r_, 8)
    n.g_up[:, :768] = up[0:6]
    n.g_up[:, 768:] = up[8:14]
    links.conv.receive()
    conv = total(n.conv_r_, 8)
    n.g_conv[0] = conv[0:6, :768]
    n.g_conv[1] = jnp.concatenate([conv[0:6, 768:], conv[8:14, :256]], axis=1)
    n.g_conv[2] = conv[8:14, 256:1024]
    stem = conv[8:16, 1024:1152].astype(BF16)
    for code in range(4):
        taps = iota((128, 15), 0) == 4 * iota((128, 15), 1) + code
        n.g_stem[:, code, :] = dot(stem, zero_one(taps))[:6]
    links.down.receive()
    links.first.receive()
    down = total(n.down_r_, 8) + total(n.first_r_, 8)
    n.g_down[0:6, :] = down[0:6]
    n.g_down[6:12, :] = down[8:14]
    links.gain.receive()
    gains = total(n.gain_r_, 8)
    high = gains.astype(BF16)
    fine = (gains - high.astype(F32)).astype(BF16)
    shift = zero_one(jnp.logical_and(row == column + 12 * b, column < 12))
    n.g_gain[...] = (dot(high, shift) + dot(fine, shift))[0:1]
    for link in vars(links).values():
        link.drain()


def finish_body(*refs):
    number = len(OUTPUTS)
    for source, target in zip(refs[:number], refs[number:]):
        target[...] = source[...]


def per_device(
    base_codes,
    stem_weight,
    conv_weight,
    down_weight,
    norm_gain,
    query_weight,
    key_weight,
    value_weight,
    output_weight,
    up_weight,
    cotangent,
):
    vmem, anywhere = pl.BlockSpec(memory_space=pltpu.VMEM), pl.BlockSpec(memory_space=pl.ANY)
    semaphores = [pltpu.SemaphoreType.DMA((7,))] + [pltpu.SemaphoreType.DMA((2,))] * 2
    shapes = {name: x[0] for name, x in SCRATCH.items()}
    for name, pattern in LINKS.items():
        semaphores += [
            pltpu.SemaphoreType.DMA((pattern.count,)),
            pltpu.SemaphoreType.DMA((shapes[name + "_r"][0],)),
        ]
    out_shape = [jax.ShapeDtypeStruct(shape, dtype) for shape, dtype in OUTPUTS.values()]
    results = pl.pallas_call(
        kernel_body,
        out_shape=out_shape,
        in_specs=[vmem] * 4 + [anywhere] * 7,
        out_specs=[vmem] * len(OUTPUTS),
        scratch_shapes=[pltpu.VMEM(shape, dtype) for shape, dtype in SCRATCH.values()] + semaphores,
        compiler_params=pltpu.CompilerParams(
            collective_id=0, has_side_effects=True, vmem_limit_bytes=60 * 1024 * 1024
        ),
        name="step",
    )(
        base_codes,
        cotangent[0],
        norm_gain,
        stem_weight,
        conv_weight.reshape(2304, 768),
        down_weight,
        query_weight,
        key_weight,
        value_weight.T,
        output_weight,
        up_weight,
    )
    features, g_stem, g_conv, g_down, g_gain, g_up, g_q, g_k, g_v, g_o = pl.pallas_call(
        finish_body,
        out_shape=out_shape,
        in_specs=[vmem] * len(OUTPUTS),
        out_specs=[vmem] * len(OUTPUTS),
        name="finish",
    )(*results)
    return (
        features[None],
        g_stem.transpose(2, 1, 0),
        g_conv.transpose(0, 2, 1),
        g_down.T,
        g_gain[0, :12],
        g_up.T,
        g_q,
        g_k,
        g_v,
        g_o,
    )


def solution(mesh):
    placed = (
        P("batch", "seq"),
        P(),
        P(),
        P(),
        P(),
        P(None, "batch"),
        P(None, "batch"),
        P(None, "batch"),
        P("batch", None),
        P(),
        P("batch", "seq", None),
    )
    return jax.shard_map(
        per_device,
        mesh=mesh,
        in_specs=placed,
        out_specs=(
            P("batch", "seq", None),
            P(None, None, ("seq", "batch")),
            P(None, None, ("seq", "batch")),
            P(None, ("seq", "batch")),
            P(("seq", "batch")),
            P(None, ("seq", "batch")),
            P("seq", "batch"),
            P("seq", "batch"),
            P("seq", "batch"),
            P("seq", "batch"),
        ),
        check_vma=False,
    )
```

```python
import functools
import math

import jax
import jax.numpy as jnp
from jax import lax
from jax.experimental import pallas as pl
from jax.experimental.pallas import tpu as pltpu
from jax.sharding import PartitionSpec as P

EPSILON = 1e-06
MESH = pl.DeviceIdType.MESH
F32 = jnp.float32
BF16 = jnp.bfloat16
SEQ = 16
BATCH = 8


class OverBatch:
    count = BATCH

    def dst(self, i, s, b):
        j = lax.rem(b + i, BATCH)
        return j, s, j, b

    def src(self, i, s, b):
        j = lax.rem(b + BATCH - i, BATCH)
        return j, s, j


class Share:
    count = BATCH

    def dst(self, i, s, b):
        return 0, s, lax.rem(b + i, BATCH), b

    def src(self, i, s, b):
        j = lax.rem(b + BATCH - i, BATCH)
        return j, s, j


class OverQuads:
    count = SEQ // 2

    def dst(self, i, s, b):
        j = lax.rem(s // 2 + i, SEQ // 2)
        return j, 2 * j + lax.rem(s, 2), b, s // 2

    def src(self, i, s, b):
        j = lax.rem(s // 2 + SEQ // 2 - i, SEQ // 2)
        return j, 2 * j + lax.rem(s, 2), b


class QuadShare:
    count = SEQ // 2

    def dst(self, i, s, b):
        j = lax.rem(s // 2 + i, SEQ // 2)
        return 0, 2 * j + lax.rem(s, 2), b, s // 2

    def src(self, i, s, b):
        j = lax.rem(s // 2 + SEQ // 2 - i, SEQ // 2)
        return j, 2 * j + lax.rem(s, 2), b


class Core:
    count = 1

    def dst(self, i, s, b):
        other = 1 - lax.rem(s, 2)
        return other, s - lax.rem(s, 2) + other, b, 0

    def src(self, i, s, b):
        return 0, s + 1 - 2 * lax.rem(s, 2), b


class XBlocks:
    count = 8

    def dst(self, i, s, b):
        z, x = b // 4, lax.rem(b, 4)
        to, side = lax.rem(x + i // 2, 4), lax.rem(i, 2)
        return 4 * side + to, s, 4 * z + to, 2 * x + side

    def src(self, i, s, b):
        z, x = b // 4, lax.rem(b, 4)
        at, side = lax.rem(x + 4 - i // 2, 4), lax.rem(i, 2)
        return 2 * at + side, s, 4 * z + at


class ZBlocks:
    count = 4

    def dst(self, i, s, b):
        other = 1 - b // 4
        return 4 * other + i, s, 4 * other + lax.rem(b, 4), i

    def src(self, i, s, b):
        return i, s, 4 * (1 - b // 4) + lax.rem(b, 4)


class ZOne:
    count = 1

    def dst(self, i, s, b):
        return 0, s, 4 * (1 - b // 4) + lax.rem(b, 4), 0

    def src(self, i, s, b):
        return 0, s, 4 * (1 - b // 4) + lax.rem(b, 4)


class XOne:
    count = 4

    def dst(self, i, s, b):
        z, x = b // 4, lax.rem(b, 4)
        to = lax.rem(x + i, 4)
        return to, s, 4 * z + to, x

    def src(self, i, s, b):
        z, x = b // 4, lax.rem(b, 4)
        at = lax.rem(x + 4 - i, 4)
        return at, s, 4 * z + at


class Codes:
    count = 2 * BATCH

    def dst(self, i, s, b):
        return 0, 2 * b + lax.rem(i, 2), lax.rem(b + i // 2, BATCH), s

    def src(self, i, s, b):
        return i, i, s // 2


class Neighbours:
    count = 2

    def dst(self, i, s, b):
        target = s + 1 - 2 * i
        inside = jnp.logical_and(target >= 0, target < SEQ)
        return 0, jnp.where(inside, target, s), b, i

    def src(self, i, s, b):
        source = s - 1 + 2 * i
        inside = jnp.logical_and(source >= 0, source < SEQ)
        return i, jnp.where(inside, source, s), b


class ToBlock:
    count = 1

    def dst(self, i, s, b):
        return 0, 2 * b + s // BATCH, lax.rem(s, BATCH), 0

    def src(self, i, s, b):
        return 0, BATCH * lax.rem(s, 2) + b, s // 2


class ToOwner:
    count = 1

    def dst(self, i, s, b):
        return 0, BATCH * lax.rem(s, 2) + b, s // 2, 0

    def src(self, i, s, b):
        return 0, 2 * b + s // BATCH, lax.rem(s, BATCH)


class Link:
    def __init__(self, pattern, source, result, sends, receives, s, b):
        self.pattern, self.source, self.result = pattern, source, result
        self.sends, self.receives, self.s, self.b = sends, receives, s, b

    def copy(self, i):
        piece, target_s, target_b, slot = self.pattern.dst(i, self.s, self.b)
        away = jnp.logical_or(target_s != self.s, target_b != self.b)
        return away, pltpu.make_async_remote_copy(
            src_ref=self.source(piece),
            dst_ref=self.result.at[slot],
            send_sem=self.sends.at[i],
            recv_sem=self.receives.at[slot],
            device_id=(target_s, target_b),
            device_id_type=MESH,
        )

    def keep_one(self, i):
        piece, target_s, target_b, slot = self.pattern.dst(i, self.s, self.b)
        home = jnp.logical_and(target_s == self.s, target_b == self.b)

        @pl.when(home)
        def _():
            self.result[slot] = self.source(piece)[...]

    def each(self, action):
        loop(self.pattern.count, action)

    def start_one(self, i):
        away, copy = self.copy(i)
        pl.when(away)(copy.start)

    def keep(self):
        self.each(self.keep_one)

    def start(self):
        self.each(self.start_one)
        self.keep()

    def receive(self):
        def wait(i):
            slot, other_s, other_b = self.pattern.src(i, self.s, self.b)
            away = jnp.logical_or(other_s != self.s, other_b != self.b)
            copy = pltpu.make_async_remote_copy(
                src_ref=self.result.at[slot],
                dst_ref=self.result.at[slot],
                send_sem=self.sends.at[i],
                recv_sem=self.receives.at[slot],
                device_id=(other_s, other_b),
                device_id_type=MESH,
            )
            pl.when(away)(copy.wait_recv)

        self.each(wait)

    def drain(self):
        def wait(i):
            away, copy = self.copy(i)
            pl.when(away)(copy.wait_send)

        self.each(wait)


def dot(left, right):
    return jnp.dot(left, right, preferred_element_type=F32)


def dot_rows(left, right):
    return lax.dot_general(left, right, (((0,), (0,)), ((), ())), preferred_element_type=F32)


def dot_cols(left, right):
    return lax.dot_general(left, right, (((1,), (1,)), ((), ())), preferred_element_type=F32)


def iota(shape, dim):
    return lax.broadcasted_iota(jnp.int32, shape, dim)


def zero_one(mask):
    return jnp.where(mask, 1.0, 0.0).astype(BF16)


def gelu_grad(x):
    inner = math.sqrt(2.0 / math.pi) * (x + 0.044715 * x * x * x)
    t = jnp.tanh(inner)
    slope = math.sqrt(2.0 / math.pi) * (1.0 + 3 * 0.044715 * x * x)
    return 0.5 * (1.0 + t) + 0.5 * x * (1.0 - t * t) * slope


def total(ref, count):
    value = ref[0].astype(F32)
    for j in range(1, count):
        value = value + ref[j].astype(F32)
    return value


def loop(count, step):
    def body(i, carry):
        step(i)
        return carry

    lax.fori_loop(0, count, body, 0)


def rows_of(i, size):
    return pl.ds(pl.multiple_of(i * size, size), size)


INPUTS = dict(codes=0, cot=0, gain=0, stem=0, conv_h=0, down_h=0, q_h=0, k_h=0, v_h=0, o_h=0, up_h=0)
OUTPUTS = dict(
    features=((128, 768), BF16),
    g_stem=((6, 4, 15), F32),
    g_conv=((3, 6, 768), F32),
    g_down=((12, 768), F32),
    g_gain=((1, 128), F32),
    g_up=((6, 1536), F32),
    g_q=((96, 128), F32),
    g_k=((96, 128), F32),
    g_v=((96, 192), F32),
    g_o=((96, 192), F32),
)
SCRATCH = dict(
    conv_w=((2304, 768), BF16),
    down_w=((768, 1536), BF16),
    in_w=((1536, 512), BF16),
    in_t=((512, 1536), BF16),
    o_w=((256, 1536), BF16),
    up_w=((1536, 768), BF16),
    stem_f=((64, 768), F32),
    stem_w=((128, 768), BF16),
    select_conv=((768, 1024), BF16),
    select_down=((768, 1024), BF16),
    codes_s=((1, 8, 128), F32),
    codes_r=((16, 8, 128), F32),
    near_r=((2, 8, 128), F32),
    blk_s=((1, 64, 768), BF16),
    blk_r=((1, 64, 768), BF16),
    own_s=((1, 64, 768), BF16),
    own_r=((1, 64, 768), BF16),
    low_r=((8, 64, 768), BF16),
    code=((2, 640, 128), F32),
    picked=((2, 528, 128), F32),
    emb=((8, 128, 2304), BF16),
    conv=((128, 768), F32),
    tower=((128, 768), F32),
    own_code=((2, 192, 128), F32),
    own_emb=((128, 2304), BF16),
    pooled=((512, 768), BF16),
    lifted=((512, 1536), BF16),
    factor=((512, 128), F32),
    qkv=((512, 512), BF16),
    kv_far=((512, 384), BF16),
    d_att=((512, 256), BF16),
    att=((512, 256), BF16),
    dqkv=((512, 512), BF16),
    dkv_own=((512, 384), F32),
    dkv_far=((512, 384), F32),
    dkv_s=((512, 384), BF16),
    dkv_r=((512, 384), BF16),
    conv_acc=((128, 2304), F32),
    w_up=((256, 768), BF16),
    w_down=((512, 768), BF16),
    pick_in=((128, 512), BF16),
    pick_down=((128, 768), BF16),
    lpA_s=((8, 64, 384), BF16),
    lpA_r=((8, 64, 384), BF16),
    lpB_s=((8, 64, 384), BF16),
    lpB_r=((4, 64, 384), BF16),
    lpC_s=((1, 64, 384), BF16),
    lpC_r=((1, 64, 384), BF16),
    lpD_s=((4, 64, 384), BF16),
    lpD_r=((4, 64, 384), BF16),
    pdA_s=((8, 64, 384), BF16),
    pdA_r=((8, 64, 384), BF16),
    pdB_s=((8, 64, 384), BF16),
    pdB_r=((4, 64, 384), BF16),
    pdC_s=((1, 64, 384), BF16),
    pdC_r=((1, 64, 384), BF16),
    pdD_s=((4, 64, 384), BF16),
    pdD_r=((4, 64, 384), BF16),
    feat_s=((1, 64, 768), BF16),
    feat_r=((1, 64, 768), BF16),
    mean_s=((1, 8, 128), F32),
    mean_r=((8, 8, 128), F32),
    gain_s=((1, 8, 128), F32),
    gain_r=((8, 8, 128), F32),
    dc_s=((8, 128, 128), BF16),
    dc_r=((8, 128, 128), BF16),
    ds_s=((8, 64, 128), BF16),
    ds_r=((8, 64, 128), BF16),
    up_s=((8, 16, 768), BF16),
    up_r=((8, 16, 768), BF16),
    first_s=((8, 16, 768), BF16),
    first_r=((8, 16, 768), BF16),
    rows_c_s=((8, 2, 48, 640), BF16),
    rows_c_r=((1, 8, 48, 640), BF16),
    rows_s=((8, 48, 640), BF16),
    rows_r=((8, 48, 640), BF16),
    side_c_s=((8, 2, 48, 256), BF16),
    side_c_r=((1, 8, 48, 256), BF16),
    side_s=((8, 48, 256), BF16),
    side_r=((8, 48, 256), BF16),
    mn_s=((1, 48, 640), BF16),
    mn_r=((8, 48, 640), BF16),
    full_r=((1, 8, 48, 640), BF16),
    summed=((768, 640), BF16),
    slices=((512, 512), BF16),
    rest=((512, 256), BF16),
    down_c_s=((8, 2, 16, 768), BF16),
    down_c_r=((1, 8, 16, 768), BF16),
    down_s=((8, 16, 768), BF16),
    down_r=((8, 16, 768), BF16),
    conv_c_s=((8, 2, 16, 1280), BF16),
    conv_c_r=((1, 8, 16, 1280), BF16),
    conv_s=((8, 16, 1280), BF16),
    conv_r=((8, 16, 1280), BF16),
)
LINKS = dict(
    codes=Codes(),
    near=Neighbours(),
    own=ToBlock(),
    blk=ToBlock(),
    low=Share(),
    lpA=XBlocks(),
    lpB=ZBlocks(),
    lpC=ZOne(),
    lpD=XOne(),
    pdA=XBlocks(),
    pdB=ZBlocks(),
    pdC=ZOne(),
    pdD=XOne(),
    feat=ToOwner(),
    mean=Share(),
    gain=Share(),
    dc=OverBatch(),
    ds=OverBatch(),
    up=OverBatch(),
    first=OverBatch(),
    rows_c=Core(),
    rows=OverQuads(),
    side_c=Core(),
    side=OverQuads(),
    mn=QuadShare(),
    full=Core(),
    down_c=Core(),
    down=OverQuads(),
    conv_c=Core(),
    conv=OverQuads(),
)


FORWARDED = dict(near="codes_s", low="own_r", full="mn_r")


class Namespace:
    pass


def kernel_body(*refs):
    names = list(INPUTS) + list(OUTPUTS) + [x + "_" for x in SCRATCH]
    n = Namespace()
    for name, ref in zip(names, refs):
        setattr(n, name, ref)
    semaphores = refs[len(names) :]
    weight_sems, swap_send, swap_recv = semaphores[:3]
    s, b = lax.axis_index("seq"), lax.axis_index("batch")
    h = lax.rem(s, 2)
    z = b // 4
    peer = (s + 1 - 2 * h, b)
    links = Namespace()
    for k, (name, pattern) in enumerate(LINKS.items()):
        sent = getattr(n, FORWARDED.get(name, name + "_s") + "_")
        if name == "full":
            source = lambda piece, sent=sent: sent
        elif name.endswith("_c"):
            source = lambda piece, sent=sent: sent.at[:, piece]
        else:
            source = lambda piece, sent=sent: sent.at[piece]
        result = getattr(n, name + "_r_")
        link = Link(pattern, source, result, semaphores[3 + 2 * k], semaphores[4 + 2 * k], s, b)
        setattr(links, name, link)

    barrier = pltpu.get_barrier_semaphore()
    for link in (links.codes, links.low, links.rows, links.rows_c, links.feat, links.near):
        pattern = link.pattern

        def greet(i, pattern=pattern):
            _, other_s, other_b = pattern.src(i, s, b)

            @pl.when(jnp.logical_or(other_s != s, other_b != b))
            def _():
                pl.semaphore_signal(
                    barrier, inc=1, device_id=(other_s, other_b), device_id_type=MESH
                )

        loop(pattern.count, greet)
    own_window = (b == s // 2).astype(jnp.int32)
    own_block = own_window * (s == BATCH * h + b).astype(jnp.int32)
    ends = (s == 0).astype(jnp.int32) + (s == SEQ - 1).astype(jnp.int32)
    expected = 16 + 7 + 7 + 1 + 1 + 2 - own_window - own_block - ends

    weights = [
        pltpu.make_async_copy(source, target, weight_sems.at[k])
        for k, (source, target) in enumerate(
            [
                (n.q_h, n.in_w_.at[:, pl.ds(0, 128)]),
                (n.k_h, n.in_w_.at[:, pl.ds(128, 128)]),
                (n.v_h, n.in_t_.at[pl.ds(256, 192)]),
                (n.o_h, n.o_w_.at[pl.ds(0, 192)]),
                (n.conv_h, n.conv_w_),
                (n.down_h, n.down_w_),
                (n.up_h, n.up_w_),
            ]
        )
    ]
    for copy in weights:
        copy.start()

    row, column = iota((128, 128), 0), iota((128, 128), 1)
    order = zero_one(column == jnp.where(row < 64, 2 * row, 2 * row - 127))
    codes = jnp.broadcast_to((n.codes[...] + 1).astype(F32), (8, 128)).astype(BF16)
    n.codes_s_[0] = dot_cols(codes, order)
    cot = dot(order, n.cot[...])
    n.own_s_[0] = (cot[:64] + cot[64:]).astype(BF16)
    n.blk_s_[0] = cot[:64].astype(BF16)

    pl.semaphore_wait(barrier, expected)
    links.codes.start()
    links.own.start()
    links.near.each(links.near.start_one)

    def fill(c):
        within = iota((1, 128), 1)
        i, m = lax.rem(within, 8), within // 8
        good = i < 6
        rows = iota((768, 128), 0)
        place = rows_of(c, 128)
        n.select_conv_[:, place] = zero_one(rows == jnp.where(good, 6 * (8 * m + c) + i, -1))
        wanted = 12 * (8 * (m // 2) + c) + 6 * lax.rem(m, 2) + i
        n.select_down_[:, place] = zero_one(rows == jnp.where(good, wanted, -1))

    loop(8, fill)
    for t in range(15):
        n.stem_f_[4 * t : 4 * t + 4, :] = n.stem[t].astype(F32)
    n.stem_f_[60:, :] = jnp.zeros((4, 768), F32)
    n.stem_w_[:64, :] = n.stem_f_[...].astype(BF16)
    n.stem_w_[64:, :] = jnp.zeros((64, 768), BF16)
    for copy in weights[:4]:
        copy.wait()
    n.o_w_[192:, :] = jnp.zeros((64, 1536), BF16)
    n.in_t_[448:, :] = jnp.zeros((64, 1536), BF16)
    eye, eye2 = zero_one(row == column), zero_one(iota((256, 256), 0) == iota((256, 256), 1))
    n.in_t_[:128, :] = dot_cols(eye, n.in_w_[:, :128]).astype(BF16)
    n.in_t_[128:256, :] = dot_cols(eye, n.in_w_[:, 128:256]).astype(BF16)
    n.in_w_[:, 256:] = dot_rows(n.in_t_[256:, :], eye2).astype(BF16)

    links.codes.receive()
    ones = jnp.ones((128, 128), BF16)
    lane_tap = iota((1, 128), 1) // 4
    lane_code = (iota((1, 128), 1) % 4 + 1).astype(F32)

    def spread(line, target, i):
        lines = dot(jnp.where(row == column, line, 0.0).astype(BF16), ones)
        target[0, 64 * i : 64 * i + 64] = lines[:64]
        target[1, 64 * i : 64 * i + 64] = lines[64:]

    def pick_taps(source, parity, count, first):
        picked = jnp.zeros((count, 128), F32)
        for tap in range(15):
            offset = parity + tap - 7
            stream, shift = offset % 2, (offset - offset % 2) // 2
            begin = 56 + shift
            picked = jnp.where(lane_tap == tap, source[stream, begin : begin + count, :], picked)
        where = iota((count, 128), 0) - 8 + first
        inside = jnp.logical_and(where >= 0, where < 1024)
        return jnp.where(inside, picked, 0.0)

    for i in range(10):
        place = BATCH * h + (i - 1)
        inside = jnp.logical_and(place >= 0, place < 16)
        line = n.codes_r_[jnp.clip(place, 0, 15)][0:1]
        spread(jnp.where(inside, line, 0.0), n.code_, i)
    for parity in range(2):
        n.picked_[parity] = pick_taps(n.code_, parity, 528, 512 * h)

    links.own.receive()
    links.low.start()

    def one_hots(j):
        found = []
        for parity in range(2):
            near = n.picked_[parity, pl.ds(pl.multiple_of(64 * j, 64), 80), :]
            for step in (-4, 0, 4):
                found.append(zero_one(near[8 + step : 72 + step] == lane_code))
        return found

    def embed(j):
        value = dot(jnp.concatenate(one_hots(j), axis=0), n.stem_w_[...]).astype(BF16)
        for parity in range(2):
            for step in range(3):
                begin = 64 * (3 * parity + step)
                n.emb_[j, 64 * parity : 64 * parity + 64, 768 * step : 768 * step + 768] = value[
                    begin : begin + 64
                ]

    loop(8, embed)
    for copy in weights[4:]:
        copy.wait()
    gain = n.gain[...].reshape(1, 1536)

    def forward(t):
        four = pl.ds(4 * t, 4)
        here = rows_of(t, 256)
        conv = dot(n.emb_[four].reshape(512, 2304), n.conv_w_[...])
        center = n.emb_[four, :, 768:1536].reshape(512, 768).astype(F32)
        tower = (center + jax.nn.gelu(conv)).astype(BF16)
        halves = tower.astype(F32).reshape(4, 2, 64, 768)
        pooled = (0.5 * (halves[:, 0] + halves[:, 1])).astype(BF16).reshape(256, 768)
        n.pooled_[here, :] = pooled
        lifted = dot(pooled, n.down_w_[...]).astype(BF16)
        n.lifted_[here, :] = lifted
        lifted = lifted.astype(F32)
        factor = lax.rsqrt(jnp.mean(lifted * lifted, axis=-1, keepdims=True) + EPSILON)
        n.factor_[here, :] = jnp.broadcast_to(factor, (256, 128))
        normed = (lifted * factor * gain).astype(BF16)
        n.qkv_[here, :] = dot(normed, n.in_w_[...]).astype(BF16)

    loop(2, forward)
    swap = pltpu.make_async_remote_copy(
        src_ref=n.qkv_.at[:, pl.ds(128, 384)], dst_ref=n.kv_far_,
        send_sem=swap_send.at[0], recv_sem=swap_recv.at[0], device_id=peer, device_id_type=MESH,
    )
    swap.start()
    n.w_up_[...] = dot(n.o_w_[...], n.up_w_[...]).astype(BF16)
    links.low.receive()
    links.blk.start()

    def low():
        return n.low_r_[...].reshape(512, 768)

    n.d_att_[...] = dot_cols(low(), n.w_up_[...]).astype(BF16)
    n.dkv_own_[...] = jnp.zeros((512, 384), F32)
    n.dkv_far_[...] = jnp.zeros((512, 384), F32)
    swap.wait()

    scale = 1.0 / math.sqrt(128)

    def send_pair(name, t, value):
        half = value.astype(BF16)
        getattr(n, name + "A_s_")[pl.ds(2 * t, 2)] = half[:, :384].reshape(2, 64, 384)
        getattr(n, name + "B_s_")[pl.ds(2 * t, 2)] = half[:, 384:].reshape(2, 64, 384)
        for j in (2 * t, 2 * t + 1):
            to, side = lax.rem(j, 4), j // 4
            getattr(links, name + "A").start_one(2 * lax.rem(to - lax.rem(b, 4) + 4, 4) + side)

            @pl.when(side != z)
            def _():
                getattr(links, name + "B").start_one(to)

    def attend(t):
        here = rows_of(t, 128)
        q, da = n.qkv_[here, :128], n.d_att_[here, :]
        blocks = (
            (n.qkv_[:, 128:256], n.qkv_[:, 256:], n.dkv_own_),
            (n.kv_far_[:, :128], n.kv_far_[:, 128:], n.dkv_far_),
        )
        scores = [dot_cols(q, k) * scale for k, _, _ in blocks]
        sums = sum(jnp.sum(jnp.exp(x), axis=1, keepdims=True) for x in scores)
        log_total = jnp.log(sums)
        probs = [jnp.exp(x - log_total) for x in scores]
        dprobs = [dot_cols(da, v) for _, v, _ in blocks]
        inner = sum(jnp.sum(p * d, axis=1, keepdims=True) for p, d in zip(probs, dprobs))
        att = jnp.zeros((128, 256), F32)
        dq = jnp.zeros((128, 128), F32)
        for (k, v, total_ref), p, d in zip(blocks, probs, dprobs):
            ds = (p * (d - inner)).astype(BF16)
            pb = p.astype(BF16)
            att = att + dot(pb, v)
            dq = dq + dot(ds, k)
            total_ref[:, :128] += dot_rows(ds, q) * scale
            total_ref[:, 128:] += dot_rows(pb, da)
        att = att.astype(BF16)
        n.att_[here, :] = att
        n.dqkv_[here, :128] = (dq * scale).astype(BF16)
        send_pair("lp", t, dot(att, n.w_up_[...]))

    loop(4, attend)
    n.dkv_s_[...] = n.dkv_far_[...].astype(BF16)
    swap_back = pltpu.make_async_remote_copy(
        src_ref=n.dkv_s_, dst_ref=n.dkv_r_, send_sem=swap_send.at[1], recv_sem=swap_recv.at[1],
        device_id=peer, device_id_type=MESH,
    )
    swap_back.start()
    gained = (n.in_t_[...].astype(F32) * gain).astype(BF16)
    n.w_down_[...] = dot_cols(gained, n.down_w_[...]).astype(BF16)
    pieces = dot_rows(low(), n.att_[...])[:, :192].astype(BF16)
    n.rows_c_s_[:, :, :, 448:] = pieces.reshape(8, 2, 48, 192)
    scaled = (n.pooled_[...].astype(F32) * n.factor_[:, 0:1]).astype(BF16)
    swap_back.wait()
    n.dqkv_[:, 128:] = (n.dkv_own_[...] + n.dkv_r_[...].astype(F32)).astype(BF16)

    pieces = dot_rows(scaled, n.dqkv_[...])[:, :448].astype(BF16)
    n.rows_c_s_[:, :, :, :448] = pieces.reshape(8, 2, 48, 448)
    links.rows_c.start()

    def back_through_projections(t):
        send_pair("pd", t, dot(n.dqkv_[rows_of(t, 128), :], n.w_down_[...]))

    loop(4, back_through_projections)

    def core_sum(name):
        getattr(links, name + "_c").receive()
        mine = getattr(n, name + "_c_s_")
        far = getattr(n, name + "_c_r_")
        target = getattr(n, name + "_s_")

        def add(j):
            target[j] = (mine[j, h].astype(F32) + far[0, j].astype(F32)).astype(BF16)

        loop(8, add)
        getattr(links, name).start()

    def first_hop(name):
        over_x, over_z = getattr(links, name + "A"), getattr(links, name + "B")
        over_x.keep()
        over_x.receive()
        there = 1 - z
        value = over_x.result[there].astype(F32)
        for j in range(1, 4):
            value = value + over_x.result[2 * j + there].astype(F32)
        getattr(n, name + "C_s_")[0] = value.astype(BF16)
        getattr(links, name + "C").start()
        over_z.receive()
        value = getattr(n, name + "B_s_")[pl.ds(4 * z, 4)].astype(F32)
        value = value + over_z.result[...].astype(F32)
        getattr(n, name + "D_s_")[...] = value.astype(BF16)
        getattr(links, name + "D").start()

    def second_hop(name):
        getattr(links, name + "C").receive()
        left = getattr(links, name + "C").result[0].astype(F32)
        for j in range(4):
            left = left + getattr(links, name + "A").result[2 * j + z].astype(F32)
        getattr(links, name + "D").receive()
        return jnp.concatenate([left, total(getattr(links, name + "D").result, 4)], axis=1)

    pick = n.select_down_[:, rows_of(b, 128)]
    for half in range(2):
        wide = slice(768 * half, 768 * half + 768)
        n.slices_[:, 128 * half : 128 * half + 128] = dot(n.lifted_[:, wide], pick).astype(BF16)
    core_sum("rows")
    n.side_c_s_[...] = dot_rows(low(), n.slices_[:, :256]).astype(BF16).reshape(8, 2, 48, 256)
    links.side_c.start()
    first_hop("lp")
    first_hop("pd")
    core_sum("side")

    here = rows_of(b, 64)
    n.conv_[...] = dot(n.emb_[b], n.conv_w_[...])
    lifted = n.lifted_[here, :]
    factor = n.factor_[here, 0:1]
    cube = factor * factor * factor
    d_updated = dot_cols(n.own_r_[0], n.up_w_[...]).astype(BF16)
    behind = dot_cols(jnp.concatenate([lifted, d_updated], axis=0), n.down_w_[...])
    lowered = dot(lifted, n.up_w_[...])
    slope = gelu_grad(n.conv_[...])
    lowered = lowered + second_hop("lp")
    n.feat_s_[0] = lowered.astype(BF16)
    links.feat.start()

    lane, channel = iota((128, 1536), 0), iota((128, 1536), 1)
    wanted = jnp.where(lane < 96, 96 * s + lane, -1)
    hit = channel == wanted
    gain_here = jnp.sum(jnp.where(hit, gain, 0.0), axis=1, keepdims=True)[:96]
    n.pick_down_[...] = dot_cols(zero_one(hit), n.down_w_[...]).astype(BF16)
    wanted = 96 * s + 12 * (lane // 16) + 6 * (lane % 16 // 8) + lane % 8
    hit = jnp.logical_and(channel == wanted, lane % 8 < 6)
    gained = (n.in_t_[...].astype(F32) * gain).astype(BF16)
    n.pick_in_[...] = dot_cols(zero_one(hit), gained).astype(BF16)

    links.near.receive()
    spread(jnp.where(s > 0, n.near_r_[0][0:1], 0.0), n.own_code_, 0)
    spread(n.codes_s_[0][0:1], n.own_code_, 1)
    spread(jnp.where(s < SEQ - 1, n.near_r_[1][0:1], 0.0), n.own_code_, 2)
    for parity in range(2):
        near = pick_taps(n.own_code_, parity, 80, 64 * s)
        steps = [zero_one(near[8 + step : 72 + step] == lane_code) for step in (-4, 0, 4)]
        value = dot(jnp.concatenate(steps, axis=0), n.stem_w_[...]).astype(BF16)
        for step in range(3):
            n.own_emb_[64 * parity : 64 * parity + 64, 768 * step : 768 * step + 768] = value[
                64 * step : 64 * step + 64
            ]
    center = n.own_emb_[:, 768:1536].astype(F32)
    tower = center + jax.nn.gelu(dot(n.own_emb_[...], n.conv_w_[...]))
    n.tower_[...] = tower.astype(BF16).astype(F32)

    straight = second_hop("pd")
    mean = jnp.sum(straight * n.pooled_[here, :].astype(F32), axis=-1, keepdims=True) / 1536.0
    d_pooled = 0.5 * (factor * straight - cube * mean * behind[:64] + behind[64:])
    links.blk.receive()
    even = n.blk_r_[0].astype(F32)
    odd = n.own_r_[0].astype(F32) - even
    d_tower = jnp.concatenate([even + d_pooled, odd + d_pooled], axis=0)
    d_tower = d_tower.astype(BF16)
    d_conv = (d_tower.astype(F32) * slope).astype(BF16)
    moved = dot(d_conv, n.select_conv_[...]).astype(BF16)
    for j in range(8):
        n.dc_s_[j] = moved[:, 128 * j : 128 * j + 128]
    links.dc.start()
    diagonal = iota((64, 128), 0) == iota((64, 128), 1)
    line = jnp.sum(jnp.where(diagonal, mean, 0.0), axis=0, keepdims=True)
    n.mean_s_[0] = jnp.broadcast_to(line, (8, 128))
    links.mean.start()

    links.rows.receive()
    summed = total(n.rows_r_, 8).astype(BF16)
    n.mn_s_[0] = summed
    links.mn.start()

    hots = one_hots(b)
    d_stem = jnp.zeros((128, 768), F32)
    for step in range(3):
        d_emb = dot_cols(d_conv, n.conv_w_[768 * step : 768 * step + 768, :])
        if step == 1:
            d_emb = d_emb + d_tower.astype(F32)
        hot = jnp.concatenate([hots[step], hots[3 + step]], axis=0)
        d_stem = d_stem + dot_rows(hot, d_emb.astype(BF16))
    moved = dot(d_stem[:64].astype(BF16), n.select_conv_[...]).astype(BF16)
    for j in range(8):
        n.ds_s_[j] = moved[:, 128 * j : 128 * j + 128]
    links.ds.start()

    own = jnp.concatenate([summed[:, 448:], jnp.zeros((48, 64), BF16)], axis=1)
    wide = dot(own, n.o_w_[...])
    links.side.receive()
    sides = total(n.side_r_, 8).astype(BF16)
    sides = [dot_cols(sides[:, 128 * half : 128 * half + 128], pick) for half in range(2)]
    wide = (wide + jnp.concatenate(sides, axis=1)).astype(BF16)
    groups = iota((64, 48), 0)
    groups = jnp.where(groups % 8 < 6, 6 * (groups // 8) + groups % 8, -1)
    wide = dot(zero_one(iota((64, 48), 1) == groups), wide)
    n.up_s_[:, 0:8, :] = wide[:, :768].reshape(8, 8, 768).astype(BF16)
    n.up_s_[:, 8:16, :] = wide[:, 768:].reshape(8, 8, 768).astype(BF16)
    links.up.start()

    for half in range(2):
        wide = slice(768 * half, 768 * half + 768)
        part = dot_rows(pick, n.up_w_[wide, :]).astype(BF16)
        n.slices_[:, 256 + 128 * half : 384 + 128 * half] = dot_cols(low(), part).astype(BF16)
    n.conv_acc_[...] = jnp.zeros((128, 2304), F32)
    links.dc.receive()

    def conv_grads(t):
        pair = pl.ds(2 * t, 2)
        left = n.dc_r_[pair].reshape(256, 128)
        n.conv_acc_[...] += dot_rows(left, n.emb_[pair].reshape(256, 2304))

    loop(4, conv_grads)
    links.ds.receive()
    same = zero_one(iota((512, 128), 0) % 64 == iota((512, 128), 1))
    stem = dot_rows(n.ds_r_[...].reshape(512, 128), same)
    n.conv_c_s_[:, :, 0:8, :] = n.conv_acc_[:, :1280].reshape(8, 2, 8, 1280).astype(BF16)
    rest = jnp.concatenate([n.conv_acc_[:, 1280:], stem, jnp.zeros((128, 128), F32)], axis=1)
    n.conv_c_s_[:, :, 8:16, :] = rest.reshape(8, 2, 8, 1280).astype(BF16)
    links.conv_c.start()

    links.mean.receive()

    def remainder(j):
        rows = rows_of(j, 64)
        mean = jnp.sum(jnp.where(diagonal, n.mean_r_[j][0:1], 0.0), axis=1, keepdims=True)
        factor = n.factor_[rows, 0:1]
        part = factor * factor * factor * mean * n.slices_[rows, :256].astype(F32)
        n.rest_[rows, :] = (n.slices_[rows, 256:].astype(F32) - part).astype(BF16)

    loop(8, remainder)
    n.down_c_s_[...] = dot_rows(n.rest_[...], n.pooled_[...]).astype(BF16).reshape(8, 2, 16, 768)
    links.down_c.start()

    core_sum("conv")
    links.mn.receive()
    links.full.start()
    core_sum("down")

    links.full.receive()

    def assemble(q):
        near = pl.ds(pl.multiple_of(96 * q + 48 * h, 16), 48)
        far = pl.ds(pl.multiple_of(96 * q + 48 * (1 - h), 16), 48)
        n.summed_[near, :] = n.mn_r_[q]
        n.summed_[far, :] = n.full_r_[0, q]

    loop(8, assemble)
    first = dot_cols(n.pick_in_[...], n.summed_[:, :512])
    n.first_s_[...] = first.astype(BF16).reshape(8, 16, 768)
    links.first.start()
    inner = dot(n.pick_down_[...], n.summed_[:, :512])[:96]
    rows = pl.ds(pl.multiple_of(96 * s, 16), 96)
    part = jnp.sum(inner * n.in_w_[rows, :].astype(F32), axis=1, keepdims=True)
    diagonal = iota((96, 128), 0) == iota((96, 128), 1)
    line = jnp.sum(jnp.where(diagonal, part, 0.0), axis=0, keepdims=True)
    n.gain_s_[0] = jnp.broadcast_to(line, (8, 128))
    links.gain.start()
    inner = inner * gain_here
    n.g_q[...] = inner[:, :128]
    n.g_k[...] = inner[:, 128:256]
    n.g_v[...] = inner[:, 256:448]
    n.g_o[...] = dot(n.up_w_[rows, :], n.summed_[:, 384:])[:, 64:]

    links.feat.receive()
    lowered = n.feat_r_[0].astype(F32)
    features = n.tower_[...] + jnp.concatenate([lowered, lowered], axis=0)
    n.features[...] = dot_rows(order, features.astype(BF16)).astype(BF16)
    links.up.receive()
    up = total(n.up_r_, 8)
    n.g_up[:, :768] = up[0:6]
    n.g_up[:, 768:] = up[8:14]
    links.conv.receive()
    conv = total(n.conv_r_, 8)
    n.g_conv[0] = conv[0:6, :768]
    n.g_conv[1] = jnp.concatenate([conv[0:6, 768:], conv[8:14, :256]], axis=1)
    n.g_conv[2] = conv[8:14, 256:1024]
    stem = conv[8:16, 1024:1152].astype(BF16)
    for code in range(4):
        taps = iota((128, 15), 0) == 4 * iota((128, 15), 1) + code
        n.g_stem[:, code, :] = dot(stem, zero_one(taps))[:6]
    links.down.receive()
    links.first.receive()
    down = total(n.down_r_, 8) + total(n.first_r_, 8)
    n.g_down[0:6, :] = down[0:6]
    n.g_down[6:12, :] = down[8:14]
    links.gain.receive()
    gains = total(n.gain_r_, 8)
    high = gains.astype(BF16)
    fine = (gains - high.astype(F32)).astype(BF16)
    shift = zero_one(jnp.logical_and(row == column + 12 * b, column < 12))
    n.g_gain[...] = (dot(high, shift) + dot(fine, shift))[0:1]
    for link in vars(links).values():
        link.drain()


def finish_body(*refs):
    number = len(OUTPUTS)
    for source, target in zip(refs[:number], refs[number:]):
        target[...] = source[...]


def per_device(
    base_codes,
    stem_weight,
    conv_weight,
    down_weight,
    norm_gain,
    query_weight,
    key_weight,
    value_weight,
    output_weight,
    up_weight,
    cotangent,
):
    vmem, anywhere = pl.BlockSpec(memory_space=pltpu.VMEM), pl.BlockSpec(memory_space=pl.ANY)
    semaphores = [pltpu.SemaphoreType.DMA((7,))] + [pltpu.SemaphoreType.DMA((2,))] * 2
    shapes = {name: x[0] for name, x in SCRATCH.items()}
    for name, pattern in LINKS.items():
        semaphores += [
            pltpu.SemaphoreType.DMA((pattern.count,)),
            pltpu.SemaphoreType.DMA((shapes[name + "_r"][0],)),
        ]
    out_shape = [jax.ShapeDtypeStruct(shape, dtype) for shape, dtype in OUTPUTS.values()]
    results = pl.pallas_call(
        kernel_body,
        out_shape=out_shape,
        in_specs=[vmem] * 4 + [anywhere] * 7,
        out_specs=[vmem] * len(OUTPUTS),
        scratch_shapes=[pltpu.VMEM(shape, dtype) for shape, dtype in SCRATCH.values()] + semaphores,
        compiler_params=pltpu.CompilerParams(
            collective_id=0, has_side_effects=True, vmem_limit_bytes=60 * 1024 * 1024
        ),
        name="step",
    )(
        base_codes,
        cotangent[0],
        norm_gain,
        stem_weight,
        conv_weight.reshape(2304, 768),
        down_weight,
        query_weight,
        key_weight,
        value_weight.T,
        output_weight,
        up_weight,
    )
    features, g_stem, g_conv, g_down, g_gain, g_up, g_q, g_k, g_v, g_o = pl.pallas_call(
        finish_body,
        out_shape=out_shape,
        in_specs=[vmem] * len(OUTPUTS),
        out_specs=[vmem] * len(OUTPUTS),
        name="finish",
    )(*results)
    return (
        features[None],
        g_stem.transpose(2, 1, 0),
        g_conv.transpose(0, 2, 1),
        g_down.T,
        g_gain[0, :12],
        g_up.T,
        g_q,
        g_k,
        g_v,
        g_o,
    )


def solution(mesh):
    placed = (
        P("batch", "seq"),
        P(),
        P(),
        P(),
        P(),
        P(None, "batch"),
        P(None, "batch"),
        P(None, "batch"),
        P("batch", None),
        P(),
        P("batch", "seq", None),
    )
    return jax.shard_map(
        per_device,
        mesh=mesh,
        in_specs=placed,
        out_specs=(
            P("batch", "seq", None),
            P(None, None, ("seq", "batch")),
            P(None, None, ("seq", "batch")),
            P(None, ("seq", "batch")),
            P(("seq", "batch")),
            P(None, ("seq", "batch")),
            P("seq", "batch"),
            P("seq", "batch"),
            P("seq", "batch"),
            P("seq", "batch"),
        ),
        check_vma=False,
    )
```

```python
import functools
import math

import jax
import jax.numpy as jnp
from jax import lax
from jax.experimental import pallas as pl
from jax.experimental.pallas import tpu as pltpu
from jax.sharding import PartitionSpec as P

EPSILON = 1e-06
MESH = pl.DeviceIdType.MESH
F32 = jnp.float32
BF16 = jnp.bfloat16
SEQ = 16
BATCH = 8


class OverBatch:
    count = BATCH

    def dst(self, i, s, b):
        j = lax.rem(b + i, BATCH)
        return j, s, j, b

    def src(self, i, s, b):
        j = lax.rem(b + BATCH - i, BATCH)
        return j, s, j


class Share:
    count = BATCH

    def dst(self, i, s, b):
        return 0, s, lax.rem(b + i, BATCH), b

    def src(self, i, s, b):
        j = lax.rem(b + BATCH - i, BATCH)
        return j, s, j


class OverQuads:
    count = SEQ // 2

    def dst(self, i, s, b):
        j = lax.rem(s // 2 + i, SEQ // 2)
        return j, 2 * j + lax.rem(s, 2), b, s // 2

    def src(self, i, s, b):
        j = lax.rem(s // 2 + SEQ // 2 - i, SEQ // 2)
        return j, 2 * j + lax.rem(s, 2), b


class OverY:
    count = 4

    def dst(self, i, s, b):
        to = lax.rem(s // 4 + i, 4)
        return to, 4 * to + lax.rem(s, 4), b, s // 4

    def src(self, i, s, b):
        at = lax.rem(s // 4 + 4 - i, 4)
        return at, 4 * at + lax.rem(s, 4), b


class ShareY(OverY):
    def dst(self, i, s, b):
        to = lax.rem(s // 4 + i, 4)
        return 0, 4 * to + lax.rem(s, 4), b, s // 4


class FarZ:
    count = 1

    def dst(self, i, s, b):
        mine = lax.rem(s, 4) // 2
        return 1 - mine, s + 2 - 4 * mine, b, 0

    def src(self, i, s, b):
        return 0, s + 2 - 4 * (lax.rem(s, 4) // 2), b


class ShareFarZ(FarZ):
    def dst(self, i, s, b):
        return 0, s + 2 - 4 * (lax.rem(s, 4) // 2), b, 0


class Core:
    count = 1

    def dst(self, i, s, b):
        other = 1 - lax.rem(s, 2)
        return other, s - lax.rem(s, 2) + other, b, 0

    def src(self, i, s, b):
        return 0, s + 1 - 2 * lax.rem(s, 2), b


class XBlocks:
    count = 8

    def dst(self, i, s, b):
        z, x = b // 4, lax.rem(b, 4)
        to, side = lax.rem(x + i // 2, 4), lax.rem(i, 2)
        return 4 * side + to, s, 4 * z + to, 2 * x + side

    def src(self, i, s, b):
        z, x = b // 4, lax.rem(b, 4)
        at, side = lax.rem(x + 4 - i // 2, 4), lax.rem(i, 2)
        return 2 * at + side, s, 4 * z + at


class ZBlocks:
    count = 4

    def dst(self, i, s, b):
        other = 1 - b // 4
        return 4 * other + i, s, 4 * other + lax.rem(b, 4), i

    def src(self, i, s, b):
        return i, s, 4 * (1 - b // 4) + lax.rem(b, 4)


class ZOne:
    count = 1

    def dst(self, i, s, b):
        return 0, s, 4 * (1 - b // 4) + lax.rem(b, 4), 0

    def src(self, i, s, b):
        return 0, s, 4 * (1 - b // 4) + lax.rem(b, 4)


class XOne:
    count = 4

    def dst(self, i, s, b):
        z, x = b // 4, lax.rem(b, 4)
        to = lax.rem(x + i, 4)
        return to, s, 4 * z + to, x

    def src(self, i, s, b):
        z, x = b // 4, lax.rem(b, 4)
        at = lax.rem(x + 4 - i, 4)
        return at, s, 4 * z + at


class Codes:
    count = 2 * BATCH

    def dst(self, i, s, b):
        return 0, 2 * b + lax.rem(i, 2), lax.rem(b + i // 2, BATCH), s

    def src(self, i, s, b):
        return i, i, s // 2


class Neighbours:
    count = 2

    def dst(self, i, s, b):
        target = s + 1 - 2 * i
        inside = jnp.logical_and(target >= 0, target < SEQ)
        return 0, jnp.where(inside, target, s), b, i

    def src(self, i, s, b):
        source = s - 1 + 2 * i
        inside = jnp.logical_and(source >= 0, source < SEQ)
        return i, jnp.where(inside, source, s), b


class ToBlock:
    count = 1

    def dst(self, i, s, b):
        return 0, 2 * b + s // BATCH, lax.rem(s, BATCH), 0

    def src(self, i, s, b):
        return 0, BATCH * lax.rem(s, 2) + b, s // 2


class ToOwner:
    count = 1

    def dst(self, i, s, b):
        return 0, BATCH * lax.rem(s, 2) + b, s // 2, 0

    def src(self, i, s, b):
        return 0, 2 * b + s // BATCH, lax.rem(s, BATCH)


class Link:
    def __init__(self, pattern, source, result, sends, receives, s, b):
        self.pattern, self.source, self.result = pattern, source, result
        self.sends, self.receives, self.s, self.b = sends, receives, s, b

    def copy(self, i):
        piece, target_s, target_b, slot = self.pattern.dst(i, self.s, self.b)
        away = jnp.logical_or(target_s != self.s, target_b != self.b)
        return away, pltpu.make_async_remote_copy(
            src_ref=self.source(piece),
            dst_ref=self.result.at[slot],
            send_sem=self.sends.at[i],
            recv_sem=self.receives.at[slot],
            device_id=(target_s, target_b),
            device_id_type=MESH,
        )

    def keep_one(self, i):
        piece, target_s, target_b, slot = self.pattern.dst(i, self.s, self.b)
        home = jnp.logical_and(target_s == self.s, target_b == self.b)

        @pl.when(home)
        def _():
            self.result[slot] = self.source(piece)[...]

    def each(self, action):
        loop(self.pattern.count, action)

    def start_one(self, i):
        away, copy = self.copy(i)
        pl.when(away)(copy.start)

    def keep(self):
        self.each(self.keep_one)

    def start(self):
        self.each(self.start_one)
        self.keep()

    def receive(self):
        def wait(i):
            slot, other_s, other_b = self.pattern.src(i, self.s, self.b)
            away = jnp.logical_or(other_s != self.s, other_b != self.b)
            copy = pltpu.make_async_remote_copy(
                src_ref=self.result.at[slot],
                dst_ref=self.result.at[slot],
                send_sem=self.sends.at[i],
                recv_sem=self.receives.at[slot],
                device_id=(other_s, other_b),
                device_id_type=MESH,
            )
            pl.when(away)(copy.wait_recv)

        self.each(wait)

    def drain(self):
        def wait(i):
            away, copy = self.copy(i)
            pl.when(away)(copy.wait_send)

        self.each(wait)


def dot(left, right):
    return jnp.dot(left, right, preferred_element_type=F32)


def dot_rows(left, right):
    return lax.dot_general(left, right, (((0,), (0,)), ((), ())), preferred_element_type=F32)


def dot_cols(left, right):
    return lax.dot_general(left, right, (((1,), (1,)), ((), ())), preferred_element_type=F32)


def iota(shape, dim):
    return lax.broadcasted_iota(jnp.int32, shape, dim)


def zero_one(mask):
    return jnp.where(mask, 1.0, 0.0).astype(BF16)


def gelu_grad(x):
    inner = math.sqrt(2.0 / math.pi) * (x + 0.044715 * x * x * x)
    t = jnp.tanh(inner)
    slope = math.sqrt(2.0 / math.pi) * (1.0 + 3 * 0.044715 * x * x)
    return 0.5 * (1.0 + t) + 0.5 * x * (1.0 - t * t) * slope


def total(ref, count):
    value = ref[0].astype(F32)
    for j in range(1, count):
        value = value + ref[j].astype(F32)
    return value


def loop(count, step):
    def body(i, carry):
        step(i)
        return carry

    lax.fori_loop(0, count, body, 0)


def rows_of(i, size):
    return pl.ds(pl.multiple_of(i * size, size), size)


INPUTS = dict(codes=0, cot=0, gain=0, stem=0, conv_h=0, down_h=0, q_h=0, k_h=0, v_h=0, o_h=0, up_h=0)
OUTPUTS = dict(
    features=((128, 768), BF16),
    g_stem=((6, 4, 15), F32),
    g_conv=((3, 6, 768), F32),
    g_down=((12, 768), F32),
    g_gain=((1, 128), F32),
    g_up=((6, 1536), F32),
    g_q=((96, 128), F32),
    g_k=((96, 128), F32),
    g_v=((96, 192), F32),
    g_o=((96, 192), F32),
)
SCRATCH = dict(
    conv_w=((2304, 768), BF16),
    down_w=((768, 1536), BF16),
    in_w=((1536, 512), BF16),
    in_t=((512, 1536), BF16),
    o_w=((256, 1536), BF16),
    up_w=((1536, 768), BF16),
    stem_f=((64, 768), F32),
    stem_w=((128, 768), BF16),
    select_conv=((768, 1024), BF16),
    select_down=((768, 1024), BF16),
    codes_s=((1, 8, 128), F32),
    codes_r=((16, 8, 128), F32),
    near_r=((2, 8, 128), F32),
    blk_s=((1, 64, 768), BF16),
    blk_r=((1, 64, 768), BF16),
    own_s=((1, 64, 768), BF16),
    own_r=((1, 64, 768), BF16),
    low_r=((8, 64, 768), BF16),
    code=((2, 640, 128), F32),
    picked=((2, 528, 128), F32),
    emb=((8, 128, 2304), BF16),
    conv=((128, 768), F32),
    tower=((128, 768), F32),
    own_code=((2, 192, 128), F32),
    own_emb=((128, 2304), BF16),
    pooled=((512, 768), BF16),
    lifted=((512, 1536), BF16),
    factor=((512, 128), F32),
    qkv=((512, 512), BF16),
    kv_far=((512, 384), BF16),
    d_att=((512, 256), BF16),
    att=((512, 256), BF16),
    dqkv=((512, 512), BF16),
    dkv_own=((512, 384), F32),
    dkv_far=((512, 384), F32),
    dkv_s=((512, 384), BF16),
    dkv_r=((512, 384), BF16),
    conv_acc=((128, 2304), F32),
    w_up=((256, 768), BF16),
    w_down=((512, 768), BF16),
    pick_in=((128, 512), BF16),
    pick_down=((128, 768), BF16),
    lpA_s=((8, 64, 384), BF16),
    lpA_r=((8, 64, 384), BF16),
    lpB_s=((8, 64, 384), BF16),
    lpB_r=((4, 64, 384), BF16),
    lpC_s=((1, 64, 384), BF16),
    lpC_r=((1, 64, 384), BF16),
    lpD_s=((4, 64, 384), BF16),
    lpD_r=((4, 64, 384), BF16),
    pdA_s=((8, 64, 384), BF16),
    pdA_r=((8, 64, 384), BF16),
    pdB_s=((8, 64, 384), BF16),
    pdB_r=((4, 64, 384), BF16),
    pdC_s=((1, 64, 384), BF16),
    pdC_r=((1, 64, 384), BF16),
    pdD_s=((4, 64, 384), BF16),
    pdD_r=((4, 64, 384), BF16),
    feat_s=((1, 64, 768), BF16),
    feat_r=((1, 64, 768), BF16),
    mean_s=((1, 8, 128), F32),
    mean_r=((8, 8, 128), F32),
    gain_s=((1, 8, 128), F32),
    gain_r=((8, 8, 128), F32),
    dc_s=((8, 128, 128), BF16),
    dc_r=((8, 128, 128), BF16),
    ds_s=((8, 64, 128), BF16),
    ds_r=((8, 64, 128), BF16),
    up_s=((8, 16, 768), BF16),
    up_r=((8, 16, 768), BF16),
    first_s=((8, 16, 768), BF16),
    first_r=((8, 16, 768), BF16),
    rows_c_s=((8, 2, 48, 640), BF16),
    rows_c_r=((1, 8, 48, 640), BF16),
    rows_s=((8, 48, 640), BF16),
    rows_r=((4, 2, 48, 640), BF16),
    far_s=((2, 48, 640), BF16),
    far_r=((1, 48, 640), BF16),
    side_c_s=((8, 2, 48, 256), BF16),
    side_c_r=((1, 8, 48, 256), BF16),
    side_s=((8, 48, 256), BF16),
    side_r=((8, 48, 256), BF16),
    pair_s=((1, 48, 640), BF16),
    pair_r=((1, 48, 640), BF16),
    mn_s=((1, 2, 48, 640), BF16),
    mn_r=((4, 2, 48, 640), BF16),
    full_r=((1, 4, 2, 48, 640), BF16),
    summed=((768, 640), BF16),
    slices=((512, 512), BF16),
    rest=((512, 256), BF16),
    down_c_s=((8, 2, 16, 768), BF16),
    down_c_r=((1, 8, 16, 768), BF16),
    down_s=((8, 16, 768), BF16),
    down_r=((8, 16, 768), BF16),
    conv_c_s=((8, 2, 16, 1280), BF16),
    conv_c_r=((1, 8, 16, 1280), BF16),
    conv_s=((8, 16, 1280), BF16),
    conv_r=((8, 16, 1280), BF16),
)
LINKS = dict(
    codes=Codes(),
    near=Neighbours(),
    own=ToBlock(),
    blk=ToBlock(),
    low=Share(),
    lpA=XBlocks(),
    lpB=ZBlocks(),
    lpC=ZOne(),
    lpD=XOne(),
    pdA=XBlocks(),
    pdB=ZBlocks(),
    pdC=ZOne(),
    pdD=XOne(),
    feat=ToOwner(),
    mean=Share(),
    gain=Share(),
    dc=OverBatch(),
    ds=OverBatch(),
    up=OverBatch(),
    first=OverBatch(),
    rows_c=Core(),
    rows=OverY(),
    far=FarZ(),
    pair=ShareFarZ(),
    side_c=Core(),
    side=OverQuads(),
    mn=ShareY(),
    full=Core(),
    down_c=Core(),
    down=OverQuads(),
    conv_c=Core(),
    conv=OverQuads(),
)


FORWARDED = dict(near="codes_s", low="own_r", full="mn_r")


class Namespace:
    pass


def kernel_body(*refs):
    names = list(INPUTS) + list(OUTPUTS) + [x + "_" for x in SCRATCH]
    n = Namespace()
    for name, ref in zip(names, refs):
        setattr(n, name, ref)
    semaphores = refs[len(names) :]
    weight_sems, swap_send, swap_recv = semaphores[:3]
    s, b = lax.axis_index("seq"), lax.axis_index("batch")
    h = lax.rem(s, 2)
    z = b // 4
    peer = (s + 1 - 2 * h, b)
    links = Namespace()
    for k, (name, pattern) in enumerate(LINKS.items()):
        sent = getattr(n, FORWARDED.get(name, name + "_s") + "_")
        if name == "full":
            source = lambda piece, sent=sent: sent
        elif name == "rows":
            source = lambda piece, sent=sent: sent.at[pl.ds(2 * piece, 2)]
        elif name.endswith("_c"):
            source = lambda piece, sent=sent: sent.at[:, piece]
        else:
            source = lambda piece, sent=sent: sent.at[piece]
        result = getattr(n, name + "_r_")
        link = Link(pattern, source, result, semaphores[3 + 2 * k], semaphores[4 + 2 * k], s, b)
        setattr(links, name, link)

    barrier = pltpu.get_barrier_semaphore()
    for link in (links.codes, links.low, links.side, links.rows_c, links.feat, links.near):
        pattern = link.pattern

        def greet(i, pattern=pattern):
            _, other_s, other_b = pattern.src(i, s, b)

            @pl.when(jnp.logical_or(other_s != s, other_b != b))
            def _():
                pl.semaphore_signal(
                    barrier, inc=1, device_id=(other_s, other_b), device_id_type=MESH
                )

        loop(pattern.count, greet)
    own_window = (b == s // 2).astype(jnp.int32)
    own_block = own_window * (s == BATCH * h + b).astype(jnp.int32)
    ends = (s == 0).astype(jnp.int32) + (s == SEQ - 1).astype(jnp.int32)
    expected = 16 + 7 + 7 + 1 + 1 + 2 - own_window - own_block - ends

    weights = [
        pltpu.make_async_copy(source, target, weight_sems.at[k])
        for k, (source, target) in enumerate(
            [
                (n.q_h, n.in_w_.at[:, pl.ds(0, 128)]),
                (n.k_h, n.in_w_.at[:, pl.ds(128, 128)]),
                (n.v_h, n.in_t_.at[pl.ds(256, 192)]),
                (n.o_h, n.o_w_.at[pl.ds(0, 192)]),
                (n.conv_h, n.conv_w_),
                (n.down_h, n.down_w_),
                (n.up_h, n.up_w_),
            ]
        )
    ]
    for copy in weights:
        copy.start()

    row, column = iota((128, 128), 0), iota((128, 128), 1)
    order = zero_one(column == jnp.where(row < 64, 2 * row, 2 * row - 127))
    codes = jnp.broadcast_to((n.codes[...] + 1).astype(F32), (8, 128)).astype(BF16)
    n.codes_s_[0] = dot_cols(codes, order)
    cot = dot(order, n.cot[...])
    n.own_s_[0] = (cot[:64] + cot[64:]).astype(BF16)
    n.blk_s_[0] = cot[:64].astype(BF16)

    pl.semaphore_wait(barrier, expected)
    links.codes.start()
    links.own.start()
    links.near.each(links.near.start_one)

    def fill(c):
        within = iota((1, 128), 1)
        i, m = lax.rem(within, 8), within // 8
        good = i < 6
        rows = iota((768, 128), 0)
        place = rows_of(c, 128)
        n.select_conv_[:, place] = zero_one(rows == jnp.where(good, 6 * (8 * m + c) + i, -1))
        wanted = 12 * (8 * (m // 2) + c) + 6 * lax.rem(m, 2) + i
        n.select_down_[:, place] = zero_one(rows == jnp.where(good, wanted, -1))

    loop(8, fill)
    for t in range(15):
        n.stem_f_[4 * t : 4 * t + 4, :] = n.stem[t].astype(F32)
    n.stem_f_[60:, :] = jnp.zeros((4, 768), F32)
    n.stem_w_[:64, :] = n.stem_f_[...].astype(BF16)
    n.stem_w_[64:, :] = jnp.zeros((64, 768), BF16)
    for copy in weights[:4]:
        copy.wait()
    n.o_w_[192:, :] = jnp.zeros((64, 1536), BF16)
    n.in_t_[448:, :] = jnp.zeros((64, 1536), BF16)
    eye, eye2 = zero_one(row == column), zero_one(iota((256, 256), 0) == iota((256, 256), 1))
    n.in_t_[:128, :] = dot_cols(eye, n.in_w_[:, :128]).astype(BF16)
    n.in_t_[128:256, :] = dot_cols(eye, n.in_w_[:, 128:256]).astype(BF16)
    n.in_w_[:, 256:] = dot_rows(n.in_t_[256:, :], eye2).astype(BF16)

    links.codes.receive()
    ones = jnp.ones((128, 128), BF16)
    lane_tap = iota((1, 128), 1) // 4
    lane_code = (iota((1, 128), 1) % 4 + 1).astype(F32)

    def spread(line, target, i):
        lines = dot(jnp.where(row == column, line, 0.0).astype(BF16), ones)
        target[0, 64 * i : 64 * i + 64] = lines[:64]
        target[1, 64 * i : 64 * i + 64] = lines[64:]

    def pick_taps(source, parity, count, first):
        picked = jnp.zeros((count, 128), F32)
        for tap in range(15):
            offset = parity + tap - 7
            stream, shift = offset % 2, (offset - offset % 2) // 2
            begin = 56 + shift
            picked = jnp.where(lane_tap == tap, source[stream, begin : begin + count, :], picked)
        where = iota((count, 128), 0) - 8 + first
        inside = jnp.logical_and(where >= 0, where < 1024)
        return jnp.where(inside, picked, 0.0)

    for i in range(10):
        place = BATCH * h + (i - 1)
        inside = jnp.logical_and(place >= 0, place < 16)
        line = n.codes_r_[jnp.clip(place, 0, 15)][0:1]
        spread(jnp.where(inside, line, 0.0), n.code_, i)
    for parity in range(2):
        n.picked_[parity] = pick_taps(n.code_, parity, 528, 512 * h)

    links.own.receive()
    links.low.start()

    def one_hots(j):
        found = []
        for parity in range(2):
            near = n.picked_[parity, pl.ds(pl.multiple_of(64 * j, 64), 80), :]
            for step in (-4, 0, 4):
                found.append(zero_one(near[8 + step : 72 + step] == lane_code))
        return found

    def embed(j):
        value = dot(jnp.concatenate(one_hots(j), axis=0), n.stem_w_[...]).astype(BF16)
        for parity in range(2):
            for step in range(3):
                begin = 64 * (3 * parity + step)
                n.emb_[j, 64 * parity : 64 * parity + 64, 768 * step : 768 * step + 768] = value[
                    begin : begin + 64
                ]

    loop(8, embed)
    for copy in weights[4:]:
        copy.wait()
    gain = n.gain[...].reshape(1, 1536)

    def forward(t):
        four = pl.ds(4 * t, 4)
        here = rows_of(t, 256)
        conv = dot(n.emb_[four].reshape(512, 2304), n.conv_w_[...])
        center = n.emb_[four, :, 768:1536].reshape(512, 768).astype(F32)
        tower = (center + jax.nn.gelu(conv)).astype(BF16)
        halves = tower.astype(F32).reshape(4, 2, 64, 768)
        pooled = (0.5 * (halves[:, 0] + halves[:, 1])).astype(BF16).reshape(256, 768)
        n.pooled_[here, :] = pooled
        lifted = dot(pooled, n.down_w_[...]).astype(BF16)
        n.lifted_[here, :] = lifted
        lifted = lifted.astype(F32)
        factor = lax.rsqrt(jnp.mean(lifted * lifted, axis=-1, keepdims=True) + EPSILON)
        n.factor_[here, :] = jnp.broadcast_to(factor, (256, 128))
        normed = (lifted * factor * gain).astype(BF16)
        n.qkv_[here, :] = dot(normed, n.in_w_[...]).astype(BF16)

    loop(2, forward)
    swap = pltpu.make_async_remote_copy(
        src_ref=n.qkv_.at[:, pl.ds(128, 384)], dst_ref=n.kv_far_,
        send_sem=swap_send.at[0], recv_sem=swap_recv.at[0], device_id=peer, device_id_type=MESH,
    )
    swap.start()
    n.w_up_[...] = dot(n.o_w_[...], n.up_w_[...]).astype(BF16)
    links.low.receive()
    links.blk.start()

    def low():
        return n.low_r_[...].reshape(512, 768)

    n.d_att_[...] = dot_cols(low(), n.w_up_[...]).astype(BF16)
    n.dkv_own_[...] = jnp.zeros((512, 384), F32)
    n.dkv_far_[...] = jnp.zeros((512, 384), F32)
    swap.wait()

    scale = 1.0 / math.sqrt(128)

    def send_pair(name, t, value):
        half = value.astype(BF16)
        getattr(n, name + "A_s_")[pl.ds(2 * t, 2)] = half[:, :384].reshape(2, 64, 384)
        getattr(n, name + "B_s_")[pl.ds(2 * t, 2)] = half[:, 384:].reshape(2, 64, 384)
        for j in (2 * t, 2 * t + 1):
            to, side = lax.rem(j, 4), j // 4
            getattr(links, name + "A").start_one(2 * lax.rem(to - lax.rem(b, 4) + 4, 4) + side)

            @pl.when(side != z)
            def _():
                getattr(links, name + "B").start_one(to)

    def attend(t):
        here = rows_of(t, 128)
        q, da = n.qkv_[here, :128], n.d_att_[here, :]
        blocks = (
            (n.qkv_[:, 128:256], n.qkv_[:, 256:], n.dkv_own_),
            (n.kv_far_[:, :128], n.kv_far_[:, 128:], n.dkv_far_),
        )
        scores = [dot_cols(q, k) * scale for k, _, _ in blocks]
        sums = sum(jnp.sum(jnp.exp(x), axis=1, keepdims=True) for x in scores)
        log_total = jnp.log(sums)
        probs = [jnp.exp(x - log_total) for x in scores]
        dprobs = [dot_cols(da, v) for _, v, _ in blocks]
        inner = sum(jnp.sum(p * d, axis=1, keepdims=True) for p, d in zip(probs, dprobs))
        att = jnp.zeros((128, 256), F32)
        dq = jnp.zeros((128, 128), F32)
        for (k, v, total_ref), p, d in zip(blocks, probs, dprobs):
            ds = (p * (d - inner)).astype(BF16)
            pb = p.astype(BF16)
            att = att + dot(pb, v)
            dq = dq + dot(ds, k)
            total_ref[:, :128] += dot_rows(ds, q) * scale
            total_ref[:, 128:] += dot_rows(pb, da)
        att = att.astype(BF16)
        n.att_[here, :] = att
        n.dqkv_[here, :128] = (dq * scale).astype(BF16)
        send_pair("lp", t, dot(att, n.w_up_[...]))

    loop(4, attend)
    n.dkv_s_[...] = n.dkv_far_[...].astype(BF16)
    swap_back = pltpu.make_async_remote_copy(
        src_ref=n.dkv_s_, dst_ref=n.dkv_r_, send_sem=swap_send.at[1], recv_sem=swap_recv.at[1],
        device_id=peer, device_id_type=MESH,
    )
    swap_back.start()
    gained = (n.in_t_[...].astype(F32) * gain).astype(BF16)
    n.w_down_[...] = dot_cols(gained, n.down_w_[...]).astype(BF16)
    pieces = dot_rows(low(), n.att_[...])[:, :192].astype(BF16)
    n.rows_c_s_[:, :, :, 448:] = pieces.reshape(8, 2, 48, 192)
    scaled = (n.pooled_[...].astype(F32) * n.factor_[:, 0:1]).astype(BF16)
    swap_back.wait()
    n.dqkv_[:, 128:] = (n.dkv_own_[...] + n.dkv_r_[...].astype(F32)).astype(BF16)

    pieces = dot_rows(scaled, n.dqkv_[...])[:, :448].astype(BF16)
    n.rows_c_s_[:, :, :, :448] = pieces.reshape(8, 2, 48, 448)
    links.rows_c.start()

    def back_through_projections(t):
        send_pair("pd", t, dot(n.dqkv_[rows_of(t, 128), :], n.w_down_[...]))

    loop(4, back_through_projections)

    def core_sum(name):
        getattr(links, name + "_c").receive()
        mine = getattr(n, name + "_c_s_")
        far = getattr(n, name + "_c_r_")
        target = getattr(n, name + "_s_")

        def add(j):
            target[j] = (mine[j, h].astype(F32) + far[0, j].astype(F32)).astype(BF16)

        loop(8, add)
        getattr(links, name).start()

    def first_hop(name):
        over_x, over_z = getattr(links, name + "A"), getattr(links, name + "B")
        over_x.keep()
        over_x.receive()
        there = 1 - z
        value = over_x.result[there].astype(F32)
        for j in range(1, 4):
            value = value + over_x.result[2 * j + there].astype(F32)
        getattr(n, name + "C_s_")[0] = value.astype(BF16)
        getattr(links, name + "C").start()
        over_z.receive()
        value = getattr(n, name + "B_s_")[pl.ds(4 * z, 4)].astype(F32)
        value = value + over_z.result[...].astype(F32)
        getattr(n, name + "D_s_")[...] = value.astype(BF16)
        getattr(links, name + "D").start()

    def second_hop(name):
        getattr(links, name + "C").receive()
        left = getattr(links, name + "C").result[0].astype(F32)
        for j in range(4):
            left = left + getattr(links, name + "A").result[2 * j + z].astype(F32)
        getattr(links, name + "D").receive()
        return jnp.concatenate([left, total(getattr(links, name + "D").result, 4)], axis=1)

    pick = n.select_down_[:, rows_of(b, 128)]
    for half in range(2):
        wide = slice(768 * half, 768 * half + 768)
        n.slices_[:, 128 * half : 128 * half + 128] = dot(n.lifted_[:, wide], pick).astype(BF16)
    core_sum("rows")
    n.side_c_s_[...] = dot_rows(low(), n.slices_[:, :256]).astype(BF16).reshape(8, 2, 48, 256)
    links.side_c.start()
    first_hop("lp")
    first_hop("pd")
    core_sum("side")

    here = rows_of(b, 64)
    n.conv_[...] = dot(n.emb_[b], n.conv_w_[...])
    lifted = n.lifted_[here, :]
    factor = n.factor_[here, 0:1]
    cube = factor * factor * factor
    d_updated = dot_cols(n.own_r_[0], n.up_w_[...]).astype(BF16)
    behind = dot_cols(jnp.concatenate([lifted, d_updated], axis=0), n.down_w_[...])
    lowered = dot(lifted, n.up_w_[...])
    slope = gelu_grad(n.conv_[...])
    links.rows.receive()
    n.far_s_[...] = total(n.rows_r_, 4).astype(BF16)
    links.far.start()
    lowered = lowered + second_hop("lp")
    n.feat_s_[0] = lowered.astype(BF16)


    lane, channel = iota((128, 1536), 0), iota((128, 1536), 1)
    wanted = jnp.where(lane < 96, 96 * s + lane, -1)
    hit = channel == wanted
    gain_here = jnp.sum(jnp.where(hit, gain, 0.0), axis=1, keepdims=True)[:96]
    n.pick_down_[...] = dot_cols(zero_one(hit), n.down_w_[...]).astype(BF16)
    wanted = 96 * s + 12 * (lane // 16) + 6 * (lane % 16 // 8) + lane % 8
    hit = jnp.logical_and(channel == wanted, lane % 8 < 6)
    gained = (n.in_t_[...].astype(F32) * gain).astype(BF16)
    n.pick_in_[...] = dot_cols(zero_one(hit), gained).astype(BF16)

    links.near.receive()
    spread(jnp.where(s > 0, n.near_r_[0][0:1], 0.0), n.own_code_, 0)
    spread(n.codes_s_[0][0:1], n.own_code_, 1)
    spread(jnp.where(s < SEQ - 1, n.near_r_[1][0:1], 0.0), n.own_code_, 2)
    for parity in range(2):
        near = pick_taps(n.own_code_, parity, 80, 64 * s)
        steps = [zero_one(near[8 + step : 72 + step] == lane_code) for step in (-4, 0, 4)]
        value = dot(jnp.concatenate(steps, axis=0), n.stem_w_[...]).astype(BF16)
        for step in range(3):
            n.own_emb_[64 * parity : 64 * parity + 64, 768 * step : 768 * step + 768] = value[
                64 * step : 64 * step + 64
            ]
    center = n.own_emb_[:, 768:1536].astype(F32)
    tower = center + jax.nn.gelu(dot(n.own_emb_[...], n.conv_w_[...]))
    n.tower_[...] = tower.astype(BF16).astype(F32)

    zf = lax.rem(s, 4) // 2
    links.far.receive()
    summed = n.far_r_[0].astype(F32)
    for j in range(4):
        summed = summed + n.rows_r_[j, zf].astype(F32)
    summed = summed.astype(BF16)
    n.pair_s_[0] = summed
    n.mn_s_[0, zf] = summed
    links.pair.start()

    straight = second_hop("pd")
    mean = jnp.sum(straight * n.pooled_[here, :].astype(F32), axis=-1, keepdims=True) / 1536.0
    d_pooled = 0.5 * (factor * straight - cube * mean * behind[:64] + behind[64:])
    links.blk.receive()
    even = n.blk_r_[0].astype(F32)
    odd = n.own_r_[0].astype(F32) - even
    d_tower = jnp.concatenate([even + d_pooled, odd + d_pooled], axis=0)
    d_tower = d_tower.astype(BF16)
    d_conv = (d_tower.astype(F32) * slope).astype(BF16)
    moved = dot(d_conv, n.select_conv_[...]).astype(BF16)
    for j in range(8):
        n.dc_s_[j] = moved[:, 128 * j : 128 * j + 128]
    links.dc.start()
    diagonal = iota((64, 128), 0) == iota((64, 128), 1)
    line = jnp.sum(jnp.where(diagonal, mean, 0.0), axis=0, keepdims=True)
    n.mean_s_[0] = jnp.broadcast_to(line, (8, 128))
    links.mean.start()

    links.pair.receive()
    n.mn_s_[0, 1 - zf] = n.pair_r_[0]
    links.mn.start()

    hots = one_hots(b)
    d_stem = jnp.zeros((128, 768), F32)
    for step in range(3):
        d_emb = dot_cols(d_conv, n.conv_w_[768 * step : 768 * step + 768, :])
        if step == 1:
            d_emb = d_emb + d_tower.astype(F32)
        hot = jnp.concatenate([hots[step], hots[3 + step]], axis=0)
        d_stem = d_stem + dot_rows(hot, d_emb.astype(BF16))
    moved = dot(d_stem[:64].astype(BF16), n.select_conv_[...]).astype(BF16)
    for j in range(8):
        n.ds_s_[j] = moved[:, 128 * j : 128 * j + 128]
    links.ds.start()
    links.feat.start()

    own = jnp.concatenate([summed[:, 448:], jnp.zeros((48, 64), BF16)], axis=1)
    wide = dot(own, n.o_w_[...])
    links.side.receive()
    sides = total(n.side_r_, 8).astype(BF16)
    sides = [dot_cols(sides[:, 128 * half : 128 * half + 128], pick) for half in range(2)]
    wide = (wide + jnp.concatenate(sides, axis=1)).astype(BF16)
    groups = iota((64, 48), 0)
    groups = jnp.where(groups % 8 < 6, 6 * (groups // 8) + groups % 8, -1)
    wide = dot(zero_one(iota((64, 48), 1) == groups), wide)
    n.up_s_[:, 0:8, :] = wide[:, :768].reshape(8, 8, 768).astype(BF16)
    n.up_s_[:, 8:16, :] = wide[:, 768:].reshape(8, 8, 768).astype(BF16)
    links.up.start()

    for half in range(2):
        wide = slice(768 * half, 768 * half + 768)
        part = dot_rows(pick, n.up_w_[wide, :]).astype(BF16)
        n.slices_[:, 256 + 128 * half : 384 + 128 * half] = dot_cols(low(), part).astype(BF16)
    n.conv_acc_[...] = jnp.zeros((128, 2304), F32)
    links.dc.receive()

    def conv_grads(t):
        pair = pl.ds(2 * t, 2)
        left = n.dc_r_[pair].reshape(256, 128)
        n.conv_acc_[...] += dot_rows(left, n.emb_[pair].reshape(256, 2304))

    loop(4, conv_grads)
    links.ds.receive()
    same = zero_one(iota((512, 128), 0) % 64 == iota((512, 128), 1))
    stem = dot_rows(n.ds_r_[...].reshape(512, 128), same)
    n.conv_c_s_[:, :, 0:8, :] = n.conv_acc_[:, :1280].reshape(8, 2, 8, 1280).astype(BF16)
    rest = jnp.concatenate([n.conv_acc_[:, 1280:], stem, jnp.zeros((128, 128), F32)], axis=1)
    n.conv_c_s_[:, :, 8:16, :] = rest.reshape(8, 2, 8, 1280).astype(BF16)
    links.conv_c.start()

    links.mean.receive()

    def remainder(j):
        rows = rows_of(j, 64)
        mean = jnp.sum(jnp.where(diagonal, n.mean_r_[j][0:1], 0.0), axis=1, keepdims=True)
        factor = n.factor_[rows, 0:1]
        part = factor * factor * factor * mean * n.slices_[rows, :256].astype(F32)
        n.rest_[rows, :] = (n.slices_[rows, 256:].astype(F32) - part).astype(BF16)

    loop(8, remainder)
    n.down_c_s_[...] = dot_rows(n.rest_[...], n.pooled_[...]).astype(BF16).reshape(8, 2, 16, 768)
    links.down_c.start()

    core_sum("conv")
    links.mn.receive()
    links.full.start()
    core_sum("down")

    links.full.receive()

    def assemble(q):
        near = pl.ds(pl.multiple_of(96 * q + 48 * h, 16), 48)
        far = pl.ds(pl.multiple_of(96 * q + 48 * (1 - h), 16), 48)
        n.summed_[near, :] = n.mn_r_[q // 2, lax.rem(q, 2)]
        n.summed_[far, :] = n.full_r_[0, q // 2, lax.rem(q, 2)]

    loop(8, assemble)
    first = dot_cols(n.pick_in_[...], n.summed_[:, :512])
    n.first_s_[...] = first.astype(BF16).reshape(8, 16, 768)
    links.first.start()
    inner = dot(n.pick_down_[...], n.summed_[:, :512])[:96]
    rows = pl.ds(pl.multiple_of(96 * s, 16), 96)
    part = jnp.sum(inner * n.in_w_[rows, :].astype(F32), axis=1, keepdims=True)
    diagonal = iota((96, 128), 0) == iota((96, 128), 1)
    line = jnp.sum(jnp.where(diagonal, part, 0.0), axis=0, keepdims=True)
    n.gain_s_[0] = jnp.broadcast_to(line, (8, 128))
    links.gain.start()
    inner = inner * gain_here
    n.g_q[...] = inner[:, :128]
    n.g_k[...] = inner[:, 128:256]
    n.g_v[...] = inner[:, 256:448]
    n.g_o[...] = dot(n.up_w_[rows, :], n.summed_[:, 384:])[:, 64:]

    links.feat.receive()
    lowered = n.feat_r_[0].astype(F32)
    features = n.tower_[...] + jnp.concatenate([lowered, lowered], axis=0)
    n.features[...] = dot_rows(order, features.astype(BF16)).astype(BF16)
    links.up.receive()
    up = total(n.up_r_, 8)
    n.g_up[:, :768] = up[0:6]
    n.g_up[:, 768:] = up[8:14]
    links.conv.receive()
    conv = total(n.conv_r_, 8)
    n.g_conv[0] = conv[0:6, :768]
    n.g_conv[1] = jnp.concatenate([conv[0:6, 768:], conv[8:14, :256]], axis=1)
    n.g_conv[2] = conv[8:14, 256:1024]
    stem = conv[8:16, 1024:1152].astype(BF16)
    for code in range(4):
        taps = iota((128, 15), 0) == 4 * iota((128, 15), 1) + code
        n.g_stem[:, code, :] = dot(stem, zero_one(taps))[:6]
    links.down.receive()
    links.first.receive()
    down = total(n.down_r_, 8) + total(n.first_r_, 8)
    n.g_down[0:6, :] = down[0:6]
    n.g_down[6:12, :] = down[8:14]
    links.gain.receive()
    gains = total(n.gain_r_, 8)
    high = gains.astype(BF16)
    fine = (gains - high.astype(F32)).astype(BF16)
    shift = zero_one(jnp.logical_and(row == column + 12 * b, column < 12))
    n.g_gain[...] = (dot(high, shift) + dot(fine, shift))[0:1]
    for link in vars(links).values():
        link.drain()


def finish_body(*refs):
    number = len(OUTPUTS)
    for source, target in zip(refs[:number], refs[number:]):
        target[...] = source[...]


def per_device(
    base_codes,
    stem_weight,
    conv_weight,
    down_weight,
    norm_gain,
    query_weight,
    key_weight,
    value_weight,
    output_weight,
    up_weight,
    cotangent,
):
    vmem, anywhere = pl.BlockSpec(memory_space=pltpu.VMEM), pl.BlockSpec(memory_space=pl.ANY)
    semaphores = [pltpu.SemaphoreType.DMA((7,))] + [pltpu.SemaphoreType.DMA((2,))] * 2
    shapes = {name: x[0] for name, x in SCRATCH.items()}
    for name, pattern in LINKS.items():
        semaphores += [
            pltpu.SemaphoreType.DMA((pattern.count,)),
            pltpu.SemaphoreType.DMA((shapes[name + "_r"][0],)),
        ]
    out_shape = [jax.ShapeDtypeStruct(shape, dtype) for shape, dtype in OUTPUTS.values()]
    results = pl.pallas_call(
        kernel_body,
        out_shape=out_shape,
        in_specs=[vmem] * 4 + [anywhere] * 7,
        out_specs=[vmem] * len(OUTPUTS),
        scratch_shapes=[pltpu.VMEM(shape, dtype) for shape, dtype in SCRATCH.values()] + semaphores,
        compiler_params=pltpu.CompilerParams(
            collective_id=0, has_side_effects=True, vmem_limit_bytes=60 * 1024 * 1024
        ),
        name="step",
    )(
        base_codes,
        cotangent[0],
        norm_gain,
        stem_weight,
        conv_weight.reshape(2304, 768),
        down_weight,
        query_weight,
        key_weight,
        value_weight.T,
        output_weight,
        up_weight,
    )
    features, g_stem, g_conv, g_down, g_gain, g_up, g_q, g_k, g_v, g_o = pl.pallas_call(
        finish_body,
        out_shape=out_shape,
        in_specs=[vmem] * len(OUTPUTS),
        out_specs=[vmem] * len(OUTPUTS),
        name="finish",
    )(*results)
    return (
        features[None],
        g_stem.transpose(2, 1, 0),
        g_conv.transpose(0, 2, 1),
        g_down.T,
        g_gain[0, :12],
        g_up.T,
        g_q,
        g_k,
        g_v,
        g_o,
    )


def solution(mesh):
    placed = (
        P("batch", "seq"),
        P(),
        P(),
        P(),
        P(),
        P(None, "batch"),
        P(None, "batch"),
        P(None, "batch"),
        P("batch", None),
        P(),
        P("batch", "seq", None),
    )
    return jax.shard_map(
        per_device,
        mesh=mesh,
        in_specs=placed,
        out_specs=(
            P("batch", "seq", None),
            P(None, None, ("seq", "batch")),
            P(None, None, ("seq", "batch")),
            P(None, ("seq", "batch")),
            P(("seq", "batch")),
            P(None, ("seq", "batch")),
            P("seq", "batch"),
            P("seq", "batch"),
            P("seq", "batch"),
            P("seq", "batch"),
        ),
        check_vma=False,
    )
```

```python
import functools
import math

import jax
import jax.numpy as jnp
from jax import lax
from jax.experimental import pallas as pl
from jax.experimental.pallas import tpu as pltpu
from jax.sharding import PartitionSpec as P

EPSILON = 1e-06
MESH = pl.DeviceIdType.MESH
F32 = jnp.float32
BF16 = jnp.bfloat16
SEQ = 16
BATCH = 8


class OverBatch:
    count = BATCH

    def dst(self, i, s, b):
        j = lax.rem(b + i, BATCH)
        return j, s, j, b

    def src(self, i, s, b):
        j = lax.rem(b + BATCH - i, BATCH)
        return j, s, j


class Share:
    count = BATCH

    def dst(self, i, s, b):
        return 0, s, lax.rem(b + i, BATCH), b

    def src(self, i, s, b):
        j = lax.rem(b + BATCH - i, BATCH)
        return j, s, j


class OverQuads:
    count = SEQ // 2

    def dst(self, i, s, b):
        j = lax.rem(s // 2 + i, SEQ // 2)
        return j, 2 * j + lax.rem(s, 2), b, s // 2

    def src(self, i, s, b):
        j = lax.rem(s // 2 + SEQ // 2 - i, SEQ // 2)
        return j, 2 * j + lax.rem(s, 2), b


class OverY:
    count = 4

    def dst(self, i, s, b):
        to = lax.rem(s // 4 + i, 4)
        return to, 4 * to + lax.rem(s, 4), b, s // 4

    def src(self, i, s, b):
        at = lax.rem(s // 4 + 4 - i, 4)
        return at, 4 * at + lax.rem(s, 4), b


class ShareY(OverY):
    def dst(self, i, s, b):
        to = lax.rem(s // 4 + i, 4)
        return 0, 4 * to + lax.rem(s, 4), b, s // 4


class FarZ:
    count = 1

    def dst(self, i, s, b):
        mine = lax.rem(s, 4) // 2
        return 1 - mine, s + 2 - 4 * mine, b, 0

    def src(self, i, s, b):
        return 0, s + 2 - 4 * (lax.rem(s, 4) // 2), b


class ShareFarZ(FarZ):
    def dst(self, i, s, b):
        return 0, s + 2 - 4 * (lax.rem(s, 4) // 2), b, 0


class Core:
    count = 1

    def dst(self, i, s, b):
        other = 1 - lax.rem(s, 2)
        return other, s - lax.rem(s, 2) + other, b, 0

    def src(self, i, s, b):
        return 0, s + 1 - 2 * lax.rem(s, 2), b


class XBlocks:
    count = 8

    def dst(self, i, s, b):
        z, x = b // 4, lax.rem(b, 4)
        to, side = lax.rem(x + i // 2, 4), lax.rem(i, 2)
        return 4 * side + to, s, 4 * z + to, 2 * x + side

    def src(self, i, s, b):
        z, x = b // 4, lax.rem(b, 4)
        at, side = lax.rem(x + 4 - i // 2, 4), lax.rem(i, 2)
        return 2 * at + side, s, 4 * z + at


class ZBlocks:
    count = 4

    def dst(self, i, s, b):
        other = 1 - b // 4
        return 4 * other + i, s, 4 * other + lax.rem(b, 4), i

    def src(self, i, s, b):
        return i, s, 4 * (1 - b // 4) + lax.rem(b, 4)


class ZOne:
    count = 1

    def dst(self, i, s, b):
        return 0, s, 4 * (1 - b // 4) + lax.rem(b, 4), 0

    def src(self, i, s, b):
        return 0, s, 4 * (1 - b // 4) + lax.rem(b, 4)


class XOne:
    count = 4

    def dst(self, i, s, b):
        z, x = b // 4, lax.rem(b, 4)
        to = lax.rem(x + i, 4)
        return to, s, 4 * z + to, x

    def src(self, i, s, b):
        z, x = b // 4, lax.rem(b, 4)
        at = lax.rem(x + 4 - i, 4)
        return at, s, 4 * z + at


class Codes:
    count = 2 * BATCH

    def dst(self, i, s, b):
        return 0, 2 * b + lax.rem(i, 2), lax.rem(b + i // 2, BATCH), s

    def src(self, i, s, b):
        return i, i, s // 2


class Neighbours:
    count = 2

    def dst(self, i, s, b):
        target = s + 1 - 2 * i
        inside = jnp.logical_and(target >= 0, target < SEQ)
        return 0, jnp.where(inside, target, s), b, i

    def src(self, i, s, b):
        source = s - 1 + 2 * i
        inside = jnp.logical_and(source >= 0, source < SEQ)
        return i, jnp.where(inside, source, s), b


class ToBlock:
    count = 1

    def dst(self, i, s, b):
        return 0, 2 * b + s // BATCH, lax.rem(s, BATCH), 0

    def src(self, i, s, b):
        return 0, BATCH * lax.rem(s, 2) + b, s // 2


class ToOwner:
    count = 1

    def dst(self, i, s, b):
        return 0, BATCH * lax.rem(s, 2) + b, s // 2, 0

    def src(self, i, s, b):
        return 0, 2 * b + s // BATCH, lax.rem(s, BATCH)


class Link:
    def __init__(self, pattern, source, result, sends, receives, s, b):
        self.pattern, self.source, self.result = pattern, source, result
        self.sends, self.receives, self.s, self.b = sends, receives, s, b

    def copy(self, i):
        piece, target_s, target_b, slot = self.pattern.dst(i, self.s, self.b)
        away = jnp.logical_or(target_s != self.s, target_b != self.b)
        return away, pltpu.make_async_remote_copy(
            src_ref=self.source(piece),
            dst_ref=self.result.at[slot],
            send_sem=self.sends.at[i],
            recv_sem=self.receives.at[slot],
            device_id=(target_s, target_b),
            device_id_type=MESH,
        )

    def keep_one(self, i):
        piece, target_s, target_b, slot = self.pattern.dst(i, self.s, self.b)
        home = jnp.logical_and(target_s == self.s, target_b == self.b)

        @pl.when(home)
        def _():
            self.result[slot] = self.source(piece)[...]

    def each(self, action):
        loop(self.pattern.count, action)

    def start_one(self, i):
        away, copy = self.copy(i)
        pl.when(away)(copy.start)

    def keep(self):
        self.each(self.keep_one)

    def start(self):
        self.each(self.start_one)
        self.keep()

    def receive(self):
        def wait(i):
            slot, other_s, other_b = self.pattern.src(i, self.s, self.b)
            away = jnp.logical_or(other_s != self.s, other_b != self.b)
            copy = pltpu.make_async_remote_copy(
                src_ref=self.result.at[slot],
                dst_ref=self.result.at[slot],
                send_sem=self.sends.at[i],
                recv_sem=self.receives.at[slot],
                device_id=(other_s, other_b),
                device_id_type=MESH,
            )
            pl.when(away)(copy.wait_recv)

        self.each(wait)

    def drain(self):
        def wait(i):
            away, copy = self.copy(i)
            pl.when(away)(copy.wait_send)

        self.each(wait)


def dot(left, right):
    return jnp.dot(left, right, preferred_element_type=F32)


def dot_rows(left, right):
    return lax.dot_general(left, right, (((0,), (0,)), ((), ())), preferred_element_type=F32)


def dot_cols(left, right):
    return lax.dot_general(left, right, (((1,), (1,)), ((), ())), preferred_element_type=F32)


def iota(shape, dim):
    return lax.broadcasted_iota(jnp.int32, shape, dim)


def zero_one(mask):
    return jnp.where(mask, 1.0, 0.0).astype(BF16)


def gelu_grad(x):
    inner = math.sqrt(2.0 / math.pi) * (x + 0.044715 * x * x * x)
    t = jnp.tanh(inner)
    slope = math.sqrt(2.0 / math.pi) * (1.0 + 3 * 0.044715 * x * x)
    return 0.5 * (1.0 + t) + 0.5 * x * (1.0 - t * t) * slope


def total(ref, count):
    value = ref[0].astype(F32)
    for j in range(1, count):
        value = value + ref[j].astype(F32)
    return value


def loop(count, step):
    def body(i, carry):
        step(i)
        return carry

    lax.fori_loop(0, count, body, 0)


def rows_of(i, size):
    return pl.ds(pl.multiple_of(i * size, size), size)


INPUTS = dict(codes=0, cot=0, gain=0, stem=0, conv_h=0, down_h=0, q_h=0, k_h=0, v_h=0, o_h=0, up_h=0)
OUTPUTS = dict(
    features=((128, 768), BF16),
    g_stem=((6, 4, 15), F32),
    g_conv=((3, 6, 768), F32),
    g_down=((12, 768), F32),
    g_gain=((1, 128), F32),
    g_up=((6, 1536), F32),
    g_q=((96, 128), F32),
    g_k=((96, 128), F32),
    g_v=((96, 192), F32),
    g_o=((96, 192), F32),
)
SCRATCH = dict(
    conv_w=((2304, 768), BF16),
    down_w=((768, 1536), BF16),
    in_w=((1536, 512), BF16),
    in_t=((512, 1536), BF16),
    o_w=((256, 1536), BF16),
    up_w=((1536, 768), BF16),
    stem_f=((64, 768), F32),
    stem_w=((128, 768), BF16),
    select_conv=((768, 1024), BF16),
    select_down=((768, 1024), BF16),
    codes_s=((1, 8, 128), F32),
    codes_r=((16, 8, 128), F32),
    near_r=((2, 8, 128), F32),
    blk_s=((1, 64, 768), BF16),
    blk_r=((1, 64, 768), BF16),
    own_s=((1, 64, 768), BF16),
    own_r=((1, 64, 768), BF16),
    low_r=((8, 64, 768), BF16),
    code=((2, 640, 128), F32),
    picked=((2, 528, 128), F32),
    emb=((8, 128, 2304), BF16),
    conv=((128, 768), F32),
    tower=((128, 768), F32),
    own_code=((2, 192, 128), F32),
    own_emb=((128, 2304), BF16),
    pooled=((512, 768), BF16),
    lifted=((512, 1536), BF16),
    factor=((512, 128), F32),
    qkv=((512, 512), BF16),
    kv_far=((512, 384), BF16),
    d_att=((512, 256), BF16),
    att=((512, 256), BF16),
    dqkv=((512, 512), BF16),
    dkv_own=((512, 384), F32),
    dkv_far=((512, 384), F32),
    dkv_s=((512, 384), BF16),
    dkv_r=((512, 384), BF16),
    conv_acc=((128, 2304), F32),
    w_up=((256, 768), BF16),
    w_down=((512, 768), BF16),
    pick_in=((128, 512), BF16),
    pick_down=((128, 768), BF16),
    lpA_s=((8, 64, 384), BF16),
    lpA_r=((8, 64, 384), BF16),
    lpB_s=((8, 64, 384), BF16),
    lpB_r=((4, 64, 384), BF16),
    lpC_s=((1, 64, 384), BF16),
    lpC_r=((1, 64, 384), BF16),
    lpD_s=((4, 64, 384), BF16),
    lpD_r=((4, 64, 384), BF16),
    pdA_s=((8, 64, 384), BF16),
    pdA_r=((8, 64, 384), BF16),
    pdB_s=((8, 64, 384), BF16),
    pdB_r=((4, 64, 384), BF16),
    pdC_s=((1, 64, 384), BF16),
    pdC_r=((1, 64, 384), BF16),
    pdD_s=((4, 64, 384), BF16),
    pdD_r=((4, 64, 384), BF16),
    feat_s=((1, 64, 768), BF16),
    feat_r=((1, 64, 768), BF16),
    mean_s=((1, 8, 128), F32),
    mean_r=((8, 8, 128), F32),
    gain_s=((1, 8, 128), F32),
    gain_r=((8, 8, 128), F32),
    dc_s=((8, 128, 128), BF16),
    dc_r=((8, 128, 128), BF16),
    ds_s=((8, 64, 128), BF16),
    ds_r=((8, 64, 128), BF16),
    up_s=((8, 16, 768), BF16),
    up_r=((8, 16, 768), BF16),
    first_s=((8, 16, 768), BF16),
    first_r=((8, 16, 768), BF16),
    rows_c_s=((8, 2, 48, 640), BF16),
    rows_c_r=((1, 8, 48, 640), BF16),
    rows_s=((8, 48, 640), BF16),
    rows_r=((4, 2, 48, 640), BF16),
    far_s=((2, 48, 640), BF16),
    far_r=((1, 48, 640), BF16),
    side_c_s=((8, 2, 48, 256), BF16),
    side_c_r=((1, 8, 48, 256), BF16),
    side_s=((8, 48, 256), BF16),
    side_r=((8, 48, 256), BF16),
    pair_s=((1, 48, 640), BF16),
    pair_r=((1, 48, 640), BF16),
    mn_s=((1, 2, 48, 640), BF16),
    mn_r=((4, 2, 48, 640), BF16),
    full_r=((1, 4, 2, 48, 640), BF16),
    summed=((768, 640), BF16),
    slices=((512, 512), BF16),
    rest=((512, 256), BF16),
    down_c_s=((8, 2, 16, 768), BF16),
    down_c_r=((1, 8, 16, 768), BF16),
    down_s=((8, 16, 768), BF16),
    down_r=((8, 16, 768), BF16),
    conv_c_s=((8, 2, 16, 1280), BF16),
    conv_c_r=((1, 8, 16, 1280), BF16),
    conv_s=((8, 16, 1280), BF16),
    conv_r=((8, 16, 1280), BF16),
)
LINKS = dict(
    codes=Codes(),
    near=Neighbours(),
    own=ToBlock(),
    blk=ToBlock(),
    low=Share(),
    lpA=XBlocks(),
    lpB=ZBlocks(),
    lpC=ZOne(),
    lpD=XOne(),
    pdA=XBlocks(),
    pdB=ZBlocks(),
    pdC=ZOne(),
    pdD=XOne(),
    feat=ToOwner(),
    mean=Share(),
    gain=Share(),
    dc=OverBatch(),
    ds=OverBatch(),
    up=OverBatch(),
    first=OverBatch(),
    rows_c=Core(),
    rows=OverY(),
    far=FarZ(),
    pair=ShareFarZ(),
    side_c=Core(),
    side=OverQuads(),
    mn=ShareY(),
    full=Core(),
    down_c=Core(),
    down=OverQuads(),
    conv_c=Core(),
    conv=OverQuads(),
)


FORWARDED = dict(near="codes_s", low="own_r", full="mn_r")


class Namespace:
    pass


def kernel_body(*refs):
    names = list(INPUTS) + list(OUTPUTS) + [x + "_" for x in SCRATCH]
    n = Namespace()
    for name, ref in zip(names, refs):
        setattr(n, name, ref)
    semaphores = refs[len(names) :]
    weight_sems, swap_send, swap_recv = semaphores[:3]
    s, b = lax.axis_index("seq"), lax.axis_index("batch")
    h = lax.rem(s, 2)
    z = b // 4
    peer = (s + 1 - 2 * h, b)
    links = Namespace()
    for k, (name, pattern) in enumerate(LINKS.items()):
        sent = getattr(n, FORWARDED.get(name, name + "_s") + "_")
        if name == "full":
            source = lambda piece, sent=sent: sent
        elif name == "rows":
            source = lambda piece, sent=sent: sent.at[pl.ds(2 * piece, 2)]
        elif name.endswith("_c"):
            source = lambda piece, sent=sent: sent.at[:, piece]
        else:
            source = lambda piece, sent=sent: sent.at[piece]
        result = getattr(n, name + "_r_")
        link = Link(pattern, source, result, semaphores[3 + 2 * k], semaphores[4 + 2 * k], s, b)
        setattr(links, name, link)

    barrier = pltpu.get_barrier_semaphore()
    for link in (links.codes, links.low, links.side, links.rows_c, links.feat, links.near):
        pattern = link.pattern

        def greet(i, pattern=pattern):
            _, other_s, other_b = pattern.src(i, s, b)

            @pl.when(jnp.logical_or(other_s != s, other_b != b))
            def _():
                pl.semaphore_signal(
                    barrier, inc=1, device_id=(other_s, other_b), device_id_type=MESH
                )

        loop(pattern.count, greet)
    own_window = (b == s // 2).astype(jnp.int32)
    own_block = own_window * (s == BATCH * h + b).astype(jnp.int32)
    ends = (s == 0).astype(jnp.int32) + (s == SEQ - 1).astype(jnp.int32)
    expected = 16 + 7 + 7 + 1 + 1 + 2 - own_window - own_block - ends

    weights = [
        pltpu.make_async_copy(source, target, weight_sems.at[k])
        for k, (source, target) in enumerate(
            [
                (n.q_h, n.in_w_.at[:, pl.ds(0, 128)]),
                (n.k_h, n.in_w_.at[:, pl.ds(128, 128)]),
                (n.v_h, n.in_t_.at[pl.ds(256, 192)]),
                (n.o_h, n.o_w_.at[pl.ds(0, 192)]),
                (n.conv_h, n.conv_w_),
                (n.down_h, n.down_w_),
                (n.up_h, n.up_w_),
            ]
        )
    ]
    for copy in weights:
        copy.start()

    row, column = iota((128, 128), 0), iota((128, 128), 1)
    order = zero_one(column == jnp.where(row < 64, 2 * row, 2 * row - 127))
    codes = jnp.broadcast_to((n.codes[...] + 1).astype(F32), (8, 128)).astype(BF16)
    n.codes_s_[0] = dot_cols(codes, order)
    cot = dot(order, n.cot[...])
    n.own_s_[0] = (cot[:64] + cot[64:]).astype(BF16)
    n.blk_s_[0] = cot[:64].astype(BF16)

    pl.semaphore_wait(barrier, expected)
    links.codes.start()
    links.own.start()
    links.near.each(links.near.start_one)

    def fill(c):
        within = iota((1, 128), 1)
        i, m = lax.rem(within, 8), within // 8
        good = i < 6
        rows = iota((768, 128), 0)
        place = rows_of(c, 128)
        n.select_conv_[:, place] = zero_one(rows == jnp.where(good, 6 * (8 * m + c) + i, -1))
        wanted = 12 * (8 * (m // 2) + c) + 6 * lax.rem(m, 2) + i
        n.select_down_[:, place] = zero_one(rows == jnp.where(good, wanted, -1))

    loop(8, fill)
    for t in range(15):
        n.stem_f_[4 * t : 4 * t + 4, :] = n.stem[t].astype(F32)
    n.stem_f_[60:, :] = jnp.zeros((4, 768), F32)
    n.stem_w_[:64, :] = n.stem_f_[...].astype(BF16)
    n.stem_w_[64:, :] = jnp.zeros((64, 768), BF16)
    for copy in weights[:4]:
        copy.wait()
    n.o_w_[192:, :] = jnp.zeros((64, 1536), BF16)
    n.in_t_[448:, :] = jnp.zeros((64, 1536), BF16)
    eye, eye2 = zero_one(row == column), zero_one(iota((256, 256), 0) == iota((256, 256), 1))
    n.in_t_[:128, :] = dot_cols(eye, n.in_w_[:, :128]).astype(BF16)
    n.in_t_[128:256, :] = dot_cols(eye, n.in_w_[:, 128:256]).astype(BF16)
    n.in_w_[:, 256:] = dot_rows(n.in_t_[256:, :], eye2).astype(BF16)

    links.codes.receive()
    ones = jnp.ones((128, 128), BF16)
    lane_tap = iota((1, 128), 1) // 4
    lane_code = (iota((1, 128), 1) % 4 + 1).astype(F32)

    def spread(line, target, i):
        lines = dot(jnp.where(row == column, line, 0.0).astype(BF16), ones)
        target[0, 64 * i : 64 * i + 64] = lines[:64]
        target[1, 64 * i : 64 * i + 64] = lines[64:]

    def pick_taps(source, parity, count, first):
        picked = jnp.zeros((count, 128), F32)
        for tap in range(15):
            offset = parity + tap - 7
            stream, shift = offset % 2, (offset - offset % 2) // 2
            begin = 56 + shift
            picked = jnp.where(lane_tap == tap, source[stream, begin : begin + count, :], picked)
        where = iota((count, 128), 0) - 8 + first
        inside = jnp.logical_and(where >= 0, where < 1024)
        return jnp.where(inside, picked, 0.0)

    for i in range(10):
        place = BATCH * h + (i - 1)
        inside = jnp.logical_and(place >= 0, place < 16)
        line = n.codes_r_[jnp.clip(place, 0, 15)][0:1]
        spread(jnp.where(inside, line, 0.0), n.code_, i)
    for parity in range(2):
        n.picked_[parity] = pick_taps(n.code_, parity, 528, 512 * h)

    links.own.receive()
    links.low.start()

    def one_hots(j):
        found = []
        for parity in range(2):
            near = n.picked_[parity, pl.ds(pl.multiple_of(64 * j, 64), 80), :]
            for step in (-4, 0, 4):
                found.append(zero_one(near[8 + step : 72 + step] == lane_code))
        return found

    def embed(j):
        value = dot(jnp.concatenate(one_hots(j), axis=0), n.stem_w_[...]).astype(BF16)
        for parity in range(2):
            for step in range(3):
                begin = 64 * (3 * parity + step)
                n.emb_[j, 64 * parity : 64 * parity + 64, 768 * step : 768 * step + 768] = value[
                    begin : begin + 64
                ]

    loop(8, embed)
    for copy in weights[4:]:
        copy.wait()
    gain = n.gain[...].reshape(1, 1536)

    def forward(t):
        four = pl.ds(4 * t, 4)
        here = rows_of(t, 256)
        conv = dot(n.emb_[four].reshape(512, 2304), n.conv_w_[...])
        center = n.emb_[four, :, 768:1536].reshape(512, 768).astype(F32)
        tower = (center + jax.nn.gelu(conv)).astype(BF16)
        halves = tower.astype(F32).reshape(4, 2, 64, 768)
        pooled = (0.5 * (halves[:, 0] + halves[:, 1])).astype(BF16).reshape(256, 768)
        n.pooled_[here, :] = pooled
        lifted = dot(pooled, n.down_w_[...]).astype(BF16)
        n.lifted_[here, :] = lifted
        lifted = lifted.astype(F32)
        factor = lax.rsqrt(jnp.mean(lifted * lifted, axis=-1, keepdims=True) + EPSILON)
        n.factor_[here, :] = jnp.broadcast_to(factor, (256, 128))
        normed = (lifted * factor * gain).astype(BF16)
        n.qkv_[here, :] = dot(normed, n.in_w_[...]).astype(BF16)

    loop(2, forward)
    swap = pltpu.make_async_remote_copy(
        src_ref=n.qkv_.at[:, pl.ds(128, 384)], dst_ref=n.kv_far_,
        send_sem=swap_send.at[0], recv_sem=swap_recv.at[0], device_id=peer, device_id_type=MESH,
    )
    swap.start()
    n.w_up_[...] = dot(n.o_w_[...], n.up_w_[...]).astype(BF16)
    links.low.receive()
    links.blk.start()

    def low():
        return n.low_r_[...].reshape(512, 768)

    n.d_att_[...] = dot_cols(low(), n.w_up_[...]).astype(BF16)
    n.dkv_own_[...] = jnp.zeros((512, 384), F32)
    n.dkv_far_[...] = jnp.zeros((512, 384), F32)
    swap.wait()

    scale = 1.0 / math.sqrt(128)

    def send_pair(name, t, value):
        half = value.astype(BF16)
        getattr(n, name + "A_s_")[pl.ds(2 * t, 2)] = half[:, :384].reshape(2, 64, 384)
        getattr(n, name + "B_s_")[pl.ds(2 * t, 2)] = half[:, 384:].reshape(2, 64, 384)
        for j in (2 * t, 2 * t + 1):
            to, side = lax.rem(j, 4), j // 4
            getattr(links, name + "A").start_one(2 * lax.rem(to - lax.rem(b, 4) + 4, 4) + side)

            @pl.when(side != z)
            def _():
                getattr(links, name + "B").start_one(to)

    def attend(t):
        here = rows_of(t, 256)
        q, da = n.qkv_[here, :128], n.d_att_[here, :]
        blocks = (
            (n.qkv_[:, 128:256], n.qkv_[:, 256:], n.dkv_own_),
            (n.kv_far_[:, :128], n.kv_far_[:, 128:], n.dkv_far_),
        )
        scores = [dot_cols(q, k) * scale for k, _, _ in blocks]
        sums = sum(jnp.sum(jnp.exp(x), axis=1, keepdims=True) for x in scores)
        log_total = jnp.log(sums)
        probs = [jnp.exp(x - log_total) for x in scores]
        dprobs = [dot_cols(da, v) for _, v, _ in blocks]
        inner = sum(jnp.sum(p * d, axis=1, keepdims=True) for p, d in zip(probs, dprobs))
        att = jnp.zeros((256, 256), F32)
        dq = jnp.zeros((256, 128), F32)
        for (k, v, total_ref), p, d in zip(blocks, probs, dprobs):
            ds = (p * (d - inner)).astype(BF16)
            pb = p.astype(BF16)
            att = att + dot(pb, v)
            dq = dq + dot(ds, k)
            total_ref[:, :128] += dot_rows(ds, q) * scale
            total_ref[:, 128:] += dot_rows(pb, da)
        att = att.astype(BF16)
        n.att_[here, :] = att
        n.dqkv_[here, :128] = (dq * scale).astype(BF16)
        part = dot(att, n.w_up_[...])
        send_pair("lp", 2 * t, part[:128])
        send_pair("lp", 2 * t + 1, part[128:])

    loop(2, attend)
    n.dkv_s_[...] = n.dkv_far_[...].astype(BF16)
    swap_back = pltpu.make_async_remote_copy(
        src_ref=n.dkv_s_, dst_ref=n.dkv_r_, send_sem=swap_send.at[1], recv_sem=swap_recv.at[1],
        device_id=peer, device_id_type=MESH,
    )
    swap_back.start()
    gained = (n.in_t_[...].astype(F32) * gain).astype(BF16)
    n.w_down_[...] = dot_cols(gained, n.down_w_[...]).astype(BF16)
    pieces = dot_rows(low(), n.att_[...])[:, :192].astype(BF16)
    n.rows_c_s_[:, :, :, 448:] = pieces.reshape(8, 2, 48, 192)
    scaled = (n.pooled_[...].astype(F32) * n.factor_[:, 0:1]).astype(BF16)
    swap_back.wait()
    n.dqkv_[:, 128:] = (n.dkv_own_[...] + n.dkv_r_[...].astype(F32)).astype(BF16)

    pieces = dot_rows(scaled, n.dqkv_[...])[:, :448].astype(BF16)
    n.rows_c_s_[:, :, :, :448] = pieces.reshape(8, 2, 48, 448)
    links.rows_c.start()

    def back_through_projections(t):
        send_pair("pd", t, dot(n.dqkv_[rows_of(t, 128), :], n.w_down_[...]))

    loop(4, back_through_projections)

    def core_sum(name):
        getattr(links, name + "_c").receive()
        mine = getattr(n, name + "_c_s_")
        far = getattr(n, name + "_c_r_")
        target = getattr(n, name + "_s_")

        def add(j):
            target[j] = (mine[j, h].astype(F32) + far[0, j].astype(F32)).astype(BF16)

        loop(8, add)
        getattr(links, name).start()

    def first_hop(name):
        over_x, over_z = getattr(links, name + "A"), getattr(links, name + "B")
        over_x.keep()
        over_x.receive()
        there = 1 - z
        value = over_x.result[there].astype(F32)
        for j in range(1, 4):
            value = value + over_x.result[2 * j + there].astype(F32)
        getattr(n, name + "C_s_")[0] = value.astype(BF16)
        getattr(links, name + "C").start()
        over_z.receive()
        value = getattr(n, name + "B_s_")[pl.ds(4 * z, 4)].astype(F32)
        value = value + over_z.result[...].astype(F32)
        getattr(n, name + "D_s_")[...] = value.astype(BF16)
        getattr(links, name + "D").start()

    def second_hop(name):
        getattr(links, name + "C").receive()
        left = getattr(links, name + "C").result[0].astype(F32)
        for j in range(4):
            left = left + getattr(links, name + "A").result[2 * j + z].astype(F32)
        getattr(links, name + "D").receive()
        return jnp.concatenate([left, total(getattr(links, name + "D").result, 4)], axis=1)

    pick = n.select_down_[:, rows_of(b, 128)]
    for half in range(2):
        wide = slice(768 * half, 768 * half + 768)
        n.slices_[:, 128 * half : 128 * half + 128] = dot(n.lifted_[:, wide], pick).astype(BF16)
    core_sum("rows")
    n.side_c_s_[...] = dot_rows(low(), n.slices_[:, :256]).astype(BF16).reshape(8, 2, 48, 256)
    links.side_c.start()
    first_hop("lp")
    first_hop("pd")
    core_sum("side")

    here = rows_of(b, 64)
    n.conv_[...] = dot(n.emb_[b], n.conv_w_[...])
    lifted = n.lifted_[here, :]
    factor = n.factor_[here, 0:1]
    cube = factor * factor * factor
    d_updated = dot_cols(n.own_r_[0], n.up_w_[...]).astype(BF16)
    behind = dot_cols(jnp.concatenate([lifted, d_updated], axis=0), n.down_w_[...])
    lowered = dot(lifted, n.up_w_[...])
    slope = gelu_grad(n.conv_[...])
    links.rows.receive()
    n.far_s_[...] = total(n.rows_r_, 4).astype(BF16)
    links.far.start()
    lowered = lowered + second_hop("lp")
    n.feat_s_[0] = lowered.astype(BF16)


    lane, channel = iota((128, 1536), 0), iota((128, 1536), 1)
    wanted = jnp.where(lane < 96, 96 * s + lane, -1)
    hit = channel == wanted
    gain_here = jnp.sum(jnp.where(hit, gain, 0.0), axis=1, keepdims=True)[:96]
    n.pick_down_[...] = dot_cols(zero_one(hit), n.down_w_[...]).astype(BF16)
    wanted = 96 * s + 12 * (lane // 16) + 6 * (lane % 16 // 8) + lane % 8
    hit = jnp.logical_and(channel == wanted, lane % 8 < 6)
    gained = (n.in_t_[...].astype(F32) * gain).astype(BF16)
    n.pick_in_[...] = dot_cols(zero_one(hit), gained).astype(BF16)

    links.near.receive()
    spread(jnp.where(s > 0, n.near_r_[0][0:1], 0.0), n.own_code_, 0)
    spread(n.codes_s_[0][0:1], n.own_code_, 1)
    spread(jnp.where(s < SEQ - 1, n.near_r_[1][0:1], 0.0), n.own_code_, 2)
    for parity in range(2):
        near = pick_taps(n.own_code_, parity, 80, 64 * s)
        steps = [zero_one(near[8 + step : 72 + step] == lane_code) for step in (-4, 0, 4)]
        value = dot(jnp.concatenate(steps, axis=0), n.stem_w_[...]).astype(BF16)
        for step in range(3):
            n.own_emb_[64 * parity : 64 * parity + 64, 768 * step : 768 * step + 768] = value[
                64 * step : 64 * step + 64
            ]
    center = n.own_emb_[:, 768:1536].astype(F32)
    tower = center + jax.nn.gelu(dot(n.own_emb_[...], n.conv_w_[...]))
    n.tower_[...] = tower.astype(BF16).astype(F32)

    zf = lax.rem(s, 4) // 2
    links.far.receive()
    summed = n.far_r_[0].astype(F32)
    for j in range(4):
        summed = summed + n.rows_r_[j, zf].astype(F32)
    summed = summed.astype(BF16)
    n.pair_s_[0] = summed
    n.mn_s_[0, zf] = summed
    links.pair.start()

    straight = second_hop("pd")
    mean = jnp.sum(straight * n.pooled_[here, :].astype(F32), axis=-1, keepdims=True) / 1536.0
    d_pooled = 0.5 * (factor * straight - cube * mean * behind[:64] + behind[64:])
    links.blk.receive()
    even = n.blk_r_[0].astype(F32)
    odd = n.own_r_[0].astype(F32) - even
    d_tower = jnp.concatenate([even + d_pooled, odd + d_pooled], axis=0)
    d_tower = d_tower.astype(BF16)
    d_conv = (d_tower.astype(F32) * slope).astype(BF16)
    moved = dot(d_conv, n.select_conv_[...]).astype(BF16)
    for j in range(8):
        n.dc_s_[j] = moved[:, 128 * j : 128 * j + 128]
    links.dc.start()
    diagonal = iota((64, 128), 0) == iota((64, 128), 1)
    line = jnp.sum(jnp.where(diagonal, mean, 0.0), axis=0, keepdims=True)
    n.mean_s_[0] = jnp.broadcast_to(line, (8, 128))
    links.mean.start()

    links.pair.receive()
    n.mn_s_[0, 1 - zf] = n.pair_r_[0]
    links.mn.start()

    hots = one_hots(b)
    d_stem = jnp.zeros((128, 768), F32)
    for step in range(3):
        d_emb = dot_cols(d_conv, n.conv_w_[768 * step : 768 * step + 768, :])
        if step == 1:
            d_emb = d_emb + d_tower.astype(F32)
        hot = jnp.concatenate([hots[step], hots[3 + step]], axis=0)
        d_stem = d_stem + dot_rows(hot, d_emb.astype(BF16))
    moved = dot(d_stem[:64].astype(BF16), n.select_conv_[...]).astype(BF16)
    for j in range(8):
        n.ds_s_[j] = moved[:, 128 * j : 128 * j + 128]
    links.ds.start()
    links.feat.start()

    own = jnp.concatenate([summed[:, 448:], jnp.zeros((48, 64), BF16)], axis=1)
    wide = dot(own, n.o_w_[...])
    links.side.receive()
    sides = total(n.side_r_, 8).astype(BF16)
    sides = [dot_cols(sides[:, 128 * half : 128 * half + 128], pick) for half in range(2)]
    wide = (wide + jnp.concatenate(sides, axis=1)).astype(BF16)
    groups = iota((64, 48), 0)
    groups = jnp.where(groups % 8 < 6, 6 * (groups // 8) + groups % 8, -1)
    wide = dot(zero_one(iota((64, 48), 1) == groups), wide)
    n.up_s_[:, 0:8, :] = wide[:, :768].reshape(8, 8, 768).astype(BF16)
    n.up_s_[:, 8:16, :] = wide[:, 768:].reshape(8, 8, 768).astype(BF16)
    links.up.start()

    for half in range(2):
        wide = slice(768 * half, 768 * half + 768)
        part = dot_rows(pick, n.up_w_[wide, :]).astype(BF16)
        n.slices_[:, 256 + 128 * half : 384 + 128 * half] = dot_cols(low(), part).astype(BF16)
    n.conv_acc_[...] = jnp.zeros((128, 2304), F32)
    links.dc.receive()

    def conv_grads(t):
        pair = pl.ds(2 * t, 2)
        left = n.dc_r_[pair].reshape(256, 128)
        n.conv_acc_[...] += dot_rows(left, n.emb_[pair].reshape(256, 2304))

    loop(4, conv_grads)
    links.ds.receive()
    same = zero_one(iota((512, 128), 0) % 64 == iota((512, 128), 1))
    stem = dot_rows(n.ds_r_[...].reshape(512, 128), same)
    n.conv_c_s_[:, :, 0:8, :] = n.conv_acc_[:, :1280].reshape(8, 2, 8, 1280).astype(BF16)
    rest = jnp.concatenate([n.conv_acc_[:, 1280:], stem, jnp.zeros((128, 128), F32)], axis=1)
    n.conv_c_s_[:, :, 8:16, :] = rest.reshape(8, 2, 8, 1280).astype(BF16)
    links.conv_c.start()
    links.mn.receive()
    links.full.start()

    links.mean.receive()

    def remainder(j):
        rows = rows_of(j, 64)
        mean = jnp.sum(jnp.where(diagonal, n.mean_r_[j][0:1], 0.0), axis=1, keepdims=True)
        factor = n.factor_[rows, 0:1]
        part = factor * factor * factor * mean * n.slices_[rows, :256].astype(F32)
        n.rest_[rows, :] = (n.slices_[rows, 256:].astype(F32) - part).astype(BF16)

    loop(8, remainder)
    n.down_c_s_[...] = dot_rows(n.rest_[...], n.pooled_[...]).astype(BF16).reshape(8, 2, 16, 768)
    links.down_c.start()

    core_sum("conv")

    links.full.receive()

    def assemble(q):
        near = pl.ds(pl.multiple_of(96 * q + 48 * h, 16), 48)
        far = pl.ds(pl.multiple_of(96 * q + 48 * (1 - h), 16), 48)
        n.summed_[near, :] = n.mn_r_[q // 2, lax.rem(q, 2)]
        n.summed_[far, :] = n.full_r_[0, q // 2, lax.rem(q, 2)]

    loop(8, assemble)
    first = dot_cols(n.pick_in_[...], n.summed_[:, :512])
    n.first_s_[...] = first.astype(BF16).reshape(8, 16, 768)
    links.first.start()
    core_sum("down")
    inner = dot(n.pick_down_[...], n.summed_[:, :512])[:96]
    rows = pl.ds(pl.multiple_of(96 * s, 16), 96)
    part = jnp.sum(inner * n.in_w_[rows, :].astype(F32), axis=1, keepdims=True)
    diagonal = iota((96, 128), 0) == iota((96, 128), 1)
    line = jnp.sum(jnp.where(diagonal, part, 0.0), axis=0, keepdims=True)
    n.gain_s_[0] = jnp.broadcast_to(line, (8, 128))
    links.gain.start()
    inner = inner * gain_here
    n.g_q[...] = inner[:, :128]
    n.g_k[...] = inner[:, 128:256]
    n.g_v[...] = inner[:, 256:448]
    n.g_o[...] = dot(n.up_w_[rows, :], n.summed_[:, 384:])[:, 64:]

    links.feat.receive()
    lowered = n.feat_r_[0].astype(F32)
    features = n.tower_[...] + jnp.concatenate([lowered, lowered], axis=0)
    n.features[...] = dot_rows(order, features.astype(BF16)).astype(BF16)
    links.up.receive()
    up = total(n.up_r_, 8)
    n.g_up[:, :768] = up[0:6]
    n.g_up[:, 768:] = up[8:14]
    links.conv.receive()
    conv = total(n.conv_r_, 8)
    n.g_conv[0] = conv[0:6, :768]
    n.g_conv[1] = jnp.concatenate([conv[0:6, 768:], conv[8:14, :256]], axis=1)
    n.g_conv[2] = conv[8:14, 256:1024]
    stem = conv[8:16, 1024:1152].astype(BF16)
    for code in range(4):
        taps = iota((128, 15), 0) == 4 * iota((128, 15), 1) + code
        n.g_stem[:, code, :] = dot(stem, zero_one(taps))[:6]
    links.down.receive()
    links.first.receive()
    down = total(n.down_r_, 8) + total(n.first_r_, 8)
    n.g_down[0:6, :] = down[0:6]
    n.g_down[6:12, :] = down[8:14]
    links.gain.receive()
    gains = total(n.gain_r_, 8)
    high = gains.astype(BF16)
    fine = (gains - high.astype(F32)).astype(BF16)
    shift = zero_one(jnp.logical_and(row == column + 12 * b, column < 12))
    n.g_gain[...] = (dot(high, shift) + dot(fine, shift))[0:1]
    for link in vars(links).values():
        link.drain()


def finish_body(*refs):
    number = len(OUTPUTS)
    for name, source, target in zip(OUTPUTS, refs[:number], refs[number:]):
        target[...] = source[0, :12] if name == "g_gain" else source[...]


def per_device(
    base_codes,
    stem_weight,
    conv_weight,
    down_weight,
    norm_gain,
    query_weight,
    key_weight,
    value_weight,
    output_weight,
    up_weight,
    cotangent,
):
    vmem, anywhere = pl.BlockSpec(memory_space=pltpu.VMEM), pl.BlockSpec(memory_space=pl.ANY)
    semaphores = [pltpu.SemaphoreType.DMA((7,))] + [pltpu.SemaphoreType.DMA((2,))] * 2
    shapes = {name: x[0] for name, x in SCRATCH.items()}
    for name, pattern in LINKS.items():
        semaphores += [
            pltpu.SemaphoreType.DMA((pattern.count,)),
            pltpu.SemaphoreType.DMA((shapes[name + "_r"][0],)),
        ]
    out_shape = [jax.ShapeDtypeStruct(shape, dtype) for shape, dtype in OUTPUTS.values()]
    results = pl.pallas_call(
        kernel_body,
        out_shape=out_shape,
        in_specs=[vmem] * 4 + [anywhere] * 7,
        out_specs=[vmem] * len(OUTPUTS),
        scratch_shapes=[pltpu.VMEM(shape, dtype) for shape, dtype in SCRATCH.values()] + semaphores,
        compiler_params=pltpu.CompilerParams(
            collective_id=0, has_side_effects=True, vmem_limit_bytes=60 * 1024 * 1024
        ),
        name="step",
    )(
        base_codes,
        cotangent[0],
        norm_gain,
        stem_weight,
        conv_weight.reshape(2304, 768),
        down_weight,
        query_weight,
        key_weight,
        value_weight.T,
        output_weight,
        up_weight,
    )
    features, g_stem, g_conv, g_down, g_gain, g_up, g_q, g_k, g_v, g_o = pl.pallas_call(
        finish_body,
        out_shape=out_shape[:4] + [jax.ShapeDtypeStruct((12,), F32)] + out_shape[5:],
        in_specs=[vmem] * len(OUTPUTS),
        out_specs=[vmem] * len(OUTPUTS),
        name="finish",
    )(*results)
    return (
        features[None],
        g_stem.transpose(2, 1, 0),
        g_conv.transpose(0, 2, 1),
        g_down.T,
        g_gain,
        g_up.T,
        g_q,
        g_k,
        g_v,
        g_o,
    )


def solution(mesh):
    placed = (
        P("batch", "seq"),
        P(),
        P(),
        P(),
        P(),
        P(None, "batch"),
        P(None, "batch"),
        P(None, "batch"),
        P("batch", None),
        P(),
        P("batch", "seq", None),
    )
    return jax.shard_map(
        per_device,
        mesh=mesh,
        in_specs=placed,
        out_specs=(
            P("batch", "seq", None),
            P(None, None, ("seq", "batch")),
            P(None, None, ("seq", "batch")),
            P(None, ("seq", "batch")),
            P(("seq", "batch")),
            P(None, ("seq", "batch")),
            P("seq", "batch"),
            P("seq", "batch"),
            P("seq", "batch"),
            P("seq", "batch"),
        ),
        check_vma=False,
    )
```

```python
import functools
import math

import jax
import jax.numpy as jnp
from jax import lax
from jax.experimental import pallas as pl
from jax.experimental.pallas import tpu as pltpu
from jax.sharding import PartitionSpec as P

EPSILON = 1e-06
MESH = pl.DeviceIdType.MESH
F32 = jnp.float32
BF16 = jnp.bfloat16
SEQ = 16
BATCH = 8


class OverBatch:
    count = BATCH

    def dst(self, i, s, b):
        j = lax.rem(b + i, BATCH)
        return j, s, j, b

    def src(self, i, s, b):
        j = lax.rem(b + BATCH - i, BATCH)
        return j, s, j


class ShareX:
    count = 4

    def dst(self, i, s, b):
        z, x = b // 4, lax.rem(b, 4)
        return 0, s, 4 * z + lax.rem(x + i, 4), x

    def src(self, i, s, b):
        z, x = b // 4, lax.rem(b, 4)
        at = lax.rem(x + 4 - i, 4)
        return at, s, 4 * z + at


class Share:
    count = BATCH

    def dst(self, i, s, b):
        return 0, s, lax.rem(b + i, BATCH), b

    def src(self, i, s, b):
        j = lax.rem(b + BATCH - i, BATCH)
        return j, s, j


class OverQuads:
    count = SEQ // 2

    def dst(self, i, s, b):
        j = lax.rem(s // 2 + i, SEQ // 2)
        return j, 2 * j + lax.rem(s, 2), b, s // 2

    def src(self, i, s, b):
        j = lax.rem(s // 2 + SEQ // 2 - i, SEQ // 2)
        return j, 2 * j + lax.rem(s, 2), b


class OverY:
    count = 4

    def dst(self, i, s, b):
        to = lax.rem(s // 4 + i, 4)
        return to, 4 * to + lax.rem(s, 4), b, s // 4

    def src(self, i, s, b):
        at = lax.rem(s // 4 + 4 - i, 4)
        return at, 4 * at + lax.rem(s, 4), b


class ShareY(OverY):
    def dst(self, i, s, b):
        to = lax.rem(s // 4 + i, 4)
        return 0, 4 * to + lax.rem(s, 4), b, s // 4


class FarZ:
    count = 1

    def dst(self, i, s, b):
        mine = lax.rem(s, 4) // 2
        return 1 - mine, s + 2 - 4 * mine, b, 0

    def src(self, i, s, b):
        return 0, s + 2 - 4 * (lax.rem(s, 4) // 2), b


class ShareFarZ(FarZ):
    def dst(self, i, s, b):
        return 0, s + 2 - 4 * (lax.rem(s, 4) // 2), b, 0


class Core:
    count = 1

    def dst(self, i, s, b):
        other = 1 - lax.rem(s, 2)
        return other, s - lax.rem(s, 2) + other, b, 0

    def src(self, i, s, b):
        return 0, s + 1 - 2 * lax.rem(s, 2), b


class XBlocks:
    count = 8

    def dst(self, i, s, b):
        z, x = b // 4, lax.rem(b, 4)
        to, side = lax.rem(x + i // 2, 4), lax.rem(i, 2)
        return 4 * side + to, s, 4 * z + to, 2 * x + side

    def src(self, i, s, b):
        z, x = b // 4, lax.rem(b, 4)
        at, side = lax.rem(x + 4 - i // 2, 4), lax.rem(i, 2)
        return 2 * at + side, s, 4 * z + at


class ZBlocks:
    count = 4

    def dst(self, i, s, b):
        other = 1 - b // 4
        return 4 * other + i, s, 4 * other + lax.rem(b, 4), i

    def src(self, i, s, b):
        return i, s, 4 * (1 - b // 4) + lax.rem(b, 4)


class ZOne:
    count = 1

    def dst(self, i, s, b):
        return 0, s, 4 * (1 - b // 4) + lax.rem(b, 4), 0

    def src(self, i, s, b):
        return 0, s, 4 * (1 - b // 4) + lax.rem(b, 4)


class XOne:
    count = 4

    def dst(self, i, s, b):
        z, x = b // 4, lax.rem(b, 4)
        to = lax.rem(x + i, 4)
        return to, s, 4 * z + to, x

    def src(self, i, s, b):
        z, x = b // 4, lax.rem(b, 4)
        at = lax.rem(x + 4 - i, 4)
        return at, s, 4 * z + at


class Codes:
    count = 2 * BATCH

    def dst(self, i, s, b):
        return 0, 2 * b + lax.rem(i, 2), lax.rem(b + i // 2, BATCH), s

    def src(self, i, s, b):
        return i, i, s // 2


class Neighbours:
    count = 2

    def dst(self, i, s, b):
        target = s + 1 - 2 * i
        inside = jnp.logical_and(target >= 0, target < SEQ)
        return 0, jnp.where(inside, target, s), b, i

    def src(self, i, s, b):
        source = s - 1 + 2 * i
        inside = jnp.logical_and(source >= 0, source < SEQ)
        return i, jnp.where(inside, source, s), b


class ToBlock:
    count = 1

    def dst(self, i, s, b):
        return 0, 2 * b + s // BATCH, lax.rem(s, BATCH), 0

    def src(self, i, s, b):
        return 0, BATCH * lax.rem(s, 2) + b, s // 2


class ToOwner:
    count = 1

    def dst(self, i, s, b):
        return 0, BATCH * lax.rem(s, 2) + b, s // 2, 0

    def src(self, i, s, b):
        return 0, 2 * b + s // BATCH, lax.rem(s, BATCH)


class Link:
    def __init__(self, pattern, source, result, sends, receives, s, b):
        self.pattern, self.source, self.result = pattern, source, result
        self.sends, self.receives, self.s, self.b = sends, receives, s, b

    def copy(self, i):
        piece, target_s, target_b, slot = self.pattern.dst(i, self.s, self.b)
        away = jnp.logical_or(target_s != self.s, target_b != self.b)
        return away, pltpu.make_async_remote_copy(
            src_ref=self.source(piece),
            dst_ref=self.result.at[slot],
            send_sem=self.sends.at[i],
            recv_sem=self.receives.at[slot],
            device_id=(target_s, target_b),
            device_id_type=MESH,
        )

    def keep_one(self, i):
        piece, target_s, target_b, slot = self.pattern.dst(i, self.s, self.b)
        home = jnp.logical_and(target_s == self.s, target_b == self.b)

        @pl.when(home)
        def _():
            self.result[slot] = self.source(piece)[...]

    def each(self, action):
        loop(self.pattern.count, action)

    def start_one(self, i):
        away, copy = self.copy(i)
        pl.when(away)(copy.start)

    def keep(self):
        self.each(self.keep_one)

    def start(self):
        self.each(self.start_one)
        self.keep()

    def receive(self):
        def wait(i):
            slot, other_s, other_b = self.pattern.src(i, self.s, self.b)
            away = jnp.logical_or(other_s != self.s, other_b != self.b)
            copy = pltpu.make_async_remote_copy(
                src_ref=self.result.at[slot],
                dst_ref=self.result.at[slot],
                send_sem=self.sends.at[i],
                recv_sem=self.receives.at[slot],
                device_id=(other_s, other_b),
                device_id_type=MESH,
            )
            pl.when(away)(copy.wait_recv)

        self.each(wait)

    def drain(self):
        def wait(i):
            away, copy = self.copy(i)
            pl.when(away)(copy.wait_send)

        self.each(wait)


def dot(left, right):
    return jnp.dot(left, right, preferred_element_type=F32)


def dot_rows(left, right):
    return lax.dot_general(left, right, (((0,), (0,)), ((), ())), preferred_element_type=F32)


def dot_cols(left, right):
    return lax.dot_general(left, right, (((1,), (1,)), ((), ())), preferred_element_type=F32)


def iota(shape, dim):
    return lax.broadcasted_iota(jnp.int32, shape, dim)


def zero_one(mask):
    return jnp.where(mask, 1.0, 0.0).astype(BF16)


def gelu_grad(x):
    inner = math.sqrt(2.0 / math.pi) * (x + 0.044715 * x * x * x)
    t = jnp.tanh(inner)
    slope = math.sqrt(2.0 / math.pi) * (1.0 + 3 * 0.044715 * x * x)
    return 0.5 * (1.0 + t) + 0.5 * x * (1.0 - t * t) * slope


def total(ref, count):
    value = ref[0].astype(F32)
    for j in range(1, count):
        value = value + ref[j].astype(F32)
    return value


def loop(count, step):
    def body(i, carry):
        step(i)
        return carry

    lax.fori_loop(0, count, body, 0)


def rows_of(i, size):
    return pl.ds(pl.multiple_of(i * size, size), size)


INPUTS = dict(codes=0, cot=0, gain=0, stem=0, conv_h=0, down_h=0, q_h=0, k_h=0, v_h=0, o_h=0, up_h=0)
OUTPUTS = dict(
    features=((128, 768), BF16),
    g_stem=((6, 4, 15), F32),
    g_conv=((3, 6, 768), F32),
    g_down=((12, 768), F32),
    g_gain=((1, 128), F32),
    g_up=((6, 1536), F32),
    g_q=((96, 128), F32),
    g_k=((96, 128), F32),
    g_v=((96, 192), F32),
    g_o=((96, 192), F32),
)
SCRATCH = dict(
    conv_w=((2304, 768), BF16),
    down_w=((768, 1536), BF16),
    in_w=((1536, 512), BF16),
    in_t=((512, 1536), BF16),
    o_w=((256, 1536), BF16),
    up_w=((1536, 768), BF16),
    stem_f=((64, 768), F32),
    stem_w=((128, 768), BF16),
    select_conv=((768, 1024), BF16),
    select_down=((768, 1024), BF16),
    codes_s=((1, 8, 128), F32),
    codes_r=((16, 8, 128), F32),
    near_r=((2, 8, 128), F32),
    blk_s=((1, 64, 768), BF16),
    blk_r=((1, 64, 768), BF16),
    own_s=((1, 64, 768), BF16),
    own_r=((1, 64, 768), BF16),
    low=((8, 64, 768), BF16),
    low_z_s=((1, 64, 384), BF16),
    low_z_r=((1, 64, 384), BF16),
    low_zx_s=((1, 2, 64, 384), BF16),
    low_zx_r=((4, 2, 64, 384), BF16),
    low_x_s=((1, 64, 384), BF16),
    low_x_r=((4, 64, 384), BF16),
    low_xz_r=((1, 4, 64, 384), BF16),
    code=((2, 640, 128), F32),
    picked=((2, 528, 128), F32),
    emb=((8, 128, 2304), BF16),
    conv=((128, 768), F32),
    tower=((128, 768), F32),
    own_code=((2, 192, 128), F32),
    own_emb=((128, 2304), BF16),
    pooled=((512, 768), BF16),
    lifted=((512, 1536), BF16),
    factor=((512, 128), F32),
    qkv=((512, 512), BF16),
    kv_far=((512, 384), BF16),
    d_att=((512, 256), BF16),
    att=((512, 256), BF16),
    dqkv=((512, 512), BF16),
    dkv_own=((512, 384), F32),
    dkv_far=((512, 384), F32),
    dkv_s=((512, 384), BF16),
    dkv_r=((512, 384), BF16),
    conv_acc=((128, 2304), F32),
    w_up=((256, 768), BF16),
    w_down=((512, 768), BF16),
    pick_in=((128, 512), BF16),
    pick_down=((128, 768), BF16),
    lpA_s=((8, 64, 384), BF16),
    lpA_r=((8, 64, 384), BF16),
    lpB_s=((8, 64, 384), BF16),
    lpB_r=((4, 64, 384), BF16),
    lpC_s=((1, 64, 384), BF16),
    lpC_r=((1, 64, 384), BF16),
    lpD_s=((4, 64, 384), BF16),
    lpD_r=((4, 64, 384), BF16),
    pdA_s=((8, 64, 384), BF16),
    pdA_r=((8, 64, 384), BF16),
    pdB_s=((8, 64, 384), BF16),
    pdB_r=((4, 64, 384), BF16),
    pdC_s=((1, 64, 384), BF16),
    pdC_r=((1, 64, 384), BF16),
    pdD_s=((4, 64, 384), BF16),
    pdD_r=((4, 64, 384), BF16),
    feat_s=((1, 64, 768), BF16),
    feat_r=((1, 64, 768), BF16),
    mean_s=((1, 8, 128), F32),
    mean_r=((8, 8, 128), F32),
    gain_s=((1, 8, 128), F32),
    gain_r=((8, 8, 128), F32),
    dc_s=((8, 128, 128), BF16),
    dc_r=((8, 128, 128), BF16),
    ds_s=((8, 64, 128), BF16),
    ds_r=((8, 64, 128), BF16),
    up_s=((8, 16, 768), BF16),
    up_r=((8, 16, 768), BF16),
    first_s=((8, 16, 768), BF16),
    first_r=((8, 16, 768), BF16),
    rows_c_s=((8, 2, 48, 640), BF16),
    rows_c_r=((1, 8, 48, 640), BF16),
    rows_s=((8, 48, 640), BF16),
    rows_r=((4, 2, 48, 640), BF16),
    far_s=((2, 48, 640), BF16),
    far_r=((1, 48, 640), BF16),
    side_c_s=((8, 2, 48, 256), BF16),
    side_c_r=((1, 8, 48, 256), BF16),
    side_s=((8, 48, 256), BF16),
    side_r=((8, 48, 256), BF16),
    pair_s=((1, 48, 640), BF16),
    pair_r=((1, 48, 640), BF16),
    mn_s=((1, 2, 48, 640), BF16),
    mn_r=((4, 2, 48, 640), BF16),
    full_r=((1, 4, 2, 48, 640), BF16),
    summed=((768, 640), BF16),
    slices=((512, 512), BF16),
    rest=((512, 256), BF16),
    down_c_s=((8, 2, 16, 768), BF16),
    down_c_r=((1, 8, 16, 768), BF16),
    down_s=((8, 16, 768), BF16),
    down_r=((8, 16, 768), BF16),
    conv_c_s=((8, 2, 16, 1280), BF16),
    conv_c_r=((1, 8, 16, 1280), BF16),
    conv_s=((8, 16, 1280), BF16),
    conv_r=((8, 16, 1280), BF16),
)
LINKS = dict(
    codes=Codes(),
    near=Neighbours(),
    own=ToBlock(),
    blk=ToBlock(),
    low_z=ZOne(),
    low_zx=ShareX(),
    low_x=ShareX(),
    low_xz=ZOne(),
    lpA=XBlocks(),
    lpB=ZBlocks(),
    lpC=ZOne(),
    lpD=XOne(),
    pdA=XBlocks(),
    pdB=ZBlocks(),
    pdC=ZOne(),
    pdD=XOne(),
    feat=ToOwner(),
    mean=Share(),
    gain=Share(),
    dc=OverBatch(),
    ds=OverBatch(),
    up=OverBatch(),
    first=OverBatch(),
    rows_c=Core(),
    rows=OverY(),
    far=FarZ(),
    pair=ShareFarZ(),
    side_c=Core(),
    side=OverQuads(),
    mn=ShareY(),
    full=Core(),
    down_c=Core(),
    down=OverQuads(),
    conv_c=Core(),
    conv=OverQuads(),
)


FORWARDED = dict(near="codes_s", low_xz="low_x_r", full="mn_r")


class Namespace:
    pass


def kernel_body(*refs):
    names = list(INPUTS) + list(OUTPUTS) + [x + "_" for x in SCRATCH]
    n = Namespace()
    for name, ref in zip(names, refs):
        setattr(n, name, ref)
    semaphores = refs[len(names) :]
    weight_sems, swap_send, swap_recv = semaphores[:3]
    s, b = lax.axis_index("seq"), lax.axis_index("batch")
    h = lax.rem(s, 2)
    z = b // 4
    peer = (s + 1 - 2 * h, b)
    links = Namespace()
    for k, (name, pattern) in enumerate(LINKS.items()):
        sent = getattr(n, FORWARDED.get(name, name + "_s") + "_")
        if name in ("full", "low_xz"):
            source = lambda piece, sent=sent: sent
        elif name == "rows":
            source = lambda piece, sent=sent: sent.at[pl.ds(2 * piece, 2)]
        elif name.endswith("_c"):
            source = lambda piece, sent=sent: sent.at[:, piece]
        else:
            source = lambda piece, sent=sent: sent.at[piece]
        result = getattr(n, name + "_r_")
        link = Link(pattern, source, result, semaphores[3 + 2 * k], semaphores[4 + 2 * k], s, b)
        setattr(links, name, link)

    barrier = pltpu.get_barrier_semaphore()
    for link in (links.codes, links.mean, links.side, links.rows_c, links.feat, links.near):
        pattern = link.pattern

        def greet(i, pattern=pattern):
            _, other_s, other_b = pattern.src(i, s, b)

            @pl.when(jnp.logical_or(other_s != s, other_b != b))
            def _():
                pl.semaphore_signal(
                    barrier, inc=1, device_id=(other_s, other_b), device_id_type=MESH
                )

        loop(pattern.count, greet)
    own_window = (b == s // 2).astype(jnp.int32)
    own_block = own_window * (s == BATCH * h + b).astype(jnp.int32)
    ends = (s == 0).astype(jnp.int32) + (s == SEQ - 1).astype(jnp.int32)
    expected = 16 + 7 + 7 + 1 + 1 + 2 - own_window - own_block - ends

    weights = [
        pltpu.make_async_copy(source, target, weight_sems.at[k])
        for k, (source, target) in enumerate(
            [
                (n.q_h, n.in_w_.at[:, pl.ds(0, 128)]),
                (n.k_h, n.in_w_.at[:, pl.ds(128, 128)]),
                (n.v_h, n.in_t_.at[pl.ds(256, 192)]),
                (n.o_h, n.o_w_.at[pl.ds(0, 192)]),
                (n.conv_h, n.conv_w_),
                (n.down_h, n.down_w_),
                (n.up_h, n.up_w_),
            ]
        )
    ]
    for copy in weights:
        copy.start()

    row, column = iota((128, 128), 0), iota((128, 128), 1)
    order = zero_one(column == jnp.where(row < 64, 2 * row, 2 * row - 127))
    codes = jnp.broadcast_to((n.codes[...] + 1).astype(F32), (8, 128)).astype(BF16)
    n.codes_s_[0] = dot_cols(codes, order)
    cot = dot(order, n.cot[...])
    n.own_s_[0] = (cot[:64] + cot[64:]).astype(BF16)
    n.blk_s_[0] = cot[:64].astype(BF16)

    pl.semaphore_wait(barrier, expected)
    links.codes.start()
    links.own.start()
    links.near.each(links.near.start_one)

    def fill(c):
        within = iota((1, 128), 1)
        i, m = lax.rem(within, 8), within // 8
        good = i < 6
        rows = iota((768, 128), 0)
        place = rows_of(c, 128)
        n.select_conv_[:, place] = zero_one(rows == jnp.where(good, 6 * (8 * m + c) + i, -1))
        wanted = 12 * (8 * (m // 2) + c) + 6 * lax.rem(m, 2) + i
        n.select_down_[:, place] = zero_one(rows == jnp.where(good, wanted, -1))

    loop(8, fill)
    for t in range(15):
        n.stem_f_[4 * t : 4 * t + 4, :] = n.stem[t].astype(F32)
    n.stem_f_[60:, :] = jnp.zeros((4, 768), F32)
    n.stem_w_[:64, :] = n.stem_f_[...].astype(BF16)
    n.stem_w_[64:, :] = jnp.zeros((64, 768), BF16)
    for copy in weights[:4]:
        copy.wait()
    n.o_w_[192:, :] = jnp.zeros((64, 1536), BF16)
    n.in_t_[448:, :] = jnp.zeros((64, 1536), BF16)
    eye, eye2 = zero_one(row == column), zero_one(iota((256, 256), 0) == iota((256, 256), 1))
    n.in_t_[:128, :] = dot_cols(eye, n.in_w_[:, :128]).astype(BF16)
    n.in_t_[128:256, :] = dot_cols(eye, n.in_w_[:, 128:256]).astype(BF16)
    n.in_w_[:, 256:] = dot_rows(n.in_t_[256:, :], eye2).astype(BF16)

    links.codes.receive()
    ones = jnp.ones((128, 128), BF16)
    lane_tap = iota((1, 128), 1) // 4
    lane_code = (iota((1, 128), 1) % 4 + 1).astype(F32)

    def spread(line, target, i):
        lines = dot(jnp.where(row == column, line, 0.0).astype(BF16), ones)
        target[0, 64 * i : 64 * i + 64] = lines[:64]
        target[1, 64 * i : 64 * i + 64] = lines[64:]

    def pick_taps(source, parity, count, first):
        picked = jnp.zeros((count, 128), F32)
        for tap in range(15):
            offset = parity + tap - 7
            stream, shift = offset % 2, (offset - offset % 2) // 2
            begin = 56 + shift
            picked = jnp.where(lane_tap == tap, source[stream, begin : begin + count, :], picked)
        where = iota((count, 128), 0) - 8 + first
        inside = jnp.logical_and(where >= 0, where < 1024)
        return jnp.where(inside, picked, 0.0)

    for i in range(10):
        place = BATCH * h + (i - 1)
        inside = jnp.logical_and(place >= 0, place < 16)
        line = n.codes_r_[jnp.clip(place, 0, 15)][0:1]
        spread(jnp.where(inside, line, 0.0), n.code_, i)
    for parity in range(2):
        n.picked_[parity] = pick_taps(n.code_, parity, 528, 512 * h)

    links.own.receive()
    n.low_z_s_[0] = n.own_r_[0, :, :384]
    n.low_x_s_[0] = n.own_r_[0, :, 384:]
    links.low_z.start()
    links.low_x.start()

    def one_hots(j):
        found = []
        for parity in range(2):
            near = n.picked_[parity, pl.ds(pl.multiple_of(64 * j, 64), 80), :]
            for step in (-4, 0, 4):
                found.append(zero_one(near[8 + step : 72 + step] == lane_code))
        return found

    def embed(j):
        value = dot(jnp.concatenate(one_hots(j), axis=0), n.stem_w_[...]).astype(BF16)
        for parity in range(2):
            for step in range(3):
                begin = 64 * (3 * parity + step)
                n.emb_[j, 64 * parity : 64 * parity + 64, 768 * step : 768 * step + 768] = value[
                    begin : begin + 64
                ]

    loop(8, embed)
    links.low_x.receive()
    links.low_xz.start()
    links.low_z.receive()
    n.low_zx_s_[0, z] = n.low_z_s_[0]
    n.low_zx_s_[0, 1 - z] = n.low_z_r_[0]
    links.low_zx.start()
    for copy in weights[4:]:
        copy.wait()
    gain = n.gain[...].reshape(1, 1536)

    def forward(t):
        four = pl.ds(4 * t, 4)
        here = rows_of(t, 256)
        conv = dot(n.emb_[four].reshape(512, 2304), n.conv_w_[...])
        center = n.emb_[four, :, 768:1536].reshape(512, 768).astype(F32)
        tower = (center + jax.nn.gelu(conv)).astype(BF16)
        halves = tower.astype(F32).reshape(4, 2, 64, 768)
        pooled = (0.5 * (halves[:, 0] + halves[:, 1])).astype(BF16).reshape(256, 768)
        n.pooled_[here, :] = pooled
        lifted = dot(pooled, n.down_w_[...]).astype(BF16)
        n.lifted_[here, :] = lifted
        lifted = lifted.astype(F32)
        factor = lax.rsqrt(jnp.mean(lifted * lifted, axis=-1, keepdims=True) + EPSILON)
        n.factor_[here, :] = jnp.broadcast_to(factor, (256, 128))
        normed = (lifted * factor * gain).astype(BF16)
        n.qkv_[here, :] = dot(normed, n.in_w_[...]).astype(BF16)

    loop(2, forward)
    swap = pltpu.make_async_remote_copy(
        src_ref=n.qkv_.at[:, pl.ds(128, 384)], dst_ref=n.kv_far_,
        send_sem=swap_send.at[0], recv_sem=swap_recv.at[0], device_id=peer, device_id_type=MESH,
    )
    swap.start()
    n.w_up_[...] = dot(n.o_w_[...], n.up_w_[...]).astype(BF16)
    links.low_zx.receive()
    links.low_xz.receive()
    links.blk.start()

    def gather(x):
        n.low_[x, :, :384] = n.low_zx_r_[x, 0]
        n.low_[4 + x, :, :384] = n.low_zx_r_[x, 1]
        n.low_[4 * z + x, :, 384:] = n.low_x_r_[x]
        n.low_[4 * (1 - z) + x, :, 384:] = n.low_xz_r_[0, x]

    loop(4, gather)

    def low():
        return n.low_[...].reshape(512, 768)

    n.d_att_[...] = dot_cols(low(), n.w_up_[...]).astype(BF16)
    n.dkv_own_[...] = jnp.zeros((512, 384), F32)
    n.dkv_far_[...] = jnp.zeros((512, 384), F32)
    swap.wait()

    scale = 1.0 / math.sqrt(128)

    def send_pair(name, t, value):
        half = value.astype(BF16)
        getattr(n, name + "A_s_")[pl.ds(2 * t, 2)] = half[:, :384].reshape(2, 64, 384)
        getattr(n, name + "B_s_")[pl.ds(2 * t, 2)] = half[:, 384:].reshape(2, 64, 384)
        for j in (2 * t, 2 * t + 1):
            to, side = lax.rem(j, 4), j // 4
            getattr(links, name + "A").start_one(2 * lax.rem(to - lax.rem(b, 4) + 4, 4) + side)

            @pl.when(side != z)
            def _():
                getattr(links, name + "B").start_one(to)

    def attend(t):
        here = rows_of(t, 256)
        q, da = n.qkv_[here, :128], n.d_att_[here, :]
        blocks = (
            (n.qkv_[:, 128:256], n.qkv_[:, 256:], n.dkv_own_),
            (n.kv_far_[:, :128], n.kv_far_[:, 128:], n.dkv_far_),
        )
        scores = [dot_cols(q, k) * scale for k, _, _ in blocks]
        sums = sum(jnp.sum(jnp.exp(x), axis=1, keepdims=True) for x in scores)
        log_total = jnp.log(sums)
        probs = [jnp.exp(x - log_total) for x in scores]
        dprobs = [dot_cols(da, v) for _, v, _ in blocks]
        inner = sum(jnp.sum(p * d, axis=1, keepdims=True) for p, d in zip(probs, dprobs))
        att = jnp.zeros((256, 256), F32)
        dq = jnp.zeros((256, 128), F32)
        for (k, v, total_ref), p, d in zip(blocks, probs, dprobs):
            ds = (p * (d - inner)).astype(BF16)
            pb = p.astype(BF16)
            att = att + dot(pb, v)
            dq = dq + dot(ds, k)
            total_ref[:, :128] += dot_rows(ds, q) * scale
            total_ref[:, 128:] += dot_rows(pb, da)
        att = att.astype(BF16)
        n.att_[here, :] = att
        n.dqkv_[here, :128] = (dq * scale).astype(BF16)
        part = dot(att, n.w_up_[...])
        send_pair("lp", 2 * t, part[:128])
        send_pair("lp", 2 * t + 1, part[128:])

    loop(2, attend)
    n.dkv_s_[...] = n.dkv_far_[...].astype(BF16)
    swap_back = pltpu.make_async_remote_copy(
        src_ref=n.dkv_s_, dst_ref=n.dkv_r_, send_sem=swap_send.at[1], recv_sem=swap_recv.at[1],
        device_id=peer, device_id_type=MESH,
    )
    swap_back.start()
    gained = (n.in_t_[...].astype(F32) * gain).astype(BF16)
    n.w_down_[...] = dot_cols(gained, n.down_w_[...]).astype(BF16)
    pieces = dot_rows(low(), n.att_[...])[:, :192].astype(BF16)
    n.rows_c_s_[:, :, :, 448:] = pieces.reshape(8, 2, 48, 192)
    scaled = (n.pooled_[...].astype(F32) * n.factor_[:, 0:1]).astype(BF16)
    swap_back.wait()
    n.dqkv_[:, 128:] = (n.dkv_own_[...] + n.dkv_r_[...].astype(F32)).astype(BF16)

    pieces = dot_rows(scaled, n.dqkv_[...])[:, :448].astype(BF16)
    n.rows_c_s_[:, :, :, :448] = pieces.reshape(8, 2, 48, 448)
    links.rows_c.start()

    def back_through_projections(t):
        send_pair("pd", t, dot(n.dqkv_[rows_of(t, 128), :], n.w_down_[...]))

    loop(4, back_through_projections)

    def core_sum(name):
        getattr(links, name + "_c").receive()
        mine = getattr(n, name + "_c_s_")
        far = getattr(n, name + "_c_r_")
        target = getattr(n, name + "_s_")

        def add(j):
            target[j] = (mine[j, h].astype(F32) + far[0, j].astype(F32)).astype(BF16)

        loop(8, add)
        getattr(links, name).start()

    def first_hop(name):
        over_x, over_z = getattr(links, name + "A"), getattr(links, name + "B")
        over_x.keep()
        over_x.receive()
        there = 1 - z
        value = over_x.result[there].astype(F32)
        for j in range(1, 4):
            value = value + over_x.result[2 * j + there].astype(F32)
        getattr(n, name + "C_s_")[0] = value.astype(BF16)
        getattr(links, name + "C").start()
        over_z.receive()
        value = getattr(n, name + "B_s_")[pl.ds(4 * z, 4)].astype(F32)
        value = value + over_z.result[...].astype(F32)
        getattr(n, name + "D_s_")[...] = value.astype(BF16)
        getattr(links, name + "D").start()

    def second_hop(name):
        getattr(links, name + "C").receive()
        left = getattr(links, name + "C").result[0].astype(F32)
        for j in range(4):
            left = left + getattr(links, name + "A").result[2 * j + z].astype(F32)
        getattr(links, name + "D").receive()
        return jnp.concatenate([left, total(getattr(links, name + "D").result, 4)], axis=1)

    pick = n.select_down_[:, rows_of(b, 128)]
    for half in range(2):
        wide = slice(768 * half, 768 * half + 768)
        n.slices_[:, 128 * half : 128 * half + 128] = dot(n.lifted_[:, wide], pick).astype(BF16)
    core_sum("rows")
    n.side_c_s_[...] = dot_rows(low(), n.slices_[:, :256]).astype(BF16).reshape(8, 2, 48, 256)
    links.side_c.start()
    first_hop("lp")
    first_hop("pd")
    core_sum("side")

    here = rows_of(b, 64)
    n.conv_[...] = dot(n.emb_[b], n.conv_w_[...])
    lifted = n.lifted_[here, :]
    factor = n.factor_[here, 0:1]
    cube = factor * factor * factor
    d_updated = dot_cols(n.own_r_[0], n.up_w_[...]).astype(BF16)
    behind = dot_cols(jnp.concatenate([lifted, d_updated], axis=0), n.down_w_[...])
    lowered = dot(lifted, n.up_w_[...])
    slope = gelu_grad(n.conv_[...])
    links.rows.receive()
    n.far_s_[...] = total(n.rows_r_, 4).astype(BF16)
    links.far.start()
    lowered = lowered + second_hop("lp")
    n.feat_s_[0] = lowered.astype(BF16)


    lane, channel = iota((128, 1536), 0), iota((128, 1536), 1)
    wanted = jnp.where(lane < 96, 96 * s + lane, -1)
    hit = channel == wanted
    gain_here = jnp.sum(jnp.where(hit, gain, 0.0), axis=1, keepdims=True)[:96]
    n.pick_down_[...] = dot_cols(zero_one(hit), n.down_w_[...]).astype(BF16)
    wanted = 96 * s + 12 * (lane // 16) + 6 * (lane % 16 // 8) + lane % 8
    hit = jnp.logical_and(channel == wanted, lane % 8 < 6)
    gained = (n.in_t_[...].astype(F32) * gain).astype(BF16)
    n.pick_in_[...] = dot_cols(zero_one(hit), gained).astype(BF16)

    links.near.receive()
    spread(jnp.where(s > 0, n.near_r_[0][0:1], 0.0), n.own_code_, 0)
    spread(n.codes_s_[0][0:1], n.own_code_, 1)
    spread(jnp.where(s < SEQ - 1, n.near_r_[1][0:1], 0.0), n.own_code_, 2)
    for parity in range(2):
        near = pick_taps(n.own_code_, parity, 80, 64 * s)
        steps = [zero_one(near[8 + step : 72 + step] == lane_code) for step in (-4, 0, 4)]
        value = dot(jnp.concatenate(steps, axis=0), n.stem_w_[...]).astype(BF16)
        for step in range(3):
            n.own_emb_[64 * parity : 64 * parity + 64, 768 * step : 768 * step + 768] = value[
                64 * step : 64 * step + 64
            ]
    center = n.own_emb_[:, 768:1536].astype(F32)
    tower = center + jax.nn.gelu(dot(n.own_emb_[...], n.conv_w_[...]))
    n.tower_[...] = tower.astype(BF16).astype(F32)

    zf = lax.rem(s, 4) // 2
    links.far.receive()
    summed = n.far_r_[0].astype(F32)
    for j in range(4):
        summed = summed + n.rows_r_[j, zf].astype(F32)
    summed = summed.astype(BF16)
    n.pair_s_[0] = summed
    n.mn_s_[0, zf] = summed
    links.pair.start()

    straight = second_hop("pd")
    mean = jnp.sum(straight * n.pooled_[here, :].astype(F32), axis=-1, keepdims=True) / 1536.0
    d_pooled = 0.5 * (factor * straight - cube * mean * behind[:64] + behind[64:])
    links.blk.receive()
    even = n.blk_r_[0].astype(F32)
    odd = n.own_r_[0].astype(F32) - even
    d_tower = jnp.concatenate([even + d_pooled, odd + d_pooled], axis=0)
    d_tower = d_tower.astype(BF16)
    d_conv = (d_tower.astype(F32) * slope).astype(BF16)
    moved = dot(d_conv, n.select_conv_[...]).astype(BF16)
    for j in range(8):
        n.dc_s_[j] = moved[:, 128 * j : 128 * j + 128]
    links.dc.start()
    diagonal = iota((64, 128), 0) == iota((64, 128), 1)
    line = jnp.sum(jnp.where(diagonal, mean, 0.0), axis=0, keepdims=True)
    n.mean_s_[0] = jnp.broadcast_to(line, (8, 128))
    links.mean.start()

    links.pair.receive()
    n.mn_s_[0, 1 - zf] = n.pair_r_[0]
    links.mn.start()

    hots = one_hots(b)
    d_stem = jnp.zeros((128, 768), F32)
    for step in range(3):
        d_emb = dot_cols(d_conv, n.conv_w_[768 * step : 768 * step + 768, :])
        if step == 1:
            d_emb = d_emb + d_tower.astype(F32)
        hot = jnp.concatenate([hots[step], hots[3 + step]], axis=0)
        d_stem = d_stem + dot_rows(hot, d_emb.astype(BF16))
    moved = dot(d_stem[:64].astype(BF16), n.select_conv_[...]).astype(BF16)
    for j in range(8):
        n.ds_s_[j] = moved[:, 128 * j : 128 * j + 128]
    links.ds.start()
    links.feat.start()

    own = jnp.concatenate([summed[:, 448:], jnp.zeros((48, 64), BF16)], axis=1)
    wide = dot(own, n.o_w_[...])
    links.side.receive()
    sides = total(n.side_r_, 8).astype(BF16)
    sides = [dot_cols(sides[:, 128 * half : 128 * half + 128], pick) for half in range(2)]
    wide = (wide + jnp.concatenate(sides, axis=1)).astype(BF16)
    groups = iota((64, 48), 0)
    groups = jnp.where(groups % 8 < 6, 6 * (groups // 8) + groups % 8, -1)
    wide = dot(zero_one(iota((64, 48), 1) == groups), wide)
    n.up_s_[:, 0:8, :] = wide[:, :768].reshape(8, 8, 768).astype(BF16)
    n.up_s_[:, 8:16, :] = wide[:, 768:].reshape(8, 8, 768).astype(BF16)
    links.up.start()

    for half in range(2):
        wide = slice(768 * half, 768 * half + 768)
        part = dot_rows(pick, n.up_w_[wide, :]).astype(BF16)
        n.slices_[:, 256 + 128 * half : 384 + 128 * half] = dot_cols(low(), part).astype(BF16)
    n.conv_acc_[...] = jnp.zeros((128, 2304), F32)
    links.dc.receive()

    def conv_grads(t):
        pair = pl.ds(2 * t, 2)
        left = n.dc_r_[pair].reshape(256, 128)
        n.conv_acc_[...] += dot_rows(left, n.emb_[pair].reshape(256, 2304))

    loop(4, conv_grads)
    links.ds.receive()
    same = zero_one(iota((512, 128), 0) % 64 == iota((512, 128), 1))
    stem = dot_rows(n.ds_r_[...].reshape(512, 128), same)
    n.conv_c_s_[:, :, 0:8, :] = n.conv_acc_[:, :1280].reshape(8, 2, 8, 1280).astype(BF16)
    rest = jnp.concatenate([n.conv_acc_[:, 1280:], stem, jnp.zeros((128, 128), F32)], axis=1)
    n.conv_c_s_[:, :, 8:16, :] = rest.reshape(8, 2, 8, 1280).astype(BF16)
    links.conv_c.start()
    links.mn.receive()
    links.full.start()

    links.mean.receive()

    def remainder(j):
        rows = rows_of(j, 64)
        mean = jnp.sum(jnp.where(diagonal, n.mean_r_[j][0:1], 0.0), axis=1, keepdims=True)
        factor = n.factor_[rows, 0:1]
        part = factor * factor * factor * mean * n.slices_[rows, :256].astype(F32)
        n.rest_[rows, :] = (n.slices_[rows, 256:].astype(F32) - part).astype(BF16)

    loop(8, remainder)
    n.down_c_s_[...] = dot_rows(n.rest_[...], n.pooled_[...]).astype(BF16).reshape(8, 2, 16, 768)
    links.down_c.start()

    core_sum("conv")

    links.full.receive()

    def assemble(q):
        near = pl.ds(pl.multiple_of(96 * q + 48 * h, 16), 48)
        far = pl.ds(pl.multiple_of(96 * q + 48 * (1 - h), 16), 48)
        n.summed_[near, :] = n.mn_r_[q // 2, lax.rem(q, 2)]
        n.summed_[far, :] = n.full_r_[0, q // 2, lax.rem(q, 2)]

    loop(8, assemble)
    first = dot_cols(n.pick_in_[...], n.summed_[:, :512])
    n.first_s_[...] = first.astype(BF16).reshape(8, 16, 768)
    links.first.start()
    core_sum("down")
    inner = dot(n.pick_down_[...], n.summed_[:, :512])[:96]
    rows = pl.ds(pl.multiple_of(96 * s, 16), 96)
    part = jnp.sum(inner * n.in_w_[rows, :].astype(F32), axis=1, keepdims=True)
    diagonal = iota((96, 128), 0) == iota((96, 128), 1)
    line = jnp.sum(jnp.where(diagonal, part, 0.0), axis=0, keepdims=True)
    n.gain_s_[0] = jnp.broadcast_to(line, (8, 128))
    links.gain.start()
    inner = inner * gain_here
    n.g_q[...] = inner[:, :128]
    n.g_k[...] = inner[:, 128:256]
    n.g_v[...] = inner[:, 256:448]
    n.g_o[...] = dot(n.up_w_[rows, :], n.summed_[:, 384:])[:, 64:]

    links.feat.receive()
    lowered = n.feat_r_[0].astype(F32)
    features = n.tower_[...] + jnp.concatenate([lowered, lowered], axis=0)
    n.features[...] = dot_rows(order, features.astype(BF16)).astype(BF16)
    links.up.receive()
    up = total(n.up_r_, 8)
    n.g_up[:, :768] = up[0:6]
    n.g_up[:, 768:] = up[8:14]
    links.conv.receive()
    conv = total(n.conv_r_, 8)
    n.g_conv[0] = conv[0:6, :768]
    n.g_conv[1] = jnp.concatenate([conv[0:6, 768:], conv[8:14, :256]], axis=1)
    n.g_conv[2] = conv[8:14, 256:1024]
    stem = conv[8:16, 1024:1152].astype(BF16)
    for code in range(4):
        taps = iota((128, 15), 0) == 4 * iota((128, 15), 1) + code
        n.g_stem[:, code, :] = dot(stem, zero_one(taps))[:6]
    links.down.receive()
    links.first.receive()
    down = total(n.down_r_, 8) + total(n.first_r_, 8)
    n.g_down[0:6, :] = down[0:6]
    n.g_down[6:12, :] = down[8:14]
    links.gain.receive()
    gains = total(n.gain_r_, 8)
    high = gains.astype(BF16)
    fine = (gains - high.astype(F32)).astype(BF16)
    shift = zero_one(jnp.logical_and(row == column + 12 * b, column < 12))
    n.g_gain[...] = (dot(high, shift) + dot(fine, shift))[0:1]
    for link in vars(links).values():
        link.drain()


def finish_body(*refs):
    number = len(OUTPUTS)
    for name, source, target in zip(OUTPUTS, refs[:number], refs[number:]):
        target[...] = source[0, :12] if name == "g_gain" else source[...]


def per_device(
    base_codes,
    stem_weight,
    conv_weight,
    down_weight,
    norm_gain,
    query_weight,
    key_weight,
    value_weight,
    output_weight,
    up_weight,
    cotangent,
):
    vmem, anywhere = pl.BlockSpec(memory_space=pltpu.VMEM), pl.BlockSpec(memory_space=pl.ANY)
    semaphores = [pltpu.SemaphoreType.DMA((7,))] + [pltpu.SemaphoreType.DMA((2,))] * 2
    shapes = {name: x[0] for name, x in SCRATCH.items()}
    for name, pattern in LINKS.items():
        semaphores += [
            pltpu.SemaphoreType.DMA((pattern.count,)),
            pltpu.SemaphoreType.DMA((shapes[name + "_r"][0],)),
        ]
    out_shape = [jax.ShapeDtypeStruct(shape, dtype) for shape, dtype in OUTPUTS.values()]
    results = pl.pallas_call(
        kernel_body,
        out_shape=out_shape,
        in_specs=[vmem] * 4 + [anywhere] * 7,
        out_specs=[vmem] * len(OUTPUTS),
        scratch_shapes=[pltpu.VMEM(shape, dtype) for shape, dtype in SCRATCH.values()] + semaphores,
        compiler_params=pltpu.CompilerParams(
            collective_id=0, has_side_effects=True, vmem_limit_bytes=60 * 1024 * 1024
        ),
        name="step",
    )(
        base_codes,
        cotangent[0],
        norm_gain,
        stem_weight,
        conv_weight.reshape(2304, 768),
        down_weight,
        query_weight,
        key_weight,
        value_weight.T,
        output_weight,
        up_weight,
    )
    features, g_stem, g_conv, g_down, g_gain, g_up, g_q, g_k, g_v, g_o = pl.pallas_call(
        finish_body,
        out_shape=out_shape[:4] + [jax.ShapeDtypeStruct((12,), F32)] + out_shape[5:],
        in_specs=[vmem] * len(OUTPUTS),
        out_specs=[vmem] * len(OUTPUTS),
        name="finish",
    )(*results)
    return (
        features[None],
        g_stem.transpose(2, 1, 0),
        g_conv.transpose(0, 2, 1),
        g_down.T,
        g_gain,
        g_up.T,
        g_q,
        g_k,
        g_v,
        g_o,
    )


def solution(mesh):
    placed = (
        P("batch", "seq"),
        P(),
        P(),
        P(),
        P(),
        P(None, "batch"),
        P(None, "batch"),
        P(None, "batch"),
        P("batch", None),
        P(),
        P("batch", "seq", None),
    )
    return jax.shard_map(
        per_device,
        mesh=mesh,
        in_specs=placed,
        out_specs=(
            P("batch", "seq", None),
            P(None, None, ("seq", "batch")),
            P(None, None, ("seq", "batch")),
            P(None, ("seq", "batch")),
            P(("seq", "batch")),
            P(None, ("seq", "batch")),
            P("seq", "batch"),
            P("seq", "batch"),
            P("seq", "batch"),
            P("seq", "batch"),
        ),
        check_vma=False,
    )
```
